128 devices in a mesh: seq: 4 (over x), fsdp: 32 (over y, z, core).
Axes of the slice: x: 4, y: 4, z: 4, core: 2. Of those that a mesh axis runs over, the one named last changes fastest.
Arguments:
- tokens: bfloat16 [32, 2048, 768], P('fsdp', 'seq'), may hold values from -6 to 6
- cotangent: bfloat16 [32, 2048, 768], P('fsdp', 'seq'), may hold values from -6 to 6
- lengths: int32 [32], P('fsdp'), may hold values from 1537 to 2048, as said below
- routes: int32 [32, 2048, 2], P('fsdp', 'seq'), may hold values from 0 to 7, all different within a row; in each aligned block of 512 rows (0 to 511, 512 to 1023, ..., all dimensions but the last counted through in order) at most 192 rows name the same one
- prior_routes: int32 [32, 2048, 2], P('fsdp', 'seq'), may hold values from 0 to 7
- gain_attend: float32 [768], P('fsdp'), may hold values from 0.5 to 1.5
- attend_in: float32 [768, 2304], P('fsdp'), may hold values from -0.3125 to 0.3125
- attend_out: float32 [768, 768], P('fsdp'), may hold values from -1.25 to 1.25
- gain_mix: float32 [768], P('fsdp'), may hold values from 0.5 to 1.5
- router: float32 [768, 8], P('fsdp'), may hold values from -0.21875 to 0.21875
- route_table: float32 [8, 8], replicated, may hold values from -2 to 2
- const_mix: float32 [768, 4], P('fsdp'), may hold values from -0.21875 to 0.21875
- const_vector: float32 [768, 2], P('fsdp'), may hold values from -6 to 6
- expert_in: float32 [4, 768, 4096], P(None, 'fsdp'), may hold values from -0.21875 to 0.21875
- expert_out: float32 [4, 2048, 768], P(None, 'fsdp'), may hold values from -0.125 to 0.125
Outputs:
- mixed_out: bfloat16 [32, 2048, 768], P('fsdp', 'seq')
- grad_tokens: bfloat16 [32, 2048, 768], P('fsdp', 'seq')
- grad_gain_attend: float32 [768], P('fsdp')
- grad_attend_in: float32 [768, 2304], P('fsdp')
- grad_attend_out: float32 [768, 768], P('fsdp')
- grad_gain_mix: float32 [768], P('fsdp')
- grad_router: float32 [768, 8], P('fsdp')
- grad_route_table: float32 [8, 8], replicated
- grad_const_mix: float32 [768, 4], P('fsdp')
- grad_const_vector: float32 [768, 2], P('fsdp')
- grad_expert_in: float32 [4, 768, 4096], P(None, 'fsdp')
- grad_expert_out: float32 [4, 2048, 768], P(None, 'fsdp')
The draws below stay inside these ranges and needn't reach their ends.
Inputs may be any that keep to these rules, and one draw needn't show every extreme that they name: `lengths`: every length exceeds 3 * 512; in every draw some sequence has length exactly 2048. `routes`: the two numbers of a row differ; numbers below 4 name feed-forward experts, 4 the zero expert, 5 the copy expert, the rest constant experts; in the 512 rows of one device no number stands in more than 192 rows, and in every draw some number stands in exactly 192 rows of some device.
All inputs are finite; a program needn't handle non-finite values.
Results may differ from the reference program's by a relative error of at most 0.023.
The reference program's roundings to bfloat16 on the way count: a program that leaves them out, or rounds other values in their place, can miss the bound.
Values may be sent and summed in bfloat16 or wider, within the bound.
No kernel may reach another device: no remote copies, remote signals or barrier semaphores. Data moves between devices by JAX's collectives and lax.ppermute only.
A program may use at most 320 MiB of HBM per device.

```python
import math
import jax
import jax.numpy as jnp
import numpy as np
from jax import lax

D = 768
H = 2048
HEADS = 12
HEAD_DIM = 64
NC = 2
EF = 4
TOK_DEV = 512
NE = 8
CAP = 192
LEN = 2048
SEQS = 32


def draw_lengths(key, part):
    key = jax.random.fold_in(key, 7)
    first_key, second_key = jax.random.split(key)
    drawn = jax.random.randint(first_key, (SEQS,), 3 * TOK_DEV + 1, LEN + 1)
    longest = jax.random.randint(second_key, (), 0, SEQS)
    return jnp.where(jnp.arange(SEQS) == longest, LEN, drawn).astype(jnp.int32)


def place_ends(values, rng, least, top_value):
    shape = values.shape
    spot = [jax.random.randint(jax.random.fold_in(rng, axis), (), 0, shape[axis]) for axis in range(len(shape))]
    values = values.at[tuple(spot)].set(least)
    longest = shape.index(max(shape))
    spot[longest] = (spot[longest] + 1) % shape[longest]
    return values.at[tuple(spot)].set(top_value)


def level_of(key, shape, pieces, least, top_value):
    def one(axis_at, shards_of):
        draws = jax.random.uniform(jax.random.fold_in(jax.random.fold_in(key, 6), axis_at), (shards_of,), jnp.float32, least / len(pieces), top_value / len(pieces))
        return jnp.repeat(jnp.exp(draws), shape[axis_at] // shards_of).reshape((-1,) + (1,) * (len(shape) - axis_at - 1))

    factor_of = one(*pieces[0])
    for cut in pieces[1:]:
        factor_of = factor_of * one(*cut)
    return factor_of


def routed_block(stream_key, own, number, rows, number_of, top, most, lean):
    order = jax.random.permutation(stream_key, number_of)
    packed, common = portions_of(number_of, rows * top, most, lean, True), portions_of(number_of, rows * top, most, lean, False)
    places = jnp.arange(number_of)

    def named(tallies, rotation):
        used = int((tallies > 0).sum())
        fixed = max(1, used // 4)
        shifted = fixed + (places - fixed + rotation * (used - fixed)) % max(1, number_of - fixed)
        return jnp.zeros((number_of,), jnp.int32).at[order[jnp.where(places < fixed, places, shifted)]].set(jnp.asarray(tallies, jnp.int32))

    tallies = jnp.where(number % 4 == 0, named(packed, number // 4), named(common, number - number // 4 - 1))
    mixed = jax.random.permutation(jax.random.fold_in(own, 3), number_of)
    donor, sink = mixed[0:number_of // 2 * 2:2], mixed[1:number_of // 2 * 2:2]
    room = jnp.minimum(tallies[donor] - 1, most - tallies[sink]) // 2
    room = jnp.where((donor == order[0]) | (sink == order[0]) | (tallies[sink] == 0), 0, jnp.maximum(room, 0))
    shifted = jax.random.randint(jax.random.fold_in(own, 4), (number_of // 2,), 0, 1 << 20) % (room + 1)
    tallies = tallies.at[donor].add(-shifted).at[sink].add(shifted)
    members = jnp.searchsorted(jnp.cumsum(tallies), jnp.arange(rows * top), side="right").astype(jnp.int32)
    table = members.reshape(top, rows).T
    table = table[jax.random.permutation(jax.random.fold_in(own, 1), rows)]
    rotation = jax.random.randint(jax.random.fold_in(own, 2), (rows, 1), 0, top)
    return jnp.take_along_axis(table, (jnp.arange(top)[None, :] + rotation) % top, axis=1)


def portions_of(number_of, total, bound, lean, full):
    portions = [(1 << 20) // math.isqrt(rank ** lean) + 1 for rank in range(1, number_of + 1)]
    largest = bound if full else min(bound, max(-(-total // number_of), total * portions[0] // sum(portions)))
    least = 1 if total - largest >= number_of - 1 else 0
    holding, surplus = [largest] + [least] * (number_of - 1), total - largest - least * (number_of - 1)
    while surplus > 0:
        free = [i for i in range(1, number_of) if holding[i] < largest] or [i for i in range(1, number_of) if holding[i] < bound]
        whole, remaining = sum([portions[i] for i in free]), surplus
        for i in free:
            addition = min(bound - holding[i], max(1, remaining * portions[i] // whole), surplus)
            holding[i] = holding[i] + addition
            surplus = surplus - addition
    return np.array(holding)


def bell_draw(own_key, extent, spread, bound, pieces=(), kind=jnp.bfloat16):
    loudness = level_of(own_key, extent, pieces, -0.22, 0.18) if pieces else 1.0
    values = jax.random.normal(own_key, extent, jnp.float32) * spread * loudness
    return jnp.minimum(jnp.maximum(values, -bound), bound).astype(kind)


def setup_inputs(seed: int = 0) -> dict:
    key_list = jax.random.split(jax.random.key(seed), 16)
    tokens = bell_draw(key_list[0], (SEQS, LEN, D), 1.0, 6.0, ((0, 32), (1, 4)))
    cotangent = bell_draw(key_list[1], (SEQS, LEN, D), 1.0, 6.0, ((0, 32), (1, 4)))
    lengths = draw_lengths(jax.random.fold_in(key_list[15], 71), 0)
    routes_keys = jax.random.split(jax.random.fold_in(key_list[3], 1), SEQS * LEN // TOK_DEV)
    routes_turns = jax.random.permutation(jax.random.fold_in(key_list[3], 3), SEQS * LEN // TOK_DEV)
    routes = jax.vmap(lambda own, number: routed_block(jax.random.fold_in(key_list[3], 2), own, number, TOK_DEV, NE, 2, CAP, 1))(routes_keys, routes_turns).reshape((SEQS, LEN, 2))
    prior_routes = place_ends(jax.random.randint(key_list[4], (SEQS, LEN, 2), 0, NE), jax.random.fold_in(key_list[4], 1), 0, NE - 1).astype(jnp.int32)
    gain_attend = jnp.clip(1.0 + 0.1 * jax.random.normal(key_list[5], (D,), jnp.float32), 0.5, 1.5)
    attend_in = bell_draw(key_list[6], (D, 3 * D), (D // 2) ** -0.5, 0.3125, ((0, 32),), jnp.float32)
    attend_out = bell_draw(key_list[7], (D, D), (D // 32) ** -0.5, 1.25, ((0, 32),), jnp.float32)
    gain_mix = jnp.clip(1.0 + 0.1 * jax.random.normal(key_list[8], (D,), jnp.float32), 0.5, 1.5)
    router = bell_draw(key_list[9], (D, NE), D ** -0.5, 0.21875, ((0, 32),), jnp.float32)
    route_table = bell_draw(key_list[10], (NE, NE), 0.3, 2.0, (), jnp.float32)
    const_mix = bell_draw(key_list[11], (D, 2 * NC), D ** -0.5, 0.21875, ((0, 32),), jnp.float32)
    const_vector = bell_draw(key_list[12], (D, NC), 1.0, 6.0, ((0, 32),), jnp.float32)
    expert_in = bell_draw(key_list[13], (EF, D, 2 * H), D ** -0.5, 0.21875, ((1, 32),), jnp.float32)
    expert_out = bell_draw(key_list[14], (EF, H, D), H ** -0.5, 0.125, ((1, 32),), jnp.float32)
    return dict(tokens=tokens, cotangent=cotangent, lengths=lengths, routes=routes, prior_routes=prior_routes, gain_attend=gain_attend, attend_in=attend_in, attend_out=attend_out, gain_mix=gain_mix, router=router, route_table=route_table, const_mix=const_mix, const_vector=const_vector, expert_in=expert_in, expert_out=expert_out)


@jax.custom_vjp
def low(v):
    return lax.optimization_barrier(v.astype(jnp.bfloat16)).astype(jnp.float32)

@jax.custom_vjp
def low_back(v):
    return v

def low_keep(v):
    return (low(v), None)

def low_pass(kept, grad):
    return (grad,)

def back_keep(v):
    return (v, None)

def back_low(kept, grad):
    return (low(grad),)
low.defvjp(low_keep, low_pass)
low_back.defvjp(back_keep, back_low)
eps = 1e-06
precise = lax.Precision.HIGHEST

def matmul(left_side, right_side):
    return jnp.dot(left_side, right_side, precision=precise, preferred_element_type=jnp.float32)

def rms_scale(values, gain_vec):
    return values * lax.rsqrt(lax.optimization_barrier(jnp.mean(values * values, axis=-1, keepdims=True)) + eps) * gain_vec

def rotate(values, positions, sign_factor):
    half_dim = values.shape[-1] // 2
    inverse = jnp.exp(jnp.arange(half_dim, dtype=jnp.float32) * (-2.0 * math.log(10000.0) / values.shape[-1]))
    angles = positions[:, None] * inverse[None, :]
    cosine = jnp.cos(angles)[:, None, :]
    sine_part = sign_factor * jnp.sin(angles)[:, None, :]
    first_half = values[..., :half_dim]
    second = values[..., half_dim:]
    return jnp.concatenate([first_half * cosine - second * sine_part, second * cosine + first_half * sine_part], axis=-1)

def slot_plan(choices):
    flat_ids = choices.reshape(-1).astype(jnp.int32)
    pick_count = flat_ids.shape[0]
    onehot = (flat_ids[:, None] == jnp.arange(NE, dtype=jnp.int32)[None, :]).astype(jnp.int32)
    before = (jnp.cumsum(onehot, axis=0) - onehot).astype(jnp.int32)
    rank_in = lax.optimization_barrier(jnp.sum(before * onehot, axis=1)).astype(jnp.int32)
    is_ffn = flat_ids < EF
    slot_ids = jnp.where(is_ffn, flat_ids * CAP + rank_in, EF * CAP).astype(jnp.int32)
    owners = jnp.arange(pick_count, dtype=jnp.int32) // 2
    slot_owner = jnp.zeros((EF * CAP + 1,), jnp.int32).at[slot_ids].set(owners)[:EF * CAP]
    slot_filled = jnp.zeros((EF * CAP + 1,), jnp.float32).at[slot_ids].set(1.0)[:EF * CAP]
    picked = jnp.minimum(slot_ids, EF * CAP - 1).astype(jnp.int32)
    return (picked, is_ffn, slot_owner, slot_filled)

def expert_block(moe_low, block_routes, gate_probs, expert_in, expert_out):
    picked, is_ffn, slot_owner, slot_filled = slot_plan(block_routes)
    model_width = moe_low.shape[1]
    buffer = (moe_low[slot_owner] * slot_filled[:, None]).reshape(EF, CAP, model_width)
    inner_rows = low_back(jnp.einsum('ecd,edf->ecf', buffer, expert_in, precision=precise))
    hidden_dim = expert_out.shape[1]
    hidden_low = low(jax.nn.silu(inner_rows[..., :hidden_dim]) * inner_rows[..., hidden_dim:])
    result = low_back(jnp.einsum('ecf,efd->ecd', hidden_low, expert_out, precision=precise))
    result = result.reshape(EF * CAP, model_width)
    chosen = (result[picked] * is_ffn[:, None].astype(jnp.float32)).reshape(gate_probs.shape[0], 2, model_width)
    return lax.optimization_barrier(jnp.sum(gate_probs[:, :, None] * chosen, axis=1))

def sequence_forward(weights, inputs):
    gain_a, attend_w, out_w, gain_m, router_w, route_table, mix_w, vector_w, expert_w_in, expert_w_out = weights
    seq_tokens, seq_length, seq_routes, seq_prior = inputs
    seq_len = seq_tokens.shape[0]
    model_width = seq_tokens.shape[1]
    positions = jnp.arange(seq_len, dtype=jnp.float32)
    normed = low(rms_scale(seq_tokens, gain_a))
    projected = low_back(matmul(normed, attend_w))
    queries = projected[:, :model_width].reshape(seq_len, HEADS, HEAD_DIM)
    key_rows = projected[:, model_width:2 * model_width].reshape(seq_len, HEADS, HEAD_DIM)
    value_rows = projected[:, 2 * model_width:].reshape(seq_len, HEADS, HEAD_DIM)
    queries = low_back(low(rotate(queries, positions, 1.0)))
    key_rows = low_back(low(rotate(key_rows, positions, 1.0)))
    value_rows = low_back(low(value_rows))
    scores = low_back(jnp.einsum('qhd,khd->hqk', queries, key_rows, precision=precise) * HEAD_DIM ** (-0.5))
    index_row = jnp.arange(seq_len, dtype=jnp.int32)
    allowed = (index_row[None, :] <= index_row[:, None]) & (index_row[None, :] < seq_length)
    scores = jnp.where(allowed[None], scores, -1e+30)
    highest = lax.optimization_barrier(jnp.max(scores, axis=-1, keepdims=True))
    expo_scores = jnp.exp(scores - highest)
    attn_probs = low(expo_scores / lax.optimization_barrier(jnp.sum(expo_scores, axis=-1, keepdims=True)))
    mixed_rows = jnp.einsum('hqk,khd->qhd', attn_probs, value_rows, precision=precise).reshape(seq_len, model_width)
    mixed_rows = low_back(low(mixed_rows))
    residual = seq_tokens + low_back(matmul(mixed_rows, out_w))
    normed_m = rms_scale(residual, gain_m)
    moe_low = low(normed_m)
    expert_ids = jnp.arange(NE, dtype=jnp.int32)
    prior_hits = lax.optimization_barrier(jnp.sum((seq_prior[:, :, None] == expert_ids).astype(jnp.float32), axis=1))
    logits = matmul(moe_low, router_w) + matmul(prior_hits, route_table)
    chosen_logits = jnp.take_along_axis(logits, seq_routes, axis=1)
    gate_exp = jnp.exp(chosen_logits - lax.optimization_barrier(jnp.max(chosen_logits, axis=1, keepdims=True)))
    gate_probs = gate_exp / lax.optimization_barrier(jnp.sum(gate_exp, axis=1, keepdims=True))
    block_count = seq_len // TOK_DEV
    ffn_rows = jax.vmap(expert_block, in_axes=(0, 0, 0, None, None))(moe_low.reshape(block_count, TOK_DEV, model_width), seq_routes.reshape(block_count, TOK_DEV, 2), gate_probs.reshape(block_count, TOK_DEV, 2), expert_w_in, expert_w_out).reshape(seq_len, model_width)
    expert_share = lax.optimization_barrier(jnp.sum(gate_probs[:, :, None] * (seq_routes[:, :, None] == expert_ids).astype(jnp.float32), axis=1))
    mix_logits = matmul(moe_low, mix_w).reshape(seq_len, NC, 2)
    mix_exp = jnp.exp(mix_logits - lax.optimization_barrier(jnp.max(mix_logits, axis=-1, keepdims=True)))
    mix_probs = mix_exp / lax.optimization_barrier(jnp.sum(mix_exp, axis=-1, keepdims=True))
    const_out = mix_probs[..., 0:1] * normed_m[:, None, :] + mix_probs[..., 1:2] * jnp.transpose(vector_w)[None, :, :]
    expert_sum = ffn_rows + expert_share[:, EF + 1:EF + 2] * normed_m + lax.optimization_barrier(jnp.sum(expert_share[:, EF + 2:, None] * const_out, axis=1))
    return residual + expert_sum

def reference(tokens, cotangent, lengths, routes, prior_routes, gain_attend, attend_in, attend_out, gain_mix, router, route_table, const_mix, const_vector, expert_in, expert_out):
    masters = (gain_attend, attend_in, attend_out, gain_mix, router, route_table, const_mix, const_vector, expert_in, expert_out)

    def forward(inputs_f, params):
        rounded = tuple((low(item) for item in params[:5])) + (params[5],) + tuple((low(item) for item in params[6:]))

        def one_sequence(seq_items):
            return sequence_forward(rounded, seq_items)
        return lax.map(jax.checkpoint(one_sequence), (inputs_f, lengths, routes, prior_routes))
    outputs, pullback = jax.vjp(forward, tokens.astype(jnp.float32), masters)
    valid_rows = jnp.arange(LEN, dtype=jnp.int32)[None, :] < lengths[:, None]
    grad_out = cotangent.astype(jnp.float32) * valid_rows[:, :, None].astype(jnp.float32)
    grad_inputs, grads = pullback(grad_out)
    return (outputs.astype(jnp.bfloat16), grad_inputs.astype(jnp.bfloat16), grads[0], grads[1], grads[2], grads[3], grads[4], grads[5], grads[6], grads[7], grads[8], grads[9])
```

```python
import math

import jax
import jax.numpy as jnp
from jax import lax
from jax.experimental import pallas as pl
from jax.experimental.pallas import tpu as pltpu
from jax.sharding import PartitionSpec as P

HEADS = 12
HEAD_DIM = 64
HALF = HEAD_DIM // 2
NC = 2
EF = 4
NE = 8
CAP = 192
LANES = 128
EPS = 1e-06
SCALE = HEAD_DIM ** (-0.5)
LOWEST = -1e30
F32 = jnp.float32
BF16 = jnp.bfloat16
VMEM = pl.BlockSpec(memory_space=pltpu.VMEM)
SMEM = pl.BlockSpec(memory_space=pltpu.SMEM)


def mm(a, b, ca=1, cb=0):
    return lax.dot_general(a, b, (((ca,), (cb,)), ((), ())), preferred_element_type=F32)


def params(mib, grid=None):
    if grid is None:
        return pltpu.CompilerParams(vmem_limit_bytes=mib << 20)
    return pltpu.CompilerParams(
        vmem_limit_bytes=mib << 20, dimension_semantics=("arbitrary",) * grid
    )


def sds(shape, dtype):
    return jax.ShapeDtypeStruct(shape, dtype)


def cost(flops, nbytes, trans=0):
    return pl.CostEstimate(flops=int(flops), bytes_accessed=int(nbytes), transcendentals=int(trans))


def everyone(x, axis):
    copies = jnp.broadcast_to(x[None], (lax.axis_size(axis), *x.shape))
    return lax.all_to_all(copies, axis, split_axis=0, concat_axis=0, tiled=True)


def swap(x, axis):
    return lax.all_to_all(x, axis, split_axis=0, concat_axis=0, tiled=True)


def two_parts(x):
    high = x.astype(BF16)
    return high, (x - high.astype(F32)).astype(BF16)


def lane_of(shape):
    return lax.broadcasted_iota(jnp.int32, shape, 1)


def pick(values, lanes, lane):
    return jnp.sum(jnp.where(lanes == lane, values, 0.0), axis=1, keepdims=True)


def project_kernel(tok, weight, gain, cosine, sine, qkv, normed):
    v = tok[0].astype(F32)
    n = v * lax.rsqrt(jnp.mean(v * v, axis=-1, keepdims=True) + EPS) * gain[...]
    n = n.astype(BF16)
    normed[0] = n
    width = qkv.shape[1]
    part = width // 3
    flat = jnp.transpose(mm(n, weight[:, :width]))
    c, s = cosine[0], sine[0]
    for which in range(2):
        factor = SCALE if which == 0 else 1.0
        for at in range(which * part, (which + 1) * part, HEAD_DIM):
            a, b = flat[at : at + HALF], flat[at + HALF : at + HEAD_DIM]
            qkv[0, at : at + HALF] = ((a * c - b * s) * factor).astype(BF16)
            qkv[0, at + HALF : at + HEAD_DIM] = ((b * c + a * s) * factor).astype(BF16)
    qkv[0, 2 * part :] = flat[2 * part :].astype(BF16)


def project(tok, weight, gain, cosine, sine, width):
    blocks, rows, model = tok.shape
    return pl.pallas_call(
        project_kernel,
        grid=(blocks,),
        in_specs=[
            pl.BlockSpec((1, rows, model), lambda i: (i, 0, 0)),
            pl.BlockSpec(weight.shape, lambda i: (0, 0)),
            pl.BlockSpec(gain.shape, lambda i: (0, 0)),
            pl.BlockSpec((1, HALF, rows), lambda i: (i, 0, 0)),
            pl.BlockSpec((1, HALF, rows), lambda i: (i, 0, 0)),
        ],
        out_specs=[
            pl.BlockSpec((1, width, rows), lambda i: (i, 0, 0)),
            pl.BlockSpec((1, rows, model), lambda i: (i, 0, 0)),
        ],
        out_shape=[sds((blocks, width, rows), BF16), sds((blocks, rows, model), BF16)],
        compiler_params=params(40, 1),
        cost_estimate=cost(2 * blocks * rows * model * width, 8e6),
        name="project",
    )(tok, weight, gain, cosine, sine)


def mask_diagonal(scores, start, length):
    keys = lax.broadcasted_iota(jnp.int32, scores.shape, 0)
    queries = lax.broadcasted_iota(jnp.int32, scores.shape, 1)
    return jnp.where((keys <= queries) & (keys + start < length), scores, LOWEST)


def attend_kernel(meta, qkv, out, lse, top, total, acc):
    block = pl.program_id(0)
    rows = qkv.shape[2]
    part = qkv.shape[1] // 3
    heads = part // HEAD_DIM
    length = meta[0]
    for h in range(heads):
        at = slice(h * HEAD_DIM, (h + 1) * HEAD_DIM)
        k_at = slice(part + h * HEAD_DIM, part + (h + 1) * HEAD_DIM)
        v_at = slice(2 * part + h * HEAD_DIM, 2 * part + (h + 1) * HEAD_DIM)
        scores = mask_diagonal(mm(qkv[block, k_at], qkv[block, at], 0, 0), block * rows, length)
        peak = jnp.max(scores, axis=0, keepdims=True)
        e = jnp.exp(scores - peak)
        top[h : h + 1] = peak
        total[h : h + 1] = jnp.sum(e, axis=0, keepdims=True)
        acc[at] = mm(qkv[block, v_at], e.astype(BF16))

    def step(j, carry):
        for h in range(heads):
            at = slice(h * HEAD_DIM, (h + 1) * HEAD_DIM)
            k_at = slice(part + h * HEAD_DIM, part + (h + 1) * HEAD_DIM)
            v_at = slice(2 * part + h * HEAD_DIM, 2 * part + (h + 1) * HEAD_DIM)
            scores = mm(qkv[j, k_at], qkv[block, at], 0, 0)
            before = top[h : h + 1]
            peak = jnp.maximum(before, jnp.max(scores, axis=0, keepdims=True))
            e = jnp.exp(scores - peak)
            fade = jnp.exp(before - peak)
            top[h : h + 1] = peak
            total[h : h + 1] = total[h : h + 1] * fade + jnp.sum(e, axis=0, keepdims=True)
            acc[at] = acc[at] * fade + mm(qkv[j, v_at], e.astype(BF16))
        return carry

    lax.fori_loop(0, block, step, 0)
    for h in range(heads):
        at = slice(h * HEAD_DIM, (h + 1) * HEAD_DIM)
        out[0, at] = (acc[at] / total[h : h + 1]).astype(BF16)
        lse[0, h : h + 1] = top[h : h + 1] + jnp.log(total[h : h + 1])


def attend(meta, qkv):
    blocks, width, rows = qkv.shape
    part = width // 3
    pairs = blocks * (blocks + 1) // 2
    return pl.pallas_call(
        attend_kernel,
        grid=(blocks,),
        in_specs=[SMEM, pl.BlockSpec(qkv.shape, lambda i: (0, 0, 0))],
        out_specs=[
            pl.BlockSpec((1, part, rows), lambda i: (i, 0, 0)),
            pl.BlockSpec((1, 8, rows), lambda i: (i, 0, 0)),
        ],
        out_shape=[sds((blocks, part, rows), BF16), sds((blocks, 8, rows), F32)],
        scratch_shapes=[
            pltpu.VMEM((8, rows), F32),
            pltpu.VMEM((8, rows), F32),
            pltpu.VMEM((part, rows), F32),
        ],
        compiler_params=params(40, 1),
        cost_estimate=cost(4 * pairs * rows * rows * part, 4e6, pairs * rows * rows * 3),
        name="attend",
    )(meta, qkv)


def attend_back_kernel(meta, qkv, dout, out, lse, cosine, sine, dproj, dq, dk, dv, dots):
    blocks, width, rows = qkv.shape
    part = width // 3
    heads = part // HEAD_DIM
    length = meta[0]

    def pair(q, k, diagonal):
        for h in range(heads):
            at = slice(h * HEAD_DIM, (h + 1) * HEAD_DIM)
            k_at = slice(part + h * HEAD_DIM, part + (h + 1) * HEAD_DIM)
            v_at = slice(2 * part + h * HEAD_DIM, 2 * part + (h + 1) * HEAD_DIM)
            qh, kh, vh, doh = qkv[q, at], qkv[k, k_at], qkv[k, v_at], dout[q, at]
            scores = mm(kh, qh, 0, 0)
            if diagonal:
                scores = mask_diagonal(scores, k * rows, length)
            probs = jnp.exp(scores - lse[q, h : h + 1])
            dprobs = mm(vh, doh, 0, 0)
            low = probs.astype(BF16)
            dscores = (probs * (dprobs - dots[q, h : h + 1])).astype(BF16)
            if diagonal:
                dv[k, at] = mm(doh, low, 1, 1)
                dk[k, at] = mm(qh, dscores, 1, 1)
                dq[q, at] = mm(kh, dscores)
            else:
                dv[k, at] += mm(doh, low, 1, 1)
                dk[k, at] += mm(qh, dscores, 1, 1)
                dq[q, at] += mm(kh, dscores)

    def first(b, carry):
        for h in range(heads):
            at = slice(h * HEAD_DIM, (h + 1) * HEAD_DIM)
            both = dout[b, at].astype(F32) * out[b, at].astype(F32)
            dots[b, h : h + 1] = jnp.sum(both, axis=0, keepdims=True)
        return carry

    def diagonal(b, carry):
        pair(b, b, True)
        return carry

    def below(q, carry):
        def one(k, inner):
            pair(q, k, False)
            return inner

        return lax.fori_loop(0, q, one, carry)

    def last(b, carry):
        c, s = cosine[b], sine[b]
        for which, held in ((0, dq), (1, dk)):
            factor = SCALE if which == 0 else 1.0
            for h in range(heads):
                at = h * HEAD_DIM
                rounded = (held[b, at : at + HEAD_DIM] * factor).astype(BF16).astype(F32)
                x, y = rounded[:HALF], rounded[HALF:]
                to = which * part + at
                dproj[b, to : to + HALF] = (x * c + y * s).astype(BF16)
                dproj[b, to + HALF : to + HEAD_DIM] = (y * c - x * s).astype(BF16)
        dproj[b, 2 * part :] = dv[b].astype(BF16)
        return carry

    lax.fori_loop(0, blocks, first, 0)
    lax.fori_loop(0, blocks, diagonal, 0)
    lax.fori_loop(1, blocks, below, 0)
    lax.fori_loop(0, blocks, last, 0)


def attend_back(meta, qkv, dout, out, lse, cosine, sine):
    blocks, width, rows = qkv.shape
    part = width // 3
    pairs = blocks * (blocks + 1) // 2
    return pl.pallas_call(
        attend_back_kernel,
        in_specs=[SMEM] + [VMEM] * 6,
        out_specs=VMEM,
        out_shape=sds(qkv.shape, BF16),
        scratch_shapes=[pltpu.VMEM((blocks, part, rows), F32)] * 3
        + [pltpu.VMEM((blocks, 8, rows), F32)],
        compiler_params=params(48),
        cost_estimate=cost(10 * pairs * rows * rows * part, 1e7, pairs * rows * rows * 3),
        name="attend_back",
    )(meta, qkv, dout, out, lse, cosine, sine)


def route_kernel(att, out_w, tok, gain, small_w, prior, routes, slots, resid, moe, sent, stats):
    res = tok[...].astype(F32) + mm(att[...], out_w[...], 0, 0)
    resid[...] = res
    normed = res * lax.rsqrt(jnp.mean(res * res, axis=-1, keepdims=True) + EPS) * gain[...]
    low = normed.astype(BF16)
    moe[...] = low
    small = mm(low, small_w[...])
    logits = small + prior[...]
    lanes = lane_of(small.shape)
    hit0 = lanes == routes[:, 0:1]
    hit1 = lanes == routes[:, 1:2]
    chosen0 = jnp.sum(jnp.where(hit0, logits, 0.0), axis=1, keepdims=True)
    chosen1 = jnp.sum(jnp.where(hit1, logits, 0.0), axis=1, keepdims=True)
    gate0 = 1.0 / (1.0 + jnp.exp(chosen1 - chosen0))
    gate1 = 1.0 / (1.0 + jnp.exp(chosen0 - chosen1))
    share = jnp.where(hit0, gate0, 0.0) + jnp.where(hit1, gate1, 0.0)
    partner = jnp.where(lanes % 2 == 0, pltpu.roll(small, LANES - 1, 1), pltpu.roll(small, 1, 1))
    mix = 1.0 / (1.0 + jnp.exp(partner - small))
    mixing = (lanes >= NE) & (lanes < NE + 2 * NC)
    stats[...] = share + jnp.where(mixing, mix, 0.0)
    high, rest = two_parts(share)
    parts = (high.astype(F32) + pltpu.roll(rest.astype(F32), NE, 1)).astype(BF16)
    model = low.shape[1]
    for e in range(EF):
        sent[e, :, :model] = mm(slots[e], low).astype(BF16)
        sent[e, :, model:] = mm(slots[e], parts).astype(BF16)


def route(att, out_w, tok, gain, small_w, prior, routes, slots):
    rows, model = tok.shape
    return pl.pallas_call(
        route_kernel,
        in_specs=[VMEM] * 8,
        out_specs=[VMEM] * 4,
        out_shape=[
            sds((rows, model), F32),
            sds((rows, model), BF16),
            sds((EF, CAP, model + LANES), BF16),
            sds((rows, LANES), F32),
        ],
        compiler_params=params(40),
        cost_estimate=cost(2 * rows * model * (2 * model + EF * CAP), 1e7),
        name="route",
    )(att, out_w, tok, gain, small_w, prior, routes, slots)


def local_kernel(resid, stats, grad, gain, vectors, partial, small, grad_vec):
    res, g = resid[...], grad[...].astype(F32)
    normed = res * lax.rsqrt(jnp.mean(res * res, axis=-1, keepdims=True) + EPS) * gain[...]
    held = stats[...]
    lanes = lane_of(held.shape)
    copy_dot = jnp.sum(g * normed, axis=1, keepdims=True)
    factor = pick(held, lanes, EF + 1)
    result = jnp.where(lanes == EF + 1, factor * copy_dot, 0.0)
    ways = jnp.zeros_like(held)
    added = jnp.zeros_like(res)
    for j in range(NC):
        row = vectors[j : j + 1]
        weight = pick(held, lanes, EF + 2 + j)
        first = pick(held, lanes, NE + 2 * j)
        second = pick(held, lanes, NE + 2 * j + 1)
        vec_dot = jnp.sum(g * row, axis=1, keepdims=True)
        mean = first * copy_dot + second * vec_dot
        result += jnp.where(lanes == EF + 2 + j, weight * mean, 0.0)
        result += jnp.where(lanes == NE + 2 * j, weight * first * (copy_dot - mean), 0.0)
        result += jnp.where(lanes == NE + 2 * j + 1, weight * second * (vec_dot - mean), 0.0)
        ways += jnp.where(lanes == j, weight * second, 0.0)
        added += (weight * second) * row
        factor += weight * first
    small[...] = result + jnp.where(lanes == NE + 2 * NC, factor, 0.0)
    partial[...] = res + factor * normed + added
    high, rest = two_parts(ways)
    grad_vec[...] = mm(grad[...], high, 0, 0) + mm(grad[...], rest, 0, 0)


def local_part(resid, stats, grad, gain, vectors):
    rows, model = resid.shape
    return pl.pallas_call(
        local_kernel,
        in_specs=[VMEM] * 5,
        out_specs=[VMEM] * 3,
        out_shape=[sds((rows, model), F32), sds((rows, LANES), F32), sds((model, LANES), F32)],
        compiler_params=params(40),
        cost_estimate=cost(4 * rows * model * LANES, 6e6),
        name="local_part",
    )(resid, stats, grad, gain, vectors)


def expert_kernel(
    meta, sent, grads, gate_w, up_w, out_w, back, hidden, dgate, dup, scaled, rows, gate, acc, dots
):
    step = pl.program_id(0)
    model = rows.shape[1]
    count = sent.shape[0]

    @pl.when(step == 0)
    def _():
        expert = meta[1]
        for s in range(count):
            at = slice(s * CAP, (s + 1) * CAP)
            rows[at] = sent[s, :, :model]
            parts = sent[s, :, model:].astype(F32)
            lanes = lane_of(parts.shape)
            own = (lanes == expert) | (lanes == expert + NE)
            share = jnp.sum(jnp.where(own, parts, 0.0), axis=1, keepdims=True)
            gate[at] = jnp.broadcast_to(share, (CAP, LANES))
            scaled[at] = (grads[s].astype(F32) * share).astype(BF16)
        acc[...] = jnp.zeros_like(acc)
        dots[...] = jnp.zeros_like(dots)

    for s in range(count):
        at = slice(s * CAP, (s + 1) * CAP)
        x = rows[at]
        g = mm(x, gate_w[...])
        u = mm(x, up_w[...])
        v = mm(grads[s], out_w[...], 1, 1)
        sig = 1.0 / (1.0 + jnp.exp(-g))
        silu = g * sig
        low = (silu * u).astype(BF16)
        hidden[at] = low
        both = v * low.astype(F32)
        folded = both[:, :LANES]
        for c in range(LANES, both.shape[1], LANES):
            folded = folded + both[:, c : c + LANES]
        dots[at] += folded
        d = v * gate[at, 0:1]
        du = (d * silu).astype(BF16)
        dg = (d * u * (sig * (1.0 + g * (1.0 - sig)))).astype(BF16)
        dgate[at] = dg
        dup[at] = du
        acc[at] += mm(dg, gate_w[...], 1, 1) + mm(du, up_w[...], 1, 1)

    @pl.when(step == pl.num_programs(0) - 1)
    def _():
        expert = meta[1]
        for s in range(count):
            at = slice(s * CAP, (s + 1) * CAP)
            back[s, :, :model] = acc[at].astype(BF16)
            value = jnp.sum(dots[at], axis=1, keepdims=True) * gate[at]
            lanes = lane_of(value.shape)
            high, rest = two_parts(value)
            back[s, :, model:] = (
                jnp.where(lanes == expert, high.astype(F32), 0.0)
                + jnp.where(lanes == expert + NE, rest.astype(F32), 0.0)
            ).astype(BF16)


def expert(meta, sent, grads, w_in, w_out, block):
    count, cap, wide = sent.shape
    model = grads.shape[2]
    inner = w_out.shape[0]
    rows = count * cap
    steps = inner // block
    return pl.pallas_call(
        expert_kernel,
        grid=(steps,),
        in_specs=[
            SMEM,
            pl.BlockSpec(sent.shape, lambda i: (0, 0, 0)),
            pl.BlockSpec(grads.shape, lambda i: (0, 0, 0)),
            pl.BlockSpec((model, block), lambda i: (0, i)),
            pl.BlockSpec((model, block), lambda i: (0, i + steps)),
            pl.BlockSpec((block, model), lambda i: (i, 0)),
        ],
        out_specs=[
            pl.BlockSpec(sent.shape, lambda i: (0, 0, 0)),
            pl.BlockSpec((rows, block), lambda i: (0, i)),
            pl.BlockSpec((rows, block), lambda i: (0, i)),
            pl.BlockSpec((rows, block), lambda i: (0, i)),
            pl.BlockSpec((rows, model), lambda i: (0, 0)),
        ],
        out_shape=[
            sds(sent.shape, BF16),
            sds((rows, inner), BF16),
            sds((rows, inner), BF16),
            sds((rows, inner), BF16),
            sds((rows, model), BF16),
        ],
        scratch_shapes=[
            pltpu.VMEM((rows, model), BF16),
            pltpu.VMEM((rows, LANES), F32),
            pltpu.VMEM((rows, model), F32),
            pltpu.VMEM((rows, LANES), F32),
        ],
        compiler_params=params(48, 1),
        cost_estimate=cost(10 * rows * model * inner, 2.5e7, rows * inner),
        name="expert",
    )(meta, sent, grads, w_in, w_in, w_out)


def expert_grads_kernel(
    sent, scaled, gate, hidden, dgate, dup, out_w, grad_in, grad_out, branch, flipped, acc
):
    step = pl.program_id(0)
    model = acc.shape[1]
    count = sent.shape[0]

    @pl.when(step == 0)
    def _():
        for s in range(count):
            flipped[:, s * CAP : (s + 1) * CAP] = jnp.transpose(sent[s, :, :model])
        acc[...] = jnp.zeros_like(acc)

    grad_in[0] = mm(flipped[...], dgate[...]).astype(BF16)
    grad_in[1] = mm(flipped[...], dup[...]).astype(BF16)
    grad_out[...] = mm(hidden[...], scaled[...], 0, 0).astype(BF16)
    acc[...] += mm(hidden[...], out_w[...])

    @pl.when(step == pl.num_programs(0) - 1)
    def _():
        for s in range(count):
            at = slice(s * CAP, (s + 1) * CAP)
            branch[s] = (acc[at] * gate[at]).astype(BF16)


def expert_grads(sent, scaled, gate, hidden, dgate, dup, w_out, block):
    count, cap, wide = sent.shape
    rows, model = scaled.shape
    inner = w_out.shape[0]
    return pl.pallas_call(
        expert_grads_kernel,
        grid=(inner // block,),
        in_specs=[
            pl.BlockSpec(sent.shape, lambda i: (0, 0, 0)),
            pl.BlockSpec((rows, model), lambda i: (0, 0)),
            pl.BlockSpec((rows, 1), lambda i: (0, 0)),
            pl.BlockSpec((rows, block), lambda i: (0, i)),
            pl.BlockSpec((rows, block), lambda i: (0, i)),
            pl.BlockSpec((rows, block), lambda i: (0, i)),
            pl.BlockSpec((block, model), lambda i: (i, 0)),
        ],
        out_specs=[
            pl.BlockSpec((2, model, block), lambda i: (0, 0, i)),
            pl.BlockSpec((block, model), lambda i: (i, 0)),
            pl.BlockSpec((count, cap, model), lambda i: (0, 0, 0)),
        ],
        out_shape=[
            sds((2, model, inner), BF16),
            sds((inner, model), BF16),
            sds((count, cap, model), BF16),
        ],
        scratch_shapes=[pltpu.VMEM((model, rows), BF16), pltpu.VMEM((rows, model), F32)],
        compiler_params=params(48, 1),
        cost_estimate=cost(8 * rows * model * inner, 2.5e7),
        name="expert_grads",
    )(sent, scaled, gate, hidden, dgate, dup, w_out)


def unroute_kernel(
    back, slots, resid, small, stats, grad, gain, small_w, out_w, dres, dlow, datt, dlogits, dgain
):
    rows, model = resid.shape
    held, local = stats[...], small[...]
    lanes = lane_of(held.shape)
    dn = jnp.zeros((rows, model), F32)
    tail = jnp.zeros((rows, LANES), F32)
    for e in range(EF):
        dn += mm(slots[e], back[e, :, :model], 0, 0)
        tail += mm(slots[e], back[e, :, model:], 0, 0)
    ffn = tail + pltpu.roll(tail, LANES - NE, 1)
    dots = jnp.where(lanes < EF, ffn, jnp.where(lanes < NE, local, 0.0))
    total = jnp.sum(dots, axis=1, keepdims=True)
    keep = (lanes >= NE) & (lanes < NE + 2 * NC)
    dsmall = jnp.where(lanes < NE, dots - held * total, jnp.where(keep, local, 0.0))
    dlogits[...] = dsmall
    high, rest = two_parts(dsmall)
    dn += mm(high, small_w[...], 1, 1) + mm(rest, small_w[...], 1, 1)
    g = grad[...].astype(F32)
    dn += pick(local, lanes, NE + 2 * NC) * g
    res = resid[...]
    factor = lax.rsqrt(jnp.mean(res * res, axis=-1, keepdims=True) + EPS)
    normal = res * factor
    dgain[...] = jnp.sum(dn * normal, axis=0, keepdims=True)
    scaled = dn * gain[...]
    out = g + factor * (scaled - normal * jnp.mean(scaled * normal, axis=-1, keepdims=True))
    dres[...] = out
    low = out.astype(BF16)
    dlow[...] = low
    datt[...] = mm(out_w[...], low, 1, 1).astype(BF16)


def unroute(back, slots, resid, small, stats, grad, gain, small_w, out_w):
    rows, model = resid.shape
    return pl.pallas_call(
        unroute_kernel,
        in_specs=[VMEM] * 9,
        out_specs=[VMEM] * 5,
        out_shape=[
            sds((rows, model), F32),
            sds((rows, model), BF16),
            sds((model, rows), BF16),
            sds((rows, LANES), F32),
            sds((1, model), F32),
        ],
        compiler_params=params(40),
        cost_estimate=cost(2 * rows * model * (2 * model + EF * CAP), 1e7),
        name="unroute",
    )(back, slots, resid, small, stats, grad, gain, small_w, out_w)


def weight_grad_kernel(dproj, normed, out, acc):
    step = pl.program_id(0)

    @pl.when(step == 0)
    def _():
        acc[...] = jnp.zeros_like(acc)

    acc[...] += mm(dproj[0], normed[0])

    @pl.when(step == pl.num_programs(0) - 1)
    def _():
        out[...] = jnp.transpose(acc[...]).astype(BF16)


def weight_grad(dproj, normed):
    blocks, width, rows = dproj.shape
    model = normed.shape[2]
    return pl.pallas_call(
        weight_grad_kernel,
        grid=(blocks,),
        in_specs=[
            pl.BlockSpec((1, width, rows), lambda i: (i, 0, 0)),
            pl.BlockSpec((1, rows, model), lambda i: (i, 0, 0)),
        ],
        out_specs=pl.BlockSpec((model, width), lambda i: (0, 0)),
        out_shape=sds((model, width), BF16),
        scratch_shapes=[pltpu.VMEM((width, model), F32)],
        compiler_params=params(40, 1),
        cost_estimate=cost(2 * blocks * rows * width * model, 6e6),
        name="weight_grad",
    )(dproj, normed)


def finish_kernel(dproj, weight, tok, gain, dres, out):
    dn = jnp.transpose(mm(weight[...], dproj[...]))
    v = tok[...].astype(F32)
    factor = lax.rsqrt(jnp.mean(v * v, axis=-1, keepdims=True) + EPS)
    normal = v * factor
    scaled = dn * gain[...]
    dx = factor * (scaled - normal * jnp.mean(scaled * normal, axis=-1, keepdims=True))
    out[...] = (dres[...] + dx).astype(BF16)


def finish(dproj, weight, tok, gain, dres):
    rows, model = tok.shape
    return pl.pallas_call(
        finish_kernel,
        in_specs=[VMEM] * 5,
        out_specs=VMEM,
        out_shape=sds((rows, model), BF16),
        compiler_params=params(40),
        cost_estimate=cost(2 * rows * model * weight.shape[1], 1e7),
        name="finish",
    )(dproj, weight, tok, gain, dres)


def shards(
    tokens,
    cotangent,
    lengths,
    routes,
    prior_routes,
    gain_attend,
    attend_in,
    attend_out,
    gain_mix,
    router,
    route_table,
    const_mix,
    const_vector,
    expert_in,
    expert_out,
):
    seqs = lax.axis_size("seq")
    fsdp = lax.axis_size("fsdp")
    here = lax.axis_index("seq")
    tok = tokens[0]
    rows, model = tok.shape
    shard = attend_in.shape[0]
    group = model // seqs
    width = 3 * group
    length = lengths[0]
    meta = jnp.stack([length, here]).astype(jnp.int32)

    own_in = attend_in.astype(BF16).reshape(shard, 3, seqs, group)
    own_heads = lax.dynamic_index_in_dim(own_in, here, 2, keepdims=False).reshape(shard, width)
    first = jnp.concatenate(
        [own_heads, gain_attend.astype(BF16)[:, None], jnp.zeros((shard, 63), BF16)], axis=1
    )
    first_all = everyone(first, "fsdp").reshape(model, width + 64)
    tok_all = lax.all_gather(tok, "seq", axis=0)

    in_mine = lax.dynamic_index_in_dim(expert_in, here, 0, keepdims=False).astype(BF16)
    out_mine = lax.dynamic_index_in_dim(expert_out, here, 0, keepdims=False).astype(BF16)
    small_shard = jnp.concatenate(
        [
            router.astype(BF16),
            const_mix.astype(BF16),
            const_vector.astype(BF16),
            gain_mix.astype(BF16)[:, None],
            jnp.zeros((shard, LANES - NE - 3 * NC - 1), BF16),
        ],
        axis=1,
    )
    second = jnp.concatenate([in_mine, attend_out.astype(BF16), small_shard], axis=1)
    second_all = lax.all_gather(second, "fsdp", axis=0, tiled=True)
    w_out = lax.all_gather(out_mine, "fsdp", axis=0, tiled=True)
    swapped = jnp.swapaxes(own_in, 1, 2).reshape(shard, seqs * width)
    back_w = lax.all_gather(swapped, "fsdp", axis=0, tiled=True)
    inner = w_out.shape[0]
    attend_w = second_all[:, 2 * inner : 2 * inner + model]
    rest = second_all[:, 2 * inner + model :]
    small_w = jnp.where(jnp.arange(LANES) < NE + 2 * NC, rest, 0).astype(BF16)
    vectors = jnp.transpose(rest[:, NE + 2 * NC : NE + 3 * NC + 1]).astype(F32)
    gain_m = vectors[NC : NC + 1]
    gain_a = first_all[:, width].astype(F32)[None]

    choices = routes[0]
    experts = jnp.arange(NE, dtype=jnp.int32)
    hits = jnp.any(choices[:, :, None] == experts[:EF], axis=1)
    order = jnp.arange(rows, dtype=jnp.int32)
    lower = (order[:, None] > order[None, :]).astype(BF16)
    ranks = mm(hits.astype(BF16), lower, 0, 1).astype(jnp.int32)
    ranks = jnp.where(jnp.transpose(hits), ranks, -1)
    slots = (ranks[:, None, :] == jnp.arange(CAP, dtype=jnp.int32)[None, :, None]).astype(BF16)
    prior_hits = jnp.sum((prior_routes[0][:, :, None] == experts).astype(F32), axis=1)
    prior = jnp.dot(prior_hits, route_table, precision=lax.Precision.HIGHEST)
    prior = jnp.pad(prior, ((0, 0), (0, LANES - NE)))
    spots = here * rows + order
    grad = jnp.where((spots < length)[:, None], cotangent[0], 0).astype(BF16)
    grad_rows = mm(slots.reshape(-1, rows), grad).astype(BF16)
    grad_rows = swap(grad_rows.reshape(seqs, CAP, model), "seq")

    inverse = jnp.exp(
        jnp.arange(HALF, dtype=F32) * (-2.0 * math.log(10000.0) / HEAD_DIM)
    )
    angles = jnp.arange(seqs * rows, dtype=F32).reshape(seqs, 1, rows) * inverse[None, :, None]
    cosine, sine = jnp.cos(angles), jnp.sin(angles)

    qkv, normed = project(tok_all, first_all, gain_a, cosine, sine, width)
    mixed, lse = attend(meta, qkv)
    att = swap(mixed, "seq").reshape(model, rows)
    resid, moe, sent, stats = route(
        att, attend_w, tok, gain_m, small_w, prior, choices, slots
    )
    sent = swap(sent, "seq")
    partial, small, grad_vec = local_part(resid, stats, grad, gain_m, vectors)

    block = 256
    back, hidden, dgate, dup, scaled = expert(meta, sent, grad_rows, second_all, w_out, block)
    back = swap(back, "seq")
    lanes = jnp.arange(LANES)
    share = sent[:, :, model:].astype(F32)
    gate = jnp.sum(jnp.where((lanes == here) | (lanes == here + NE), share, 0.0), axis=2)
    grad_in, grad_out, branch = expert_grads(
        sent, scaled, gate.reshape(-1, 1), hidden, dgate, dup, w_out, block
    )
    branch = swap(branch, "seq")
    grad_in = lax.psum_scatter(grad_in, "fsdp", scatter_dimension=1, tiled=True)
    grad_out = swap(grad_out.reshape(fsdp, -1, model), "fsdp").astype(F32).sum(axis=0)

    dres, dlow, datt, dsmall, dgain_m = unroute(
        back, slots, resid, small, stats, grad, gain_m, small_w, attend_w
    )
    dout = swap(datt.reshape(seqs, group, rows), "seq")
    dproj = attend_back(meta, qkv, dout, mixed, lse, cosine, sine)

    mixed_out = partial + mm(slots.reshape(-1, rows), branch.reshape(-1, model), 0, 0)
    mixed_out = mixed_out.astype(BF16)[None]
    grad_att_out = mm(att, dlow)
    high, low = two_parts(dsmall)
    grad_small = mm(moe, high, 0, 0) + mm(moe, low, 0, 0)
    grad_table = jnp.dot(
        jnp.transpose(prior_hits), dsmall[:, :NE], precision=lax.Precision.HIGHEST
    )
    table_high, table_low = two_parts(grad_table)
    table_rows = jnp.concatenate([table_high, table_low], axis=1)
    table_rows = jnp.pad(table_rows, ((0, shard - NE), (0, 0)))
    table_rows = jnp.broadcast_to(table_rows[None], (fsdp, shard, 2 * NE))
    dense = jnp.concatenate(
        [
            grad_att_out,
            grad_small[:, : NE + 2 * NC],
            grad_vec[:, :NC],
            jnp.transpose(dgain_m),
        ],
        axis=1,
    ).astype(BF16)
    dense = jnp.concatenate(
        [
            dense.reshape(fsdp, shard, -1),
            table_rows,
            jnp.zeros((fsdp, shard, LANES - NE - 3 * NC - 1 - 2 * NE), BF16),
        ],
        axis=2,
    )
    dense = swap(dense, "fsdp").astype(F32).sum(axis=0)
    at = model + NE + 3 * NC + 1
    table = dense[:, at : at + NE] + dense[:, at + NE : at + 2 * NE]
    high, low = two_parts(table)
    dense = jnp.concatenate([dense[:, :at].astype(BF16), high, low], axis=1)
    dense = everyone(dense, "seq").astype(F32).sum(axis=0)
    table = (dense[:, at : at + NE] + dense[:, at + NE :])[:NE]

    back_all = swap(dproj, "seq").reshape(seqs * width, rows)
    grad_tokens = finish(back_all, back_w, tok, gain_a, dres)[None]
    grad_heads = weight_grad(dproj, normed)
    grad_heads = swap(grad_heads.reshape(fsdp, shard, width), "fsdp").astype(F32).sum(axis=0)
    grad_heads = everyone(grad_heads.astype(BF16), "seq").astype(F32)
    grad_attend_in = jnp.transpose(
        grad_heads.reshape(seqs, shard, 3, group), (1, 2, 0, 3)
    ).reshape(shard, 3 * model)
    grad_gain_a = jnp.sum(
        own_in.reshape(shard, -1).astype(F32) * grad_attend_in, axis=1
    ) / gain_attend.astype(BF16).astype(F32)

    grad_in = everyone(jnp.swapaxes(grad_in, 0, 1).reshape(shard, -1), "seq").astype(F32)
    grad_out = everyone(grad_out.astype(BF16), "seq").astype(F32)
    return (
        mixed_out,
        grad_tokens,
        grad_gain_a,
        grad_attend_in,
        dense[:, :model],
        dense[:, at - 1],
        dense[:, model : model + NE],
        table,
        dense[:, model + NE : model + NE + 2 * NC],
        dense[:, model + NE + 2 * NC : model + NE + 3 * NC],
        grad_in,
        grad_out,
    )


def solution(mesh):
    placed = (
        P("fsdp", "seq", None),
        P("fsdp", "seq", None),
        P("fsdp"),
        P("fsdp", "seq", None),
        P("fsdp", "seq", None),
        P("fsdp"),
        P("fsdp", None),
        P("fsdp", None),
        P("fsdp"),
        P("fsdp", None),
        P(),
        P("fsdp", None),
        P("fsdp", None),
        P(None, "fsdp", None),
        P(None, "fsdp", None),
    )
    return jax.shard_map(
        shards,
        mesh=mesh,
        in_specs=placed,
        out_specs=(
            P("fsdp", "seq", None),
            P("fsdp", "seq", None),
            P("fsdp"),
            P("fsdp", None),
            P("fsdp", None),
            P("fsdp"),
            P("fsdp", None),
            P(),
            P("fsdp", None),
            P("fsdp", None),
            P(None, "fsdp", None),
            P(None, "fsdp", None),
        ),
        check_vma=False,
    )
```

```python
import functools
import math

import jax
import jax.numpy as jnp
from jax import lax
from jax.experimental import pallas as pl
from jax.experimental.pallas import tpu as pltpu
from jax.sharding import Mesh
from jax.sharding import PartitionSpec as P

HEADS = 12
HEAD_DIM = 64
HALF = HEAD_DIM // 2
NC = 2
EF = 4
NE = 8
CAP = 192
LANES = 128
SEQS = 4
SIDE = 4
YZ = ("fy", "fz")
FSDP = ("fy", "fz", "core")
ANY = pl.BlockSpec(memory_space=pl.ANY)
EPS = 1e-06
SCALE = HEAD_DIM ** (-0.5)
LOWEST = -1e30
F32 = jnp.float32
BF16 = jnp.bfloat16
VMEM = pl.BlockSpec(memory_space=pltpu.VMEM)
SMEM = pl.BlockSpec(memory_space=pltpu.SMEM)


def mm(a, b, ca=1, cb=0):
    return lax.dot_general(a, b, (((ca,), (cb,)), ((), ())), preferred_element_type=F32)


def params(mib, grid=None):
    if grid is None:
        return pltpu.CompilerParams(vmem_limit_bytes=mib << 20)
    return pltpu.CompilerParams(
        vmem_limit_bytes=mib << 20, dimension_semantics=("arbitrary",) * grid
    )


def sds(shape, dtype):
    return jax.ShapeDtypeStruct(shape, dtype)


def took(us):
    return pl.CostEstimate(flops=int(us * 1.1e9), bytes_accessed=1 << 16, transcendentals=0)


def far(x):
    return pltpu.with_memory_space_constraint(x, pltpu.HBM)


def hbm(shape, dtype):
    return pltpu.HBM(shape, dtype)


def whole(x):
    return pl.BlockSpec(x.shape, lambda i: (0,) * len(x.shape))


def one_step(body, us, meta, inputs, results, scratch=(), before=(), mib=14, near=0):
    inputs = [x if isinstance(x, tuple) else (x, whole(x)) for x in inputs]
    shapes = [(sds if k < near else hbm)(*r) for k, r in enumerate(results)]
    return pl.pallas_call(
        body,
        grid=(1,),
        in_specs=[SMEM] + [spec for _, spec in inputs] + [ANY] * len(before),
        out_specs=[VMEM if k < near else whole(r) for k, r in enumerate(shapes)],
        out_shape=shapes,
        scratch_shapes=list(scratch),
        compiler_params=params(mib, 1),
        cost_estimate=took(us),
        name=getattr(body, "func", body).__name__.removesuffix("_kernel"),
    )(meta, *[far(x) for x, _ in inputs], *map(far, before))


def shift(x, by):
    count = lax.axis_size("seq")
    return lax.ppermute(x, "seq", [(i, (i + by) % count) for i in range(count)])


def trade(x, by, axis="seq"):
    count = lax.axis_size(axis)
    return lax.ppermute(x, axis, [(i, i ^ by) for i in range(count)]) if by else x


def trades(pieces, axis="seq"):
    return [trade(piece, k, axis) for k, piece in enumerate(pieces)]


def around(meta, by):
    return lax.bitwise_xor(meta[1], by)


def swap(x, axis):
    return lax.all_to_all(x, axis, split_axis=0, concat_axis=0, tiled=True)


def two_parts(x):
    high = x.astype(BF16)
    return high, (x - high.astype(F32)).astype(BF16)


def lane_of(shape):
    return lax.broadcasted_iota(jnp.int32, shape, 1)


def pick(values, lanes, lane):
    return jnp.sum(jnp.where(lanes == lane, values, 0.0), axis=1, keepdims=True)


def tiles_moved(x, rows, columns):
    tiles = [
        x[r : r + 8, c : c + LANES]
        for r in range(0, x.shape[0], 8)
        for c in range(0, x.shape[1], LANES)
    ]
    count = columns // LANES
    lines = [jnp.concatenate(tiles[k : k + count], axis=1) for k in range(0, len(tiles), count)]
    return jnp.concatenate(lines, axis=0)


def pack_kernel(
    meta,
    attend_in,
    gain_a,
    attend_out,
    router,
    const_mix,
    const_vector,
    gain_m,
    w_in,
    w_out,
    first,
    second,
    back,
    in_mine,
    out_mine,
    sems,
):
    shard, model = attend_out.shape
    group = model // SEQS
    me = meta[1]
    in_copy = pltpu.make_async_copy(w_in.at[me], in_mine, sems.at[0])
    out_copy = pltpu.make_async_copy(w_out.at[me], out_mine, sems.at[1])
    in_copy.start()
    out_copy.start()
    used = NE + 3 * NC + 2
    rows = [router[...], const_mix[...], const_vector[...], gain_m[...], gain_a[...]]
    rows = jnp.concatenate([*rows, jnp.zeros((LANES - used, shard), F32)], axis=0)
    rows = jnp.concatenate([rows, jnp.zeros((LANES, LANES - shard), F32)], axis=1)
    small = jnp.transpose(rows)[:shard]
    lanes = lane_of(small.shape)

    pieces, own = [], []
    for k in range(3):
        parts = [
            attend_in[:, k * model + g * group : k * model + (g + 1) * group] for g in range(SEQS)
        ]
        mine = parts[0]
        for g in range(1, SEQS):
            mine = jnp.where(me == g, parts[g], mine)
        pieces.append(parts)
        own.append(mine)
    gain = pltpu.roll(small, LANES - (used - 1), 1)[:, :64]
    gain = jnp.where(lane_of(gain.shape) == 0, gain, 0.0)
    row = jnp.concatenate([*own, gain], axis=1).astype(BF16)
    first[...] = jnp.broadcast_to(row[None], first.shape)
    back[...] = jnp.concatenate(
        [pieces[k][g] for g in range(SEQS) for k in range(3)], axis=1
    ).astype(BF16)

    small = jnp.where(lanes < used - 1, small, 0.0)
    second[:, :model] = attend_out[...].astype(BF16)
    second[:, model : model + 2 * LANES] = jnp.concatenate(
        [small, jnp.zeros_like(small)], axis=1
    ).astype(BF16)
    at = model + 2 * LANES
    wide = in_mine.shape[1]
    in_copy.wait()
    second[:, at : at + wide] = in_mine[...].astype(BF16)
    out_copy.wait()
    at += wide
    second[:, at:] = tiles_moved(out_mine[...], shard, second.shape[1] - at).astype(BF16)


def pack(meta, attend_in, gain_a, attend_out, router, const_mix, const_vector, gain_m, w_in, w_out, count):
    shard, model = attend_out.shape
    wide = model + 2 * LANES + w_in.shape[2] + w_out.shape[1] * model // shard
    plain = (attend_in, gain_a, attend_out, router, const_mix, const_vector, gain_m)
    results = [
        sds((count, shard, 3 * model // SEQS + 64), BF16),
        sds((shard, wide), BF16),
        sds(attend_in.shape, BF16),
    ]
    return pl.pallas_call(
        pack_kernel,
        grid=(1,),
        in_specs=[SMEM] + [whole(x) for x in plain] + [ANY] * 2,
        out_specs=[whole(x) for x in results],
        out_shape=results,
        scratch_shapes=[
            pltpu.VMEM(w_in.shape[1:], F32),
            pltpu.VMEM(w_out.shape[1:], F32),
            pltpu.SemaphoreType.DMA((2,)),
        ],
        compiler_params=params(14, 1),
        cost_estimate=took(2),
        name="pack",
    )(meta, *map(far, (*plain, w_in, w_out)))


def project_kernel(meta, *refs):
    own, left, right, far0, far1, weight, gain, cosine, sine, qkv, normed = refs
    rows = own.shape[0]
    width = qkv.shape[1]
    part = width // 3
    for to, sources in ((0, (own,)), (3, (left,)), (1, (right,)), (2, (far0, far1))):
        place = lax.rem(meta[1] + to, SEQS)
        done = 0
        for source in sources:
            at = slice(done, done + source.shape[0])
            done = at.stop
            v = source[...].astype(F32)
            n = v * lax.rsqrt(jnp.mean(v * v, axis=-1, keepdims=True) + EPS) * gain[...]
            normed[place, at] = n.astype(BF16)
        flat = jnp.transpose(mm(normed[place], weight[:, :width]))
        c, s = cosine[place], sine[place]
        for which in range(2):
            factor = SCALE if which == 0 else 1.0
            for at in range(which * part, (which + 1) * part, HEAD_DIM):
                a, b = flat[at : at + HALF], flat[at + HALF : at + HEAD_DIM]
                qkv[place, at : at + HALF] = ((a * c - b * s) * factor).astype(BF16)
                qkv[place, at + HALF : at + HEAD_DIM] = ((b * c + a * s) * factor).astype(BF16)
        qkv[place, 2 * part :] = flat[2 * part :].astype(BF16)


def project(meta, sources, weight, gain, cosine, sine, width):
    rows, model = sources[0].shape
    results = [((SEQS, width, rows), BF16), ((SEQS, rows, model), BF16)]
    inputs = [*sources, weight, gain, cosine, sine]
    return one_step(project_kernel, 20, meta, inputs, results, mib=20, near=1)


def mask_diagonal(scores, start, length):
    keys = lax.broadcasted_iota(jnp.int32, scores.shape, 0)
    queries = lax.broadcasted_iota(jnp.int32, scores.shape, 1)
    return jnp.where((keys <= queries) & (keys + start < length), scores, LOWEST)


def attend_kernel(rounds, meta, qkv, *refs):
    outs, (top, total, acc) = refs[-2 * len(rounds) - 3 : -3], refs[-3:]
    rows = qkv.shape[2]
    part = qkv.shape[1] // 3
    heads = part // HEAD_DIM
    length = meta[0]
    spans = [
        [slice(k * part + h * HEAD_DIM, k * part + (h + 1) * HEAD_DIM) for k in range(3)]
        for h in range(heads)
    ]
    for n, by in enumerate(rounds):
        out, lse = outs[2 * n], outs[2 * n + 1]
        block = around(meta, by)
        for h, (at, k_at, v_at) in enumerate(spans):
            scores = mm(qkv[block, k_at], qkv[block, at], 0, 0)
            scores = mask_diagonal(scores, block * rows, length)
            peak = jnp.max(scores, axis=0, keepdims=True)
            e = jnp.exp(scores - peak)
            top[h : h + 1] = peak
            total[h : h + 1] = jnp.sum(e, axis=0, keepdims=True)
            acc[at] = mm(qkv[block, v_at], e.astype(BF16))

        def step(j, carry, block=block):
            for h, (at, k_at, v_at) in enumerate(spans):
                scores = mm(qkv[j, k_at], qkv[block, at], 0, 0)
                last = top[h : h + 1]
                peak = jnp.maximum(last, jnp.max(scores, axis=0, keepdims=True))
                e = jnp.exp(scores - peak)
                fade = jnp.exp(last - peak)
                top[h : h + 1] = peak
                total[h : h + 1] = total[h : h + 1] * fade + jnp.sum(e, axis=0, keepdims=True)
                acc[at] = acc[at] * fade + mm(qkv[j, v_at], e.astype(BF16))
            return carry

        lax.fori_loop(0, block, step, 0)
        for h, (at, _, _) in enumerate(spans):
            out[at] = (acc[at] / total[h : h + 1]).astype(BF16)
            lse[h : h + 1] = top[h : h + 1] + jnp.log(total[h : h + 1])


def attend(rounds, meta, qkv, *before):
    _, width, rows = qkv.shape
    part = width // 3
    return pl.pallas_call(
        functools.partial(attend_kernel, rounds),
        in_specs=[SMEM, VMEM] + [ANY] * len(before),
        out_specs=[VMEM] * (2 * len(rounds)),
        out_shape=[sds((part, rows), BF16), sds((8, rows), F32)] * len(rounds),
        scratch_shapes=[
            pltpu.VMEM((8, rows), F32),
            pltpu.VMEM((8, rows), F32),
            pltpu.VMEM((part, rows), F32),
        ],
        compiler_params=params(14),
        cost_estimate=took(50),
        name="attend",
    )(meta, qkv, *map(far, before))


def attend_back_kernel(last, meta, qkv, *refs):
    dout_in, out, lse_in = refs[:SEQS], refs[SEQS : 2 * SEQS], refs[2 * SEQS : 3 * SEQS]
    cosine, sine = refs[3 * SEQS : 3 * SEQS + 2]
    dout, lse, dq, dk, dv, dots = refs[-6:]
    dproj = refs[-8:-6] if last else refs[-11:-9]
    rounds = (3, 0) if last else (1, 2)
    held = refs[3 * SEQS + 2 : 3 * SEQS + 5] if last else refs[-9:-6]
    blocks, width, rows = qkv.shape
    part = width // 3
    heads = part // HEAD_DIM
    length = meta[0]
    sums = (dq, dk, dv)

    def pair(q, k, diagonal):
        for h in range(heads):
            at = slice(h * HEAD_DIM, (h + 1) * HEAD_DIM)
            k_at = slice(part + h * HEAD_DIM, part + (h + 1) * HEAD_DIM)
            v_at = slice(2 * part + h * HEAD_DIM, 2 * part + (h + 1) * HEAD_DIM)
            qh, kh, vh, doh = qkv[q, at], qkv[k, k_at], qkv[k, v_at], dout[q, at]
            scores = mm(kh, qh, 0, 0)
            if diagonal:
                scores = mask_diagonal(scores, k * rows, length)
            probs = jnp.exp(scores - lse[q, h : h + 1])
            dprobs = mm(vh, doh, 0, 0)
            low = probs.astype(BF16)
            dscores = (probs * (dprobs - dots[q, h : h + 1])).astype(BF16)
            dv[k, at] += mm(doh, low, 1, 1)
            dk[k, at] += mm(qh, dscores, 1, 1)
            dq[q, at] += mm(kh, dscores)

    for s in range(SEQS):
        b = around(meta, s)
        dout[b] = dout_in[s][...]
        lse[b] = lse_in[s][...]
        for h in range(heads):
            at = slice(h * HEAD_DIM, (h + 1) * HEAD_DIM)
            both = dout_in[s][at].astype(F32) * out[s][at].astype(F32)
            dots[b, h : h + 1] = jnp.sum(both, axis=0, keepdims=True)
    if last:
        for n, to in enumerate(rounds):
            for total, kept in zip(sums, held):
                total[around(meta, to)] = kept[n]
    else:
        for total in sums:
            total[...] = jnp.zeros_like(total)

    def diagonal(i, carry):
        b = around(meta, 3 * (1 - i) if last else 1 + i)
        pair(b, b, True)
        return carry

    def below(i, carry):
        first = around(meta, 3 if last else jnp.where(i < 3, 1, 2))
        second = around(meta, 0 if last else jnp.where(i == 0, 2, jnp.where(i % 2 == 1, 3, 0)))
        pair(jnp.maximum(first, second), jnp.minimum(first, second), False)
        return carry

    lax.fori_loop(0, 2, diagonal, 0)
    lax.fori_loop(0, 1 if last else 5, below, 0)
    for n, to in enumerate(rounds):
        b = around(meta, to)
        c, s = cosine[b], sine[b]
        for which, total in ((0, dq), (1, dk)):
            factor = SCALE if which == 0 else 1.0
            for h in range(heads):
                at = h * HEAD_DIM
                rounded = (total[b, at : at + HEAD_DIM] * factor).astype(BF16).astype(F32)
                x, y = rounded[:HALF], rounded[HALF:]
                at += which * part
                dproj[n][at : at + HALF] = (x * c + y * s).astype(BF16)
                dproj[n][at + HALF : at + HEAD_DIM] = (y * c - x * s).astype(BF16)
        dproj[n][2 * part :] = dv[b].astype(BF16)
    if not last:
        for n, to in enumerate((3, 0)):
            for total, kept in zip(sums, held):
                kept[n] = total[around(meta, to)]


def attend_back(meta, held, before, qkv, dout, out, lse, cosine, sine):
    blocks, width, rows = qkv.shape
    part = width // 3
    scratch = [pltpu.VMEM((blocks, part, rows), BF16), pltpu.VMEM((blocks, 8, rows), F32)]
    scratch += [pltpu.VMEM((blocks, part, rows), F32)] * 3
    scratch += [pltpu.VMEM((blocks, 8, rows), F32)]
    inputs = [qkv, *dout, *out, *lse, cosine, sine, *held]
    results = [((width, rows), BF16)] * 2
    if not held:
        results += [((2, part, rows), F32)] * 3
    body = functools.partial(attend_back_kernel, bool(held))
    return one_step(body, 50, meta, inputs, results, scratch, before, 40)


def route_kernel(meta, *refs):
    att = refs[:SEQS]
    out_w, small_w, tok, prior, routes, slots = refs[SEQS : SEQS + 6]
    sent = refs[SEQS + 6 : 2 * SEQS + 6]
    resid, moe, stats, vectors = refs[2 * SEQS + 6 :]
    group = att[0].shape[0]
    res = tok[...].astype(F32)
    for s in range(SEQS):
        at = pl.multiple_of(around(meta, s) * group, 64)
        res += mm(att[s][...], out_w[pl.ds(at, group)], 0, 0)
    flipped = jnp.transpose(small_w[...].astype(F32))
    vectors[...] = flipped[NE + 2 * NC : NE + 2 * NC + 8]
    gain = flipped[NE + 3 * NC : NE + 3 * NC + 1]
    resid[...] = res
    normed = res * lax.rsqrt(jnp.mean(res * res, axis=-1, keepdims=True) + EPS) * gain
    low = normed.astype(BF16)
    moe[...] = low
    small = mm(low, small_w[...])
    small = jnp.where(lane_of(small.shape) < NE + 2 * NC, small, 0.0)
    logits = small + prior[...]
    lanes = lane_of(small.shape)
    hit0 = lanes == routes[:, 0:1]
    hit1 = lanes == routes[:, 1:2]
    chosen0 = jnp.sum(jnp.where(hit0, logits, 0.0), axis=1, keepdims=True)
    chosen1 = jnp.sum(jnp.where(hit1, logits, 0.0), axis=1, keepdims=True)
    gate0 = 1.0 / (1.0 + jnp.exp(chosen1 - chosen0))
    gate1 = 1.0 / (1.0 + jnp.exp(chosen0 - chosen1))
    share = jnp.where(hit0, gate0, 0.0) + jnp.where(hit1, gate1, 0.0)
    partner = jnp.where(lanes % 2 == 0, pltpu.roll(small, LANES - 1, 1), pltpu.roll(small, 1, 1))
    mix = 1.0 / (1.0 + jnp.exp(partner - small))
    mixing = (lanes >= NE) & (lanes < NE + 2 * NC)
    stats[...] = share + jnp.where(mixing, mix, 0.0)
    high, rest = two_parts(share)
    parts = (high.astype(F32) + pltpu.roll(rest.astype(F32), NE, 1)).astype(BF16)
    model = low.shape[1]
    for s in range(SEQS):
        chosen = slots[around(meta, s)]
        sent[s][:, :model] = mm(chosen, low).astype(BF16)
        sent[s][:, model:] = mm(chosen, parts).astype(BF16)


def weight_blocks(weights):
    model = weights.shape[0]
    return [
        (weights, pl.BlockSpec((model, model), lambda i: (0, 0))),
        (weights, pl.BlockSpec((model, LANES), lambda i: (0, model // LANES))),
    ]


def route(meta, att, weights, tok, prior, routes, slots):
    rows, model = tok.shape
    results = [((CAP, model + LANES), BF16)] * SEQS + [
        ((rows, model), F32),
        ((rows, model), BF16),
        ((rows, LANES), F32),
        ((8, model), F32),
    ]
    inputs = [*att, *weight_blocks(weights), tok, prior, routes, slots]
    return one_step(route_kernel, 20, meta, inputs, results, mib=24)


def local_part_kernel(meta, resid, stats, grad, vectors, partial, small, grad_vec):
    gain = vectors[NC : NC + 1]
    res, g = resid[...], grad[...].astype(F32)
    normed = res * lax.rsqrt(jnp.mean(res * res, axis=-1, keepdims=True) + EPS) * gain
    held = stats[...]
    lanes = lane_of(held.shape)
    copy_dot = jnp.sum(g * normed, axis=1, keepdims=True)
    factor = pick(held, lanes, EF + 1)
    result = jnp.where(lanes == EF + 1, factor * copy_dot, 0.0)
    ways = jnp.zeros_like(held)
    added = jnp.zeros_like(res)
    for j in range(NC):
        row = vectors[j : j + 1]
        weight = pick(held, lanes, EF + 2 + j)
        first = pick(held, lanes, NE + 2 * j)
        second = pick(held, lanes, NE + 2 * j + 1)
        vec_dot = jnp.sum(g * row, axis=1, keepdims=True)
        mean = first * copy_dot + second * vec_dot
        result += jnp.where(lanes == EF + 2 + j, weight * mean, 0.0)
        result += jnp.where(lanes == NE + 2 * j, weight * first * (copy_dot - mean), 0.0)
        result += jnp.where(lanes == NE + 2 * j + 1, weight * second * (vec_dot - mean), 0.0)
        ways += jnp.where(lanes == j, weight * second, 0.0)
        added += (weight * second) * row
        factor += weight * first
    small[...] = result + jnp.where(lanes == NE + 2 * NC, factor, 0.0)
    partial[...] = res + factor * normed + added
    high, rest = two_parts(ways)
    grad_vec[...] = mm(grad[...], high, 0, 0) + mm(grad[...], rest, 0, 0)


def local_part(meta, resid, stats, grad, vectors):
    rows, model = resid.shape
    results = [((rows, model), F32), ((rows, LANES), F32), ((model, LANES), F32)]
    return one_step(local_part_kernel, 0.1, meta, [resid, stats, grad, vectors], results, mib=16)


def expert_kernel(meta, *refs):
    sent, grads = refs[:SEQS], refs[SEQS : 2 * SEQS]
    gate_w, up_w, out_w = refs[2 * SEQS + 1 : 2 * SEQS + 4]
    back = refs[2 * SEQS + 4 : 3 * SEQS + 4]
    rows, scaled, gate, hidden, dgate, dup, held, acc, dots = refs[3 * SEQS + 4 :]
    step = pl.program_id(0)
    count, model = rows.shape
    block = gate_w.shape[1]
    me = meta[1]

    @pl.when(step == 0)
    def _():
        for s in range(SEQS):
            at = slice(s * CAP, (s + 1) * CAP)
            rows[at] = sent[s][:, :model]
            held[at] = grads[s][...]
            parts = sent[s][:, model:].astype(F32)
            lanes = lane_of(parts.shape)
            own = (lanes == me) | (lanes == me + NE)
            share = jnp.sum(jnp.where(own, parts, 0.0), axis=1, keepdims=True)
            gate[at] = jnp.broadcast_to(share, (CAP, LANES))
            scaled[at] = (grads[s][...].astype(F32) * share).astype(BF16)
        acc[...] = jnp.zeros_like(acc)
        dots[...] = jnp.zeros_like(dots)

    for at in (slice(0, count // 2), slice(count // 2, count)):
        g = mm(rows[at], gate_w[...])
        u = mm(rows[at], up_w[...])
        v = mm(held[at], out_w[...], 1, 1)
        sig = 1.0 / (1.0 + jnp.exp(-g))
        silu = g * sig
        low = (silu * u).astype(BF16)
        hidden[at] = low
        both = v * low.astype(F32)
        folded = both[:, :LANES]
        for c in range(LANES, block, LANES):
            folded = folded + both[:, c : c + LANES]
        dots[at] += folded
        d = v * gate[at, 0:1]
        du = (d * silu).astype(BF16)
        dg = (d * u * (sig * (1.0 + g * (1.0 - sig)))).astype(BF16)
        dgate[at] = dg
        dup[at] = du
        acc[at] += mm(dg, gate_w[...], 1, 1) + mm(du, up_w[...], 1, 1)

    @pl.when(step == pl.num_programs(0) - 1)
    def _():
        for s in range(SEQS):
            at = slice(s * CAP, (s + 1) * CAP)
            back[s][:, :model] = acc[at].astype(BF16)
            value = jnp.sum(dots[at], axis=1, keepdims=True) * gate[at]
            lanes = lane_of(value.shape)
            high, rest = two_parts(value)
            back[s][:, model:] = (
                jnp.where(lanes == me, high.astype(F32), 0.0)
                + jnp.where(lanes == me + NE, rest.astype(F32), 0.0)
            ).astype(BF16)


def expert(meta, sent, grads, before, weights, w_out, block):
    count, model = SEQS * CAP, grads[0].shape[1]
    inner = w_out.shape[0]
    steps = inner // block
    skip = (model + 2 * LANES) // block
    results = [sds(sent[0].shape, BF16)] * SEQS + [
        sds((count, model), BF16),
        sds((count, model), BF16),
        sds((count, LANES), F32),
    ]
    return pl.pallas_call(
        expert_kernel,
        grid=(steps,),
        in_specs=[SMEM]
        + [whole(x) for x in (*sent, *grads)]
        + [
            ANY,
            pl.BlockSpec((model, block), lambda i: (0, i + skip)),
            pl.BlockSpec((model, block), lambda i: (0, i + skip + steps)),
            pl.BlockSpec((block, model), lambda i: (i, 0)),
        ],
        out_specs=[whole(x) for x in results]
        + [pl.BlockSpec((count, block), lambda i: (0, i))] * 3,
        out_shape=[hbm(r.shape, r.dtype) for r in results] + [hbm((count, inner), BF16)] * 3,
        scratch_shapes=[
            pltpu.VMEM((count, model), BF16),
            pltpu.VMEM((count, model), F32),
            pltpu.VMEM((count, LANES), F32),
        ],
        compiler_params=params(24, 1),
        cost_estimate=took(50),
        name="expert",
    )(meta, *map(far, (*sent, *grads, before, weights, weights, w_out)))


def expert_grads_kernel(
    meta, rows, scaled, gate, hidden, dgate, dup, out_w, in_kept, in_sent, out_kept, out_sent, *refs
):
    branch, (flipped, acc) = refs[:SEQS], refs[SEQS:]
    step = pl.program_id(0)
    half = pl.num_programs(0) // 2
    even = meta[2] == 0

    def halves(x, kept, sent):
        pairs, shard, wide = kept.shape
        x = x.reshape(pairs, 2 * shard, wide)
        first, second = x[:, :shard], x[:, shard:]
        kept[...] = jnp.where(even, first, second).astype(BF16)
        sent[...] = jnp.where(even, second, first).astype(BF16)

    @pl.when(step == 0)
    def _():
        for s in range(SEQS):
            flipped[:, s * CAP : (s + 1) * CAP] = jnp.transpose(rows[s * CAP : (s + 1) * CAP])
        acc[...] = jnp.zeros_like(acc)

    @pl.when(step < half)
    def _():
        halves(mm(flipped[...], dgate[...]), in_kept, in_sent)
        halves(mm(hidden[...], scaled[...], 0, 0), out_kept, out_sent)

    @pl.when(step >= half)
    def _():
        halves(mm(flipped[...], dup[...]), in_kept, in_sent)
        acc[...] += mm(hidden[...], out_w[...])

    @pl.when(step == pl.num_programs(0) - 1)
    def _():
        for s in range(SEQS):
            at = slice(s * CAP, (s + 1) * CAP)
            branch[s][...] = (acc[at] * gate[at, 0:1]).astype(BF16)


def expert_grads(meta, rows, scaled, gate, hidden, dgate, dup, w_out, block, fsdp):
    count, model = scaled.shape
    inner = w_out.shape[0]
    half = inner // block
    pairs = fsdp // 2
    in_rows, out_rows = model // fsdp, inner // fsdp
    per = block // (2 * out_rows)

    def low(i):
        return jnp.minimum(i, half - 1)

    def high(i):
        return jnp.maximum(i - half, 0)

    in_spec = pl.BlockSpec((pairs, in_rows, block), lambda i: (0, 0, i))
    out_spec = pl.BlockSpec((per, out_rows, model), lambda i: (low(i), 0, 0))
    return pl.pallas_call(
        expert_grads_kernel,
        grid=(2 * half,),
        in_specs=[
            SMEM,
            whole(rows),
            whole(scaled),
            whole(gate),
            pl.BlockSpec((count, block), lambda i: (0, lax.rem(i, half))),
            pl.BlockSpec((count, block), lambda i: (0, low(i))),
            pl.BlockSpec((count, block), lambda i: (0, high(i))),
            pl.BlockSpec((block, model), lambda i: (high(i), 0)),
        ],
        out_specs=[in_spec, in_spec, out_spec, out_spec]
        + [pl.BlockSpec((CAP, model), lambda i: (0, 0))] * SEQS,
        out_shape=[hbm((pairs, in_rows, 2 * inner), BF16)] * 2
        + [hbm((pairs, out_rows, model), BF16)] * 2
        + [hbm((CAP, model), BF16)] * SEQS,
        scratch_shapes=[pltpu.VMEM((model, count), BF16), pltpu.VMEM((count, model), F32)],
        compiler_params=params(24, 1),
        cost_estimate=took(50),
        name="expert_grads",
    )(meta, *map(far, (rows, scaled, gate, hidden, dgate, dup, w_out)))


def split_again(small):
    lanes = lane_of(small.shape)
    table = small + pltpu.roll(small, LANES - NE, 1)
    high = table.astype(BF16).astype(F32)
    rest = pltpu.roll(table - high, NE, 1)
    at = lanes // NE
    return jnp.where(at == 2, high, jnp.where(at == 3, rest, small))


def add_cores_kernel(meta, in_a, in_b, out_a, out_b, dense_a, dense_b, *refs):
    by_z, by_y = refs[-SIDE - 1], refs[-SIDE:]
    step = pl.program_id(0)
    shard, wide = in_a.shape[1:]
    half = by_z.shape[3]
    model = dense_a.shape[2] - LANES
    for k in range(SIDE):
        whole = in_a[k].astype(F32) + in_b[k].astype(F32)
        more = out_a[k].astype(F32) + out_b[k].astype(F32)
        more = tiles_moved(more, shard, 2 * half - wide - model - 2 * LANES)
        last = dense_a[k].astype(F32) + dense_b[k].astype(F32)
        small = split_again(last[:, model:])
        by_z[k, 0] = whole[:, :half].astype(BF16)
        rest = [whole[:, half:], more, last[:, :model], small, jnp.zeros((shard, LANES), F32)]
        rest = jnp.concatenate(rest, axis=1).astype(BF16)
        for to in range(SIDE):

            @pl.when(step == to)
            def _(to=to, rest=rest, k=k):
                by_y[to][k] = rest


def add_cores(meta, *parts):
    parts, before = parts[:6], parts[6:]
    pairs, shard, wide = parts[0].shape
    half = (wide + parts[2].shape[1] * parts[2].shape[2] // shard + parts[4].shape[2] + LANES) // 2

    def turned(i, meta):
        return lax.bitwise_xor(meta[3], i)

    def some(x):
        return pl.BlockSpec((SIDE, *x.shape[1:]), lambda i, meta: (turned(i, meta), 0, 0))

    return pl.pallas_call(
        add_cores_kernel,
        grid_spec=pltpu.PrefetchScalarGridSpec(
            num_scalar_prefetch=1,
            grid=(SIDE,),
            in_specs=[some(x) for x in parts] + [ANY] * len(before),
            out_specs=[
                pl.BlockSpec((SIDE, 1, shard, half), lambda i, meta: (0, turned(i, meta), 0, 0))
            ]
            + [pl.BlockSpec((SIDE, shard, half), lambda i, meta: (0, 0, 0))] * SIDE,
        ),
        out_shape=[hbm((SIDE, SIDE, shard, half), BF16)]
        + [hbm((SIDE, shard, half), BF16)] * SIDE,
        compiler_params=params(24, 1),
        cost_estimate=took(0.1),
        name="add_cores",
    )(meta, *map(far, (*parts, *before)))


def add_sides_kernel(meta, by_z, *refs):
    by_y, first, second = refs[:SIDE], refs[-SIDE - 1], refs[-SIDE:]
    for k in range(SIDE):
        total = by_z[0, k].astype(F32)
        for z in range(1, SIDE):
            total += by_z[z, k].astype(F32)
        first[k] = total.astype(BF16)
    for s in range(SIDE):
        k = lax.bitwise_xor(meta[4], s)
        total = by_y[0][k].astype(F32)
        for piece in by_y[1:]:
            total += piece[k].astype(F32)
        at = total.shape[1] - 2 * LANES
        small = split_again(total[:, at : at + LANES])
        total = jnp.concatenate([total[:, :at], small, total[:, at + LANES :]], axis=1)
        second[s][...] = total.astype(BF16)


def add_sides(meta, by_z, by_y, *before):
    _, shard, half = by_y[0].shape
    results = [((SIDE, shard, half), BF16)] + [((shard, half), BF16)] * SIDE
    return one_step(add_sides_kernel, 0.1, meta, [by_z, *by_y], results, (), before, 24)


def add_last_kernel(meta, first, *refs):
    half = first.shape[2]
    total = first[0].astype(F32)
    for k in range(1, SIDE):
        total += first[k].astype(F32)
    refs[-1][:, :half] = total.astype(BF16)
    total = refs[0][...].astype(F32)
    for piece in refs[1:SIDE]:
        total += piece[...].astype(F32)
    at = half - 2 * LANES
    small = split_again(total[:, at : at + LANES])
    total = jnp.concatenate([total[:, :at], small, total[:, at + LANES :]], axis=1)
    refs[-1][:, half:] = total.astype(BF16)


def add_last(meta, first, second, *before):
    _, shard, half = first.shape
    results = [((shard, 2 * half), BF16)]
    return one_step(add_last_kernel, 0.1, meta, [first, *second], results, (), before)[0]


def mixed_kernel(meta, partial, slots, *refs):
    result = partial[...]
    for s in range(SEQS):
        result += mm(slots[around(meta, s)], refs[s][...], 0, 0)
    refs[-1][...] = result.astype(BF16)


def mixed(meta, partial, slots, branch, *before):
    results = [(partial.shape, BF16)]
    (out,) = one_step(mixed_kernel, 50, meta, [partial, slots, *branch], results, (), before)
    return out


def unroute_kernel(meta, *refs):
    back = refs[:SEQS]
    out_w, small_w, slots, resid, small, stats, grad, vectors = refs[SEQS : SEQS + 8]
    datt = refs[-4 - SEQS : -4]
    dres, dlow, dlogits, dgain = refs[-4:]
    gain = vectors[NC : NC + 1]
    rows, model = resid.shape
    held, local = stats[...], small[...]
    lanes = lane_of(held.shape)
    dn = jnp.zeros((rows, model), F32)
    tail = jnp.zeros((rows, LANES), F32)
    for s in range(SEQS):
        chosen = slots[around(meta, s)]
        dn += mm(chosen, back[s][:, :model], 0, 0)
        tail += mm(chosen, back[s][:, model:], 0, 0)
    ffn = tail + pltpu.roll(tail, LANES - NE, 1)
    dots = jnp.where(lanes < EF, ffn, jnp.where(lanes < NE, local, 0.0))
    total = jnp.sum(dots, axis=1, keepdims=True)
    keep = (lanes >= NE) & (lanes < NE + 2 * NC)
    dsmall = jnp.where(lanes < NE, dots - held * total, jnp.where(keep, local, 0.0))
    dlogits[...] = dsmall
    high, rest = two_parts(dsmall)
    dn += mm(high, small_w[...], 1, 1) + mm(rest, small_w[...], 1, 1)
    g = grad[...].astype(F32)
    dn += pick(local, lanes, NE + 2 * NC) * g
    res = resid[...]
    factor = lax.rsqrt(jnp.mean(res * res, axis=-1, keepdims=True) + EPS)
    normal = res * factor
    dgain[...] = jnp.sum(dn * normal, axis=0, keepdims=True)
    scaled = dn * gain
    out = g + factor * (scaled - normal * jnp.mean(scaled * normal, axis=-1, keepdims=True))
    dres[...] = out
    low = out.astype(BF16)
    dlow[...] = low
    group = datt[0].shape[0]
    for s in range(SEQS):
        at = pl.multiple_of(around(meta, s) * group, 64)
        datt[s][...] = mm(out_w[pl.ds(at, group)], low, 1, 1).astype(BF16)


def unroute(meta, before, back, weights, slots, resid, small, stats, grad, vectors):
    rows, model = resid.shape
    inputs = [*back, *weight_blocks(weights), slots, resid, small, stats, grad, vectors]
    results = [((model // SEQS, rows), BF16)] * SEQS + [
        ((rows, model), F32),
        ((rows, model), BF16),
        ((rows, LANES), F32),
        ((1, model), F32),
    ]
    return one_step(unroute_kernel, 50, meta, inputs, results, (), before, 24)


def dense_kernel(meta, *refs):
    att = refs[:SEQS]
    dlow, moe, dlogits, grad_vec, dgain, prior_hits = refs[SEQS : SEQS + 6]
    kept, sent, flat = refs[-3:]
    pairs, shard, _ = kept.shape
    model = dlow.shape[1]
    even = meta[2] == 0
    group = model // SEQS
    for s in range(SEQS):
        at = pl.multiple_of(around(meta, s) * group, 64)
        flat[pl.ds(at, group)] = mm(att[s][...], dlow[...])
    full = flat[...].reshape(pairs, 2 * shard, model)
    kept[:, :, :model] = jnp.where(even, full[:, :shard], full[:, shard:]).astype(BF16)
    sent[:, :, :model] = jnp.where(even, full[:, shard:], full[:, :shard]).astype(BF16)
    high, rest = two_parts(dlogits[...])
    result = mm(moe[...], high, 0, 0) + mm(moe[...], rest, 0, 0)
    result += pltpu.roll(grad_vec[...], NE + 2 * NC, 1)
    lanes = lane_of(result.shape)
    column = jnp.transpose(jnp.broadcast_to(dgain[...], (LANES, model)))
    result += jnp.where(lanes == NE + 3 * NC, column, 0.0)
    table = mm(prior_hits[...], high, 0, 0) + mm(prior_hits[...], rest, 0, 0)
    table = jnp.where(lane_of((NE, LANES)) < NE, table[:NE], 0.0)
    high, rest = two_parts(table)
    block = pltpu.roll(high.astype(F32), 2 * NE, 1) + pltpu.roll(rest.astype(F32), 3 * NE, 1)
    block = jnp.concatenate([block, jnp.zeros((shard - NE, LANES), F32)], axis=0)
    full = result.reshape(pairs, 2 * shard, LANES)
    first, second = full[:, :shard] + block[None], full[:, shard:] + block[None]
    kept[:, :, model:] = jnp.where(even, first, second).astype(BF16)
    sent[:, :, model:] = jnp.where(even, second, first).astype(BF16)


def dense(meta, before, att, dlow, moe, dlogits, grad_vec, dgain, prior_hits, count):
    model = dlow.shape[1]
    inputs = [*att, dlow, moe, dlogits, grad_vec, dgain, prior_hits]
    results = [((count // 2, model // count, model + LANES), BF16)] * 2
    scratch = [pltpu.VMEM((model, model), F32)]
    return one_step(dense_kernel, 50, meta, inputs, results, scratch, before, 24)


def weight_grad_kernel(meta, *refs):
    dproj, normed, out = refs[:SEQS], refs[SEQS], refs[-1]
    total = mm(dproj[0][...], normed[around(meta, 0)])
    for s in range(1, SEQS):
        total += mm(dproj[s][...], normed[around(meta, s)])
    out[...] = jnp.transpose(total).reshape(out.shape).astype(BF16)


def weight_grad(meta, dproj, normed, count, *before):
    width = dproj[0].shape[0]
    model = normed.shape[2]
    results = [((count, model // count, width), BF16)]
    return one_step(weight_grad_kernel, 50, meta, [*dproj, normed], results, (), before, 24)[0]


def finish_kernel(meta, *refs):
    dproj, (weight, tok, gain, dres) = refs[:SEQS], refs[SEQS : SEQS + 4]
    out, flat = refs[-2:]
    width = dproj[0].shape[0]
    for s in range(SEQS):
        at = pl.multiple_of(around(meta, s) * width, 64)
        flat[pl.ds(at, width)] = dproj[s][...]
    dn = jnp.transpose(mm(weight[...], flat[...]))
    v = tok[...].astype(F32)
    factor = lax.rsqrt(jnp.mean(v * v, axis=-1, keepdims=True) + EPS)
    normal = v * factor
    scaled = dn * gain[...]
    dx = factor * (scaled - normal * jnp.mean(scaled * normal, axis=-1, keepdims=True))
    out[...] = (dres[...] + dx).astype(BF16)


def finish(meta, dproj, weight, tok, gain, dres, *before):
    width, rows = dproj[0].shape
    scratch = [pltpu.VMEM((SEQS * width, rows), BF16)]
    results = [(tok.shape, BF16)]
    inputs = [*dproj, weight, tok, gain, dres]
    return one_step(finish_kernel, 50, meta, inputs, results, scratch, before, 24)[0]


def gather_kernel(meta, *refs):
    pieces = refs[:SEQS]
    grad_in, grad_out, att_out, router, const_mix, const_vector, gain, table, held = refs[-9:]
    shard, model = att_out.shape
    wide = grad_in.shape[2]
    at = pieces[0].shape[1] - 2 * LANES - model
    for s in range(SEQS):
        place = around(meta, s)
        grad_in[place] = pieces[s][:, :wide].astype(F32)
        grad_out[place] = tiles_moved(pieces[s][:, wide:at].astype(F32), *grad_out.shape[1:])
        held[place] = pieces[s][:, at : at + model + LANES].astype(F32)
    total = held[0]
    for s in range(1, SEQS):
        total += held[s]
    att_out[...] = total[:, :model]
    small = jnp.concatenate([total[:, model:], jnp.zeros((LANES - shard, LANES), F32)], axis=0)
    both = small + pltpu.roll(small, LANES - NE, 1)
    table[...] = pltpu.roll(both, LANES - 2 * NE, 1)[:NE, :NE]
    small = jnp.transpose(small)[:, :shard]
    at = NE + 2 * NC
    router[...] = small[:NE]
    const_mix[...] = small[NE:at]
    const_vector[...] = small[at : at + NC]
    gain[...] = small[at + NC : at + NC + 1]


def gather(meta, pieces, wide, rows, model, *before):
    shard = pieces[0].shape[0]
    results = [(SEQS, shard, wide), (SEQS, rows, model)]
    results += [(shard, model), (NE, shard), (2 * NC, shard), (NC, shard), (1, shard), (NE, NE)]
    scratch = [pltpu.VMEM((SEQS, shard, model + LANES), F32)]
    results = [(r, F32) for r in results]
    return one_step(gather_kernel, 0.1, meta, pieces, results, scratch, before, 24)


def gather_heads_kernel(meta, *refs):
    pieces, attend_in, gain = refs[:SEQS], refs[SEQS], refs[SEQS + 1]
    out, grad_gain, held = refs[-3:]
    shard = out.shape[0]
    model = out.shape[1] // 3
    group = model // SEQS
    for s in range(SEQS):
        held[around(meta, s)] = pieces[s][...].astype(F32)
    order = [(k, g) for k in range(3) for g in range(SEQS)]
    full = jnp.concatenate([held[g][:, k * group : (k + 1) * group] for k, g in order], axis=1)
    out[...] = full
    low = attend_in[...].astype(BF16).astype(F32)
    column = jnp.sum(full * low, axis=1, keepdims=True)
    column = jnp.concatenate([column, jnp.zeros((LANES - shard, 1), F32)], axis=0)
    row = jnp.transpose(jnp.broadcast_to(column, (LANES, LANES)))[:1, :shard]
    grad_gain[...] = row / gain[...].astype(BF16).astype(F32)


def gather_heads(meta, pieces, attend_in, gain):
    shard, width = pieces[0].shape
    results = [((shard, SEQS * width), F32), ((1, shard), F32)]
    scratch = [pltpu.VMEM((SEQS, shard, width), F32)]
    return one_step(gather_heads_kernel, 0.1, meta, [*pieces, attend_in, gain], results, scratch)


def shards(
    tokens,
    cotangent,
    lengths,
    routes,
    prior_routes,
    gain_attend,
    attend_in,
    attend_out,
    gain_mix,
    router,
    route_table,
    const_mix,
    const_vector,
    expert_in,
    expert_out,
):
    seqs = lax.axis_size("seq")
    fsdp = lax.axis_size(FSDP)
    here = lax.axis_index("seq")
    tok = tokens[0]
    rows, model = tok.shape
    shard = attend_in.shape[0]
    group = model // seqs
    width = 3 * group
    length = lengths[0]
    meta = jnp.stack([length, here, *(lax.axis_index(a) for a in ("core", *YZ))])
    meta = meta.astype(jnp.int32)

    first, second, back_mine = pack(
        meta,
        attend_in,
        gain_attend[None],
        attend_out,
        router.T,
        const_mix.T,
        const_vector.T,
        gain_mix[None],
        expert_in,
        expert_out,
        fsdp,
    )
    first_all = swap(first, FSDP).reshape(model, width + 64)
    half = rows // 2
    left = shift(tok, 1)
    right = shift(tok, -1)
    far0 = shift(left[:half], 1)
    far1 = shift(right[half:], -1)
    weights = lax.all_gather(second, FSDP, axis=0, tiled=True)
    back_w = lax.all_gather(back_mine, FSDP, axis=0, tiled=True)
    inner = expert_out.shape[1] * fsdp
    wide = expert_out.shape[1] * model // shard
    w_out = weights[:, model + 2 * LANES + 2 * inner :]
    w_out = w_out.reshape(-1, shard // 8, 8, wide // LANES, LANES).transpose(0, 1, 3, 2, 4)
    w_out = w_out.reshape(-1, model // LANES, 8, LANES).transpose(0, 2, 1, 3).reshape(inner, model)
    gain_a = first_all[:, width].astype(F32)[None]

    choices = routes[0]
    experts = jnp.arange(NE, dtype=jnp.int32)
    hits = jnp.any(choices[:, :, None] == experts[:EF], axis=1)
    order = jnp.arange(rows, dtype=jnp.int32)
    lower = (order[:, None] > order[None, :]).astype(BF16)
    ranks = mm(hits.astype(BF16), lower, 0, 1).astype(jnp.int32)
    ranks = jnp.where(jnp.transpose(hits), ranks, -1)
    slots = (ranks[:, None, :] == jnp.arange(CAP, dtype=jnp.int32)[None, :, None]).astype(BF16)
    prior_hits = jnp.sum((prior_routes[0][:, :, None] == experts).astype(F32), axis=1)
    prior = jnp.dot(prior_hits, route_table, precision=lax.Precision.HIGHEST)
    prior = jnp.pad(prior, ((0, 0), (0, LANES - NE)))
    prior_hits = jnp.pad(prior_hits, ((0, 0), (0, LANES - NE))).astype(BF16)
    spots = here * rows + order
    grad = jnp.where((spots < length)[:, None], cotangent[0], 0).astype(BF16)
    inverse = jnp.exp(
        jnp.arange(HALF, dtype=F32) * (-2.0 * math.log(10000.0) / HEAD_DIM)
    )
    angles = jnp.arange(seqs * rows, dtype=F32).reshape(seqs, 1, rows) * inverse[None, :, None]
    cosine, sine = jnp.cos(angles), jnp.sin(angles)

    grad_rows = mm(slots.reshape(-1, rows), grad).astype(BF16).reshape(seqs, CAP, model)
    grad_rows = [
        lax.dynamic_index_in_dim(grad_rows, here ^ s, 0, keepdims=False)
        for s in range(seqs)
    ]
    left, right, *grad_rows = lax.optimization_barrier((left, right, *grad_rows))
    grad_rows = trades(grad_rows)

    qkv, normed = project(
        meta, [tok, left, right, far0, far1], first_all, gain_a, cosine, sine, width
    )
    mixed_by, lse = [None] * seqs, [None] * seqs
    mixed_by[1], lse[1], mixed_by[2], lse[2] = attend((1, 2), meta, qkv)
    mixed_by[3], lse[3], mixed_by[0], lse[0] = attend((3, 0), meta, qkv, lse[1], *grad_rows[1:])
    att = trades(mixed_by)
    *sent, resid, moe, stats, vectors = route(meta, att, weights, tok, prior, choices, slots)
    sent = trades(sent)
    partial, small, grad_vec = local_part(meta, resid, stats, grad, vectors)

    *back, row, scaled, gate, hidden, dgate, dup = expert(
        meta, sent, grad_rows, small, weights, w_out, 512
    )
    back = trades(back)
    in_kept, in_sent, out_kept, out_sent, *branch = expert_grads(
        meta, row, scaled, gate, hidden, dgate, dup, w_out, 512, fsdp
    )
    branch = trades(branch)
    in_come, out_come = trade(in_sent, 1, "core"), trade(out_sent, 1, "core")
    *datt, dres, dlow, dlogits, dgain_m = unroute(
        meta, (in_kept, back_w), back, weights, slots, resid, small, stats, grad, vectors
    )
    dout = trades(datt)
    kept, gone = dense(
        meta,
        (in_come, out_come, branch[1], branch[3]),
        att,
        dlow,
        moe,
        dlogits,
        grad_vec,
        dgain_m,
        prior_hits,
        fsdp,
    )
    come = trade(gone, 1, "core")
    by_z, *by_y = add_cores(meta, in_kept, in_come, out_kept, out_come, kept, come)
    both = by_z
    by_z, by_y = swap(by_z, "fz"), trades(by_y, "fy")
    state = (qkv, dout, mixed_by, lse, cosine, sine)
    dproj = [None] * seqs
    dproj[1], dproj[2], *held = attend_back(meta, (), (both,), *state)
    later = add_sides(meta, by_z, by_y, held[0], branch[2])
    dproj[3], dproj[0] = attend_back(meta, held, (later[0],), *state)
    back_all = trades(dproj)
    grad_heads = weight_grad(meta, dproj, normed, fsdp)
    by_y, *by_z = later
    part = add_last(meta, swap(by_y, "fy"), trades(by_z, "fz"), grad_heads)
    grad_heads = swap(grad_heads, FSDP)
    grad_tokens = finish(meta, back_all, back_w, tok, gain_a, dres, part)
    grad_heads, grad_tokens = lax.optimization_barrier((grad_heads, grad_tokens))
    grad_heads = grad_heads.astype(F32).sum(axis=0).astype(BF16)
    mixed_out = mixed(meta, partial, slots, branch, grad_heads)
    grad_in, grad_out, grad_att_out, grad_router, grad_mix, grad_vector, grad_gain_m, table = gather(
        meta, trades([part] * seqs), 2 * inner, expert_out.shape[1], model, mixed_out
    )
    grad_attend_in, grad_gain_a = gather_heads(
        meta, trades([grad_heads] * seqs), attend_in, gain_attend[None]
    )
    return (
        mixed_out[None],
        grad_tokens[None],
        grad_gain_a[0],
        grad_attend_in,
        grad_att_out,
        grad_gain_m[0],
        grad_router.T,
        table,
        grad_mix.T,
        grad_vector.T,
        grad_in,
        grad_out,
    )


def solution(mesh):
    fsdp = mesh.shape["fsdp"]
    finer = Mesh(
        mesh.devices.reshape(mesh.shape["seq"], fsdp // (2 * SIDE), SIDE, 2), ("seq", *FSDP)
    )
    placed = (
        P(FSDP, "seq", None),
        P(FSDP, "seq", None),
        P(FSDP),
        P(FSDP, "seq", None),
        P(FSDP, "seq", None),
        P(FSDP),
        P(FSDP, None),
        P(FSDP, None),
        P(FSDP),
        P(FSDP, None),
        P(),
        P(FSDP, None),
        P(FSDP, None),
        P(None, FSDP, None),
        P(None, FSDP, None),
    )
    return jax.shard_map(
        shards,
        mesh=finer,
        in_specs=placed,
        out_specs=(
            P(FSDP, "seq", None),
            P(FSDP, "seq", None),
            P(FSDP),
            P(FSDP, None),
            P(FSDP, None),
            P(FSDP),
            P(FSDP, None),
            P(),
            P(FSDP, None),
            P(FSDP, None),
            P(None, FSDP, None),
            P(None, FSDP, None),
        ),
        check_vma=False,
    )
```

```python
import functools
import math

import jax
import jax.numpy as jnp
from jax import lax
from jax.experimental import pallas as pl
from jax.experimental.pallas import tpu as pltpu
from jax.sharding import Mesh
from jax.sharding import PartitionSpec as P

HEADS = 12
HEAD_DIM = 64
HALF = HEAD_DIM // 2
NC = 2
EF = 4
NE = 8
CAP = 192
LANES = 128
SEQS = 4
SIDE = 4
YZ = ("fy", "fz")
FSDP = ("fy", "fz", "core")
ANY = pl.BlockSpec(memory_space=pl.ANY)
EPS = 1e-06
SCALE = HEAD_DIM ** (-0.5)
LOWEST = -1e30
F32 = jnp.float32
BF16 = jnp.bfloat16
VMEM = pl.BlockSpec(memory_space=pltpu.VMEM)
SMEM = pl.BlockSpec(memory_space=pltpu.SMEM)


def mm(a, b, ca=1, cb=0):
    return lax.dot_general(a, b, (((ca,), (cb,)), ((), ())), preferred_element_type=F32)


def params(mib, grid=None):
    if grid is None:
        return pltpu.CompilerParams(vmem_limit_bytes=mib << 20)
    return pltpu.CompilerParams(
        vmem_limit_bytes=mib << 20, dimension_semantics=("arbitrary",) * grid
    )


def sds(shape, dtype):
    return jax.ShapeDtypeStruct(shape, dtype)


def took(us):
    return pl.CostEstimate(flops=int(us * 1.1e9), bytes_accessed=1 << 16, transcendentals=0)


def far(x):
    return pltpu.with_memory_space_constraint(x, pltpu.HBM)


def hbm(shape, dtype):
    return pltpu.HBM(shape, dtype)


def whole(x):
    return pl.BlockSpec(x.shape, lambda i: (0,) * len(x.shape))


def come(*arrays):
    return [(x, whole(x)) for x in arrays]


def one_step(body, us, meta, inputs, results, scratch=(), before=(), mib=14, near=0):
    inputs = [x if isinstance(x, tuple) else (far(x), whole(x)) for x in inputs]
    shapes = [(sds if k < near else hbm)(*r) for k, r in enumerate(results)]
    return pl.pallas_call(
        body,
        grid=(1,),
        in_specs=[SMEM] + [spec for _, spec in inputs] + [ANY] * len(before),
        out_specs=[VMEM if k < near else whole(r) for k, r in enumerate(shapes)],
        out_shape=shapes,
        scratch_shapes=list(scratch),
        compiler_params=params(mib, 1),
        cost_estimate=took(us),
        name=getattr(body, "func", body).__name__.removesuffix("_kernel"),
    )(meta, *[x for x, _ in inputs], *map(far, before))


def shift(x, by):
    count = lax.axis_size("seq")
    return lax.ppermute(x, "seq", [(i, (i + by) % count) for i in range(count)])


def trade(x, by, axis="seq"):
    count = lax.axis_size(axis)
    return lax.ppermute(x, axis, [(i, i ^ by) for i in range(count)]) if by else x


def trades(pieces, axis="seq"):
    return [trade(piece, k, axis) for k, piece in enumerate(pieces)]


def around(meta, by):
    return lax.bitwise_xor(meta[1], by)


def swap(x, axis):
    return lax.all_to_all(x, axis, split_axis=0, concat_axis=0, tiled=True)


def two_parts(x):
    high = x.astype(BF16)
    return high, (x - high.astype(F32)).astype(BF16)


def lane_of(shape):
    return lax.broadcasted_iota(jnp.int32, shape, 1)


def pick(values, lanes, lane):
    return jnp.sum(jnp.where(lanes == lane, values, 0.0), axis=1, keepdims=True)


def tiles_moved(x, rows, columns):
    tiles = [
        x[r : r + 8, c : c + LANES]
        for r in range(0, x.shape[0], 8)
        for c in range(0, x.shape[1], LANES)
    ]
    count = columns // LANES
    lines = [jnp.concatenate(tiles[k : k + count], axis=1) for k in range(0, len(tiles), count)]
    return jnp.concatenate(lines, axis=0)


def pack_kernel(
    meta,
    attend_in,
    gain_a,
    attend_out,
    router,
    const_mix,
    const_vector,
    gain_m,
    w_in,
    w_out,
    first,
    second,
    back,
    in_mine,
    out_mine,
    sems,
):
    shard, model = attend_out.shape
    group = model // SEQS
    me = meta[1]
    in_copy = pltpu.make_async_copy(w_in.at[me], in_mine, sems.at[0])
    out_copy = pltpu.make_async_copy(w_out.at[me], out_mine, sems.at[1])
    in_copy.start()
    out_copy.start()
    used = NE + 3 * NC + 2
    rows = [router[...], const_mix[...], const_vector[...], gain_m[...], gain_a[...]]
    rows = jnp.concatenate([*rows, jnp.zeros((LANES - used, shard), F32)], axis=0)
    rows = jnp.concatenate([rows, jnp.zeros((LANES, LANES - shard), F32)], axis=1)
    small = jnp.transpose(rows)[:shard]
    lanes = lane_of(small.shape)

    pieces, own = [], []
    for k in range(3):
        parts = [
            attend_in[:, k * model + g * group : k * model + (g + 1) * group] for g in range(SEQS)
        ]
        mine = parts[0]
        for g in range(1, SEQS):
            mine = jnp.where(me == g, parts[g], mine)
        pieces.append(parts)
        own.append(mine)
    gain = pltpu.roll(small, LANES - (used - 1), 1)[:, :64]
    gain = jnp.where(lane_of(gain.shape) == 0, gain, 0.0)
    row = jnp.concatenate([*own, gain], axis=1).astype(BF16)
    first[...] = jnp.broadcast_to(row[None], first.shape)
    back[...] = jnp.concatenate(
        [pieces[k][g] for g in range(SEQS) for k in range(3)], axis=1
    ).astype(BF16)

    small = jnp.where(lanes < used - 1, small, 0.0)
    second[:, :model] = attend_out[...].astype(BF16)
    second[:, model : model + 2 * LANES] = jnp.concatenate(
        [small, jnp.zeros_like(small)], axis=1
    ).astype(BF16)
    at = model + 2 * LANES
    wide = in_mine.shape[1]
    in_copy.wait()
    second[:, at : at + wide] = in_mine[...].astype(BF16)
    out_copy.wait()
    at += wide
    second[:, at:] = tiles_moved(out_mine[...], shard, second.shape[1] - at).astype(BF16)


def pack(meta, attend_in, gain_a, attend_out, router, const_mix, const_vector, gain_m, w_in, w_out, count):
    shard, model = attend_out.shape
    wide = model + 2 * LANES + w_in.shape[2] + w_out.shape[1] * model // shard
    plain = (attend_in, gain_a, attend_out, router, const_mix, const_vector, gain_m)
    results = [
        sds((count, shard, 3 * model // SEQS + 64), BF16),
        sds((shard, wide), BF16),
        sds(attend_in.shape, BF16),
    ]
    return pl.pallas_call(
        pack_kernel,
        grid=(1,),
        in_specs=[SMEM] + [whole(x) for x in plain] + [ANY] * 2,
        out_specs=[whole(x) for x in results],
        out_shape=results,
        scratch_shapes=[
            pltpu.VMEM(w_in.shape[1:], F32),
            pltpu.VMEM(w_out.shape[1:], F32),
            pltpu.SemaphoreType.DMA((2,)),
        ],
        compiler_params=params(14, 1),
        cost_estimate=took(2),
        name="pack",
    )(meta, *map(far, (*plain, w_in, w_out)))


def plan_kernel(meta, routes, prior, table, cotangent, slots, grad, logits, counts, *sent):
    rows = routes.shape[1]
    width = cotangent.shape[1]
    ids = lax.broadcasted_iota(jnp.int32, (NE, rows), 0)
    hits = (ids == routes[0:1]) | (ids == routes[1:2])
    before = lax.broadcasted_iota(jnp.int32, (rows, rows), 0)
    before = before < lax.broadcasted_iota(jnp.int32, (rows, rows), 1)
    ranks = mm(jnp.where(hits, 1.0, 0.0).astype(BF16), jnp.where(before, 1.0, 0.0).astype(BF16))
    ranks = jnp.where(hits, ranks.astype(jnp.int32), -1)
    lines = lax.broadcasted_iota(jnp.int32, (CAP, rows), 0)
    for e in range(EF):
        slots[e] = jnp.where(lines == ranks[e : e + 1], 1.0, 0.0).astype(BF16)
    spots = lax.broadcasted_iota(jnp.int32, (rows, width), 0) + meta[1] * rows
    live = jnp.where(spots < meta[0], cotangent[...].astype(F32), 0.0).astype(BF16)
    grad[...] = live
    for s in range(SEQS):
        sent[s][...] = mm(slots[around(meta, s)], live).astype(BF16)
    count = (ids == prior[0:1]).astype(F32) + (ids == prior[1:2]).astype(F32)
    named = routes[...].astype(F32)
    flat = [count, named, jnp.zeros((LANES - NE - 2, rows), F32)]
    flat = jnp.transpose(jnp.concatenate(flat, axis=0))
    lanes = lane_of(flat.shape)
    count = jnp.where(lanes < NE, flat, 0.0).astype(BF16)
    counts[...] = count
    full = jnp.concatenate([table[...], jnp.zeros((NE, LANES - NE), F32)], axis=1)
    full = jnp.concatenate([full, jnp.zeros((LANES - NE, LANES), F32)], axis=0)
    total = jnp.zeros(flat.shape, F32)
    for _ in range(3):
        part = full.astype(BF16)
        full = full - part.astype(F32)
        total += mm(count, part)
    named = pltpu.roll(flat, NE, 1)
    logits[...] = jnp.where((lanes >= 2 * NE) & (lanes < 2 * NE + 2), named, total)


def plan(meta, routes, prior, table, cotangent):
    rows, model = cotangent.shape
    results = [
        ((EF, CAP, rows), BF16),
        ((rows, model), BF16),
        ((rows, LANES), F32),
        ((rows, LANES), BF16),
    ] + [((CAP, model), BF16)] * SEQS
    return one_step(plan_kernel, 1, meta, [routes, prior, table, cotangent], results, mib=24)


def project_kernel(meta, *refs):
    sources, (weight, gain, cosine, sine, qkv, normed) = refs[:5], refs[5:]
    width = qkv.shape[1]
    part = width // 3
    for to, which in ((0, (0,)), (3, (1,)), (1, (2,)), (2, (3, 4))):
        place = lax.rem(meta[1] + to, SEQS)
        done = 0
        for source in [sources[k] for k in which]:
            at = slice(done, done + source.shape[0])
            done = at.stop
            v = source[...].astype(F32)
            n = v * lax.rsqrt(jnp.mean(v * v, axis=-1, keepdims=True) + EPS) * gain[...]
            normed[place, at] = n.astype(BF16)
        flat = jnp.transpose(mm(normed[place], weight[:, :width]))
        c, s = cosine[place], sine[place]
        for which in range(2):
            factor = SCALE if which == 0 else 1.0
            for at in range(which * part, (which + 1) * part, HEAD_DIM):
                a, b = flat[at : at + HALF], flat[at + HALF : at + HEAD_DIM]
                qkv[place, at : at + HALF] = ((a * c - b * s) * factor).astype(BF16)
                qkv[place, at + HALF : at + HEAD_DIM] = ((b * c + a * s) * factor).astype(BF16)
        qkv[place, 2 * part :] = flat[2 * part :].astype(BF16)


def project(meta, sources, weight, gain, cosine, sine, width):
    rows, model = sources[0].shape
    results = [((SEQS, width, rows), BF16), ((SEQS, rows, model), BF16)]
    inputs = [*come(*sources, weight, gain), cosine, sine]
    return one_step(project_kernel, 100, meta, inputs, results, mib=20, near=1)


def mask_diagonal(scores, start, length):
    keys = lax.broadcasted_iota(jnp.int32, scores.shape, 0)
    queries = lax.broadcasted_iota(jnp.int32, scores.shape, 1)
    return jnp.where((keys <= queries) & (keys + start < length), scores, LOWEST)


def attend_kernel(meta, qkv, *refs):
    out, lse, top, total, acc = refs[-5:]
    rows = qkv.shape[2]
    part = qkv.shape[1] // 3
    heads = part // HEAD_DIM
    length = meta[0]
    spans = [
        [slice(k * part + h * HEAD_DIM, k * part + (h + 1) * HEAD_DIM) for k in range(3)]
        for h in range(heads)
    ]
    for block in range(SEQS):
        for h, (at, k_at, v_at) in enumerate(spans):
            scores = mm(qkv[block, k_at], qkv[block, at], 0, 0)
            scores = mask_diagonal(scores, block * rows, length)
            peak = jnp.max(scores, axis=0, keepdims=True)
            e = jnp.exp(scores - peak)
            top[h : h + 1] = peak
            total[h : h + 1] = jnp.sum(e, axis=0, keepdims=True)
            acc[at] = mm(qkv[block, v_at], e.astype(BF16))

        def step(j, carry, block=block):
            for h, (at, k_at, v_at) in enumerate(spans):
                scores = mm(qkv[j, k_at], qkv[block, at], 0, 0)
                last = top[h : h + 1]
                peak = jnp.maximum(last, jnp.max(scores, axis=0, keepdims=True))
                e = jnp.exp(scores - peak)
                fade = jnp.exp(last - peak)
                top[h : h + 1] = peak
                total[h : h + 1] = total[h : h + 1] * fade + jnp.sum(e, axis=0, keepdims=True)
                acc[at] = acc[at] * fade + mm(qkv[j, v_at], e.astype(BF16))
            return carry

        lax.fori_loop(0, block, step, 0)
        for h, (at, _, _) in enumerate(spans):
            out[block, at] = (acc[at] / total[h : h + 1]).astype(BF16)
            lse[block, h : h + 1] = top[h : h + 1] + jnp.log(total[h : h + 1])


def attend(meta, qkv):
    _, width, rows = qkv.shape
    part = width // 3
    results = [((SEQS, part, rows), BF16), ((SEQS, 8, rows), F32)]
    scratch = [
        pltpu.VMEM((8, rows), F32),
        pltpu.VMEM((8, rows), F32),
        pltpu.VMEM((part, rows), F32),
    ]
    inputs = [(qkv, VMEM)]
    return one_step(attend_kernel, 0.1, meta, inputs, results, scratch, mib=20)


def attend_back_kernel(meta, qkv, *refs):
    dout, out, lse, cosine, sine, normed = refs[:6]
    dproj = refs[-8 - SEQS : -8]
    kept, gone, dq, dk, dv, dots, normed_held, sem = refs[-8:]
    blocks, width, rows = qkv.shape
    part = width // 3
    heads = part // HEAD_DIM
    length = meta[0]

    normed_copy = pltpu.make_async_copy(normed, normed_held, sem)
    normed_copy.start()

    def pair(q, k, diagonal):
        for h in range(heads):
            at = slice(h * HEAD_DIM, (h + 1) * HEAD_DIM)
            k_at = slice(part + h * HEAD_DIM, part + (h + 1) * HEAD_DIM)
            v_at = slice(2 * part + h * HEAD_DIM, 2 * part + (h + 1) * HEAD_DIM)
            qh, kh, vh, doh = qkv[q, at], qkv[k, k_at], qkv[k, v_at], dout[q, at]
            scores = mm(kh, qh, 0, 0)
            if diagonal:
                scores = mask_diagonal(scores, k * rows, length)
            probs = jnp.exp(scores - lse[q, h : h + 1])
            dprobs = mm(vh, doh, 0, 0)
            low = probs.astype(BF16)
            dscores = (probs * (dprobs - dots[q, h : h + 1])).astype(BF16)
            if diagonal:
                dv[k, at] = mm(doh, low, 1, 1)
                dk[k, at] = mm(qh, dscores, 1, 1)
                dq[q, at] = mm(kh, dscores)
            else:
                dv[k, at] += mm(doh, low, 1, 1)
                dk[k, at] += mm(qh, dscores, 1, 1)
                dq[q, at] += mm(kh, dscores)

    for b in range(SEQS):
        for h in range(heads):
            at = slice(h * HEAD_DIM, (h + 1) * HEAD_DIM)
            both = dout[b, at].astype(F32) * out[b, at].astype(F32)
            dots[b, h : h + 1] = jnp.sum(both, axis=0, keepdims=True)

    def diagonal(b, carry):
        pair(b, b, True)
        return carry

    def below(q, carry):
        def one(k, inner):
            pair(q, k, False)
            return inner

        return lax.fori_loop(0, q, one, carry)

    lax.fori_loop(0, blocks, diagonal, 0)
    lax.fori_loop(1, blocks, below, 0)
    for to in range(SEQS):
        b = around(meta, to)
        c, s = cosine[b], sine[b]
        for which, held in ((0, dq), (1, dk)):
            factor = SCALE if which == 0 else 1.0
            for h in range(heads):
                at = h * HEAD_DIM
                rounded = (held[b, at : at + HEAD_DIM] * factor).astype(BF16).astype(F32)
                x, y = rounded[:HALF], rounded[HALF:]
                at += which * part
                dproj[to][at : at + HALF] = (x * c + y * s).astype(BF16)
                dproj[to][at + HALF : at + HEAD_DIM] = (y * c - x * s).astype(BF16)
        dproj[to][2 * part :] = dv[b].astype(BF16)

    normed_copy.wait()
    total = mm(dproj[0][...], normed_held[around(meta, 0)])
    for to in range(1, SEQS):
        total += mm(dproj[to][...], normed_held[around(meta, to)])
    pairs, shard, _ = kept.shape
    total = jnp.transpose(total).reshape(pairs, 2 * shard, width)
    even = meta[2] == 0
    kept[...] = jnp.where(even, total[:, :shard], total[:, shard:]).astype(BF16)
    gone[...] = jnp.where(even, total[:, shard:], total[:, :shard]).astype(BF16)


def attend_back(meta, before, qkv, dout, out, lse, cosine, sine, normed, count):
    blocks, width, rows = qkv.shape
    part = width // 3
    model = normed.shape[2]
    scratch = [pltpu.VMEM((blocks, part, rows), F32)] * 3
    scratch += [pltpu.VMEM((blocks, 8, rows), F32), pltpu.VMEM(normed.shape, BF16)]
    scratch += [pltpu.SemaphoreType.DMA]
    inputs = [*come(qkv, dout), out, lse, cosine, sine, (far(normed), ANY)]
    results = [((width, rows), BF16)] * SEQS
    results += [((count // 2, model // count, width), BF16)] * 2
    return one_step(attend_back_kernel, 100, meta, inputs, results, scratch, before, 48)


def route_kernel(meta, att, out_w, small_w, tok, prior, slots, *refs):
    sent = refs[-4 - SEQS : -4]
    resid, moe, stats, vectors = refs[-4:]
    res = tok[...].astype(F32) + mm(att[...], out_w[...], 0, 0)
    flipped = jnp.transpose(small_w[...].astype(F32))
    vectors[...] = flipped[NE + 2 * NC : NE + 2 * NC + 8]
    gain = flipped[NE + 3 * NC : NE + 3 * NC + 1]
    resid[...] = res
    normed = res * lax.rsqrt(jnp.mean(res * res, axis=-1, keepdims=True) + EPS) * gain
    low = normed.astype(BF16)
    moe[...] = low
    small = mm(low, small_w[...])
    small = jnp.where(lane_of(small.shape) < NE + 2 * NC, small, 0.0)
    lanes = lane_of(small.shape)
    known = prior[...]
    logits = small + jnp.where(lanes < NE, known, 0.0)
    named = lanes.astype(F32)
    hit0 = named == known[:, 2 * NE : 2 * NE + 1]
    hit1 = named == known[:, 2 * NE + 1 : 2 * NE + 2]
    chosen0 = jnp.sum(jnp.where(hit0, logits, 0.0), axis=1, keepdims=True)
    chosen1 = jnp.sum(jnp.where(hit1, logits, 0.0), axis=1, keepdims=True)
    gate0 = 1.0 / (1.0 + jnp.exp(chosen1 - chosen0))
    gate1 = 1.0 / (1.0 + jnp.exp(chosen0 - chosen1))
    share = jnp.where(hit0, gate0, 0.0) + jnp.where(hit1, gate1, 0.0)
    partner = jnp.where(lanes % 2 == 0, pltpu.roll(small, LANES - 1, 1), pltpu.roll(small, 1, 1))
    mix = 1.0 / (1.0 + jnp.exp(partner - small))
    mixing = (lanes >= NE) & (lanes < NE + 2 * NC)
    stats[...] = share + jnp.where(mixing, mix, 0.0)
    high, rest = two_parts(share)
    parts = (high.astype(F32) + pltpu.roll(rest.astype(F32), NE, 1)).astype(BF16)
    model = low.shape[1]
    for s in range(SEQS):
        chosen = slots[around(meta, s)]
        sent[s][:, :model] = mm(chosen, low).astype(BF16)
        sent[s][:, model:] = mm(chosen, parts).astype(BF16)


def weight_blocks(weights):
    model = weights.shape[0]
    return [
        (far(weights), pl.BlockSpec((model, model), lambda i: (0, 0))),
        (far(weights), pl.BlockSpec((model, LANES), lambda i: (0, model // LANES))),
    ]


def route(meta, att, weights, tok, prior, slots, *before):
    rows, model = tok.shape
    results = [((CAP, model + LANES), BF16)] * SEQS + [
        ((rows, model), F32),
        ((rows, model), BF16),
        ((rows, LANES), F32),
        ((8, model), F32),
    ]
    inputs = [*come(att), *weight_blocks(weights), tok, prior, slots]
    return one_step(route_kernel, 100, meta, inputs, results, (), before, 24)


def local_part_kernel(meta, resid, stats, grad, vectors, partial, small, grad_vec):
    gain = vectors[NC : NC + 1]
    res, g = resid[...], grad[...].astype(F32)
    normed = res * lax.rsqrt(jnp.mean(res * res, axis=-1, keepdims=True) + EPS) * gain
    held = stats[...]
    lanes = lane_of(held.shape)
    copy_dot = jnp.sum(g * normed, axis=1, keepdims=True)
    factor = pick(held, lanes, EF + 1)
    result = jnp.where(lanes == EF + 1, factor * copy_dot, 0.0)
    ways = jnp.zeros_like(held)
    added = jnp.zeros_like(res)
    for j in range(NC):
        row = vectors[j : j + 1]
        weight = pick(held, lanes, EF + 2 + j)
        first = pick(held, lanes, NE + 2 * j)
        second = pick(held, lanes, NE + 2 * j + 1)
        vec_dot = jnp.sum(g * row, axis=1, keepdims=True)
        mean = first * copy_dot + second * vec_dot
        result += jnp.where(lanes == EF + 2 + j, weight * mean, 0.0)
        result += jnp.where(lanes == NE + 2 * j, weight * first * (copy_dot - mean), 0.0)
        result += jnp.where(lanes == NE + 2 * j + 1, weight * second * (vec_dot - mean), 0.0)
        ways += jnp.where(lanes == j, weight * second, 0.0)
        added += (weight * second) * row
        factor += weight * first
    small[...] = result + jnp.where(lanes == NE + 2 * NC, factor, 0.0)
    partial[...] = res + factor * normed + added
    high, rest = two_parts(ways)
    grad_vec[...] = mm(grad[...], high, 0, 0) + mm(grad[...], rest, 0, 0)


def local_part(meta, resid, stats, grad, vectors):
    rows, model = resid.shape
    results = [((rows, model), F32), ((rows, LANES), F32), ((model, LANES), F32)]
    return one_step(local_part_kernel, 0.1, meta, [resid, stats, grad, vectors], results, mib=16)


def expert_kernel(meta, *refs):
    sent, grads = refs[:SEQS], refs[SEQS : 2 * SEQS]
    gate_w, up_w, out_w = refs[2 * SEQS + 1 : 2 * SEQS + 4]
    back = refs[2 * SEQS + 4 : 3 * SEQS + 4]
    rows, scaled, gate, hidden, dgate, dup, held, acc, dots = refs[3 * SEQS + 4 :]
    step = pl.program_id(0)
    count, model = rows.shape
    block = gate_w.shape[1]
    me = meta[1]

    @pl.when(step == 0)
    def _():
        for s in range(SEQS):
            at = slice(s * CAP, (s + 1) * CAP)
            rows[at] = sent[s][:, :model]
            held[at] = grads[s][...]
            parts = sent[s][:, model:].astype(F32)
            lanes = lane_of(parts.shape)
            own = (lanes == me) | (lanes == me + NE)
            share = jnp.sum(jnp.where(own, parts, 0.0), axis=1, keepdims=True)
            gate[at] = jnp.broadcast_to(share, (CAP, LANES))
            scaled[at] = (grads[s][...].astype(F32) * share).astype(BF16)
        acc[...] = jnp.zeros_like(acc)
        dots[...] = jnp.zeros_like(dots)

    for at in (slice(0, count // 2), slice(count // 2, count)):
        g = mm(rows[at], gate_w[...])
        u = mm(rows[at], up_w[...])
        v = mm(held[at], out_w[...], 1, 1)
        sig = 1.0 / (1.0 + jnp.exp(-g))
        silu = g * sig
        low = (silu * u).astype(BF16)
        hidden[at] = low
        both = v * low.astype(F32)
        folded = both[:, :LANES]
        for c in range(LANES, block, LANES):
            folded = folded + both[:, c : c + LANES]
        dots[at] += folded
        d = v * gate[at, 0:1]
        du = (d * silu).astype(BF16)
        dg = (d * u * (sig * (1.0 + g * (1.0 - sig)))).astype(BF16)
        dgate[at] = dg
        dup[at] = du
        acc[at] += mm(dg, gate_w[...], 1, 1) + mm(du, up_w[...], 1, 1)

    @pl.when(step == pl.num_programs(0) - 1)
    def _():
        for s in range(SEQS):
            at = slice(s * CAP, (s + 1) * CAP)
            back[s][:, :model] = acc[at].astype(BF16)
            value = jnp.sum(dots[at], axis=1, keepdims=True) * gate[at]
            lanes = lane_of(value.shape)
            high, rest = two_parts(value)
            back[s][:, model:] = (
                jnp.where(lanes == me, high.astype(F32), 0.0)
                + jnp.where(lanes == me + NE, rest.astype(F32), 0.0)
            ).astype(BF16)


def expert(meta, sent, grads, before, weights, w_out, block):
    count, model = SEQS * CAP, grads[0].shape[1]
    inner = w_out.shape[0]
    steps = inner // block
    skip = (model + 2 * LANES) // block
    results = [sds(sent[0].shape, BF16)] * SEQS + [
        sds((count, model), BF16),
        sds((count, model), BF16),
        sds((count, LANES), F32),
    ]
    return pl.pallas_call(
        expert_kernel,
        grid=(steps,),
        in_specs=[SMEM]
        + [whole(x) for x in (*sent, *grads)]
        + [
            ANY,
            pl.BlockSpec((model, block), lambda i: (0, i + skip)),
            pl.BlockSpec((model, block), lambda i: (0, i + skip + steps)),
            pl.BlockSpec((block, model), lambda i: (i, 0)),
        ],
        out_specs=[whole(x) for x in results]
        + [pl.BlockSpec((count, block), lambda i: (0, i))] * 3,
        out_shape=[hbm(r.shape, r.dtype) for r in results] + [hbm((count, inner), BF16)] * 3,
        scratch_shapes=[
            pltpu.VMEM((count, model), BF16),
            pltpu.VMEM((count, model), F32),
            pltpu.VMEM((count, LANES), F32),
        ],
        compiler_params=params(24, 1),
        cost_estimate=took(10),
        name="expert",
    )(meta, *sent, *grads, *map(far, (before, weights, weights, w_out)))


def expert_grads_kernel(
    meta, rows, scaled, gate, hidden, dgate, dup, out_w, before, *refs
):
    in_kept, in_sent, out_kept, out_sent = refs[:4]
    branch, (flipped, acc) = refs[4 : SEQS + 4], refs[SEQS + 4 :]
    step = pl.program_id(0)
    half = pl.num_programs(0) // 2
    even = meta[2] == 0

    def halves(x, kept, sent):
        pairs, shard, wide = kept.shape
        x = x.reshape(pairs, 2 * shard, wide)
        first, second = x[:, :shard], x[:, shard:]
        kept[...] = jnp.where(even, first, second).astype(BF16)
        sent[...] = jnp.where(even, second, first).astype(BF16)

    @pl.when(step == 0)
    def _():
        for s in range(SEQS):
            flipped[:, s * CAP : (s + 1) * CAP] = jnp.transpose(rows[s * CAP : (s + 1) * CAP])
        acc[...] = jnp.zeros_like(acc)

    @pl.when(step < half)
    def _():
        halves(mm(flipped[...], dgate[...]), in_kept, in_sent)
        halves(mm(hidden[...], scaled[...], 0, 0), out_kept, out_sent)

    @pl.when(step >= half)
    def _():
        halves(mm(flipped[...], dup[...]), in_kept, in_sent)
        acc[...] += mm(hidden[...], out_w[...])

    @pl.when(step == pl.num_programs(0) - 1)
    def _():
        for s in range(SEQS):
            at = slice(s * CAP, (s + 1) * CAP)
            branch[s][...] = (acc[at] * gate[at, 0:1]).astype(BF16)


def expert_grads(meta, rows, scaled, gate, hidden, dgate, dup, w_out, before, block, fsdp):
    count, model = scaled.shape
    inner = w_out.shape[0]
    half = inner // block
    pairs = fsdp // 2
    in_rows, out_rows = model // fsdp, inner // fsdp
    per = block // (2 * out_rows)

    def low(i):
        return jnp.minimum(i, half - 1)

    def high(i):
        return jnp.maximum(i - half, 0)

    in_spec = pl.BlockSpec((pairs, in_rows, block), lambda i: (0, 0, i))
    out_spec = pl.BlockSpec((per, out_rows, model), lambda i: (low(i), 0, 0))
    return pl.pallas_call(
        expert_grads_kernel,
        grid=(2 * half,),
        in_specs=[
            SMEM,
            whole(rows),
            whole(scaled),
            whole(gate),
            pl.BlockSpec((count, block), lambda i: (0, lax.rem(i, half))),
            pl.BlockSpec((count, block), lambda i: (0, low(i))),
            pl.BlockSpec((count, block), lambda i: (0, high(i))),
            pl.BlockSpec((block, model), lambda i: (high(i), 0)),
            ANY,
        ],
        out_specs=[in_spec, in_spec, out_spec, out_spec]
        + [pl.BlockSpec((CAP, model), lambda i: (0, 0))] * SEQS,
        out_shape=[hbm((pairs, in_rows, 2 * inner), BF16)] * 2
        + [hbm((pairs, out_rows, model), BF16)] * 2
        + [hbm((CAP, model), BF16)] * SEQS,
        scratch_shapes=[pltpu.VMEM((model, count), BF16), pltpu.VMEM((count, model), F32)],
        compiler_params=params(24, 1),
        cost_estimate=took(100),
        name="expert_grads",
    )(meta, *map(far, (rows, scaled, gate, hidden, dgate, dup, w_out, before)))


def split_again(small):
    lanes = lane_of(small.shape)
    table = small + pltpu.roll(small, LANES - NE, 1)
    high = table.astype(BF16).astype(F32)
    rest = pltpu.roll(table - high, NE, 1)
    at = lanes // NE
    return jnp.where(at == 2, high, jnp.where(at == 3, rest, small))


def add_cores_kernel(in_a, in_b, out_a, out_b, *refs):
    shard, wide = in_a.shape[1:]
    for k in range(in_a.shape[0]):
        both = refs[-1].at[k]
        both[:, :wide] = (in_a[k].astype(F32) + in_b[k].astype(F32)).astype(BF16)
        more = out_a[k].astype(F32) + out_b[k].astype(F32)
        both[:, wide:] = tiles_moved(more, shard, both.shape[1] - wide).astype(BF16)


def add_cores(parts, *before):
    pairs, shard, wide = parts[0].shape
    more = parts[2].shape[1] * parts[2].shape[2] // shard

    def some(shape):
        return pl.BlockSpec((SIDE, *shape), lambda i: (i, 0, 0))

    return pl.pallas_call(
        add_cores_kernel,
        grid=(pairs // SIDE,),
        in_specs=[some(x.shape[1:]) for x in parts] + [ANY] * len(before),
        out_specs=some((shard, wide + more)),
        out_shape=hbm((pairs, shard, wide + more), BF16),
        compiler_params=params(24, 1),
        cost_estimate=took(100),
        name="add_cores",
    )(*[x if k % 2 else far(x) for k, x in enumerate(parts)], *map(far, before))


def add_dense_kernel(meta, dense_a, dense_b, heads_a, heads_b, out):
    pairs, shard, wide = dense_a.shape
    width, model = heads_a.shape[2], wide - LANES
    for k in range(pairs):
        total = dense_a[k].astype(F32) + dense_b[k].astype(F32)
        out[k, :, :model] = total[:, :model].astype(BF16)
        out[k, :, model:wide] = split_again(total[:, model:]).astype(BF16)
        heads = heads_a[k].astype(F32) + heads_b[k].astype(F32)
        rest = jnp.zeros((shard, out.shape[2] - wide - width), F32)
        out[k, :, wide:] = jnp.concatenate([heads, rest], axis=1).astype(BF16)


def add_dense(meta, kept, come_dense, heads, come_heads):
    pairs, shard, wide = kept.shape
    results = [((pairs, shard, -(-(wide + heads.shape[2]) // LANES) * LANES), BF16)]
    inputs = [kept, *come(come_dense), heads, *come(come_heads)]
    return one_step(add_dense_kernel, 0.1, meta, inputs, results, mib=24)[0]


def add_pieces_kernel(meta, pieces, *refs):
    total = pieces[0].astype(F32)
    for k in range(1, pieces.shape[0]):
        total += pieces[k].astype(F32)
    model = pieces.shape[0] * pieces.shape[1] * 2
    small = split_again(total[:, model : model + LANES])
    refs[-1][:, :model] = total[:, :model].astype(BF16)
    refs[-1][:, model : model + LANES] = small.astype(BF16)
    refs[-1][:, model + LANES :] = total[:, model + LANES :].astype(BF16)


def add_pieces(meta, pieces, *before):
    results = [(pieces.shape[1:], BF16)]
    return one_step(add_pieces_kernel, 0.1, meta, come(pieces), results, (), before, 24)[0]


def mixed_kernel(meta, partial, slots, *refs):
    result = partial[...]
    for s in range(SEQS):
        result += mm(slots[around(meta, s)], refs[s][...], 0, 0)
    refs[-1][...] = result.astype(BF16)


def mixed(meta, partial, slots, branch, *before):
    results = [(partial.shape, BF16)]
    (out,) = one_step(mixed_kernel, 0.1, meta, [partial, slots, *come(*branch)], results, (), before)
    return out


def unroute_kernel(meta, *refs):
    back = refs[:SEQS]
    out_w, small_w, slots, resid, small, stats, grad, vectors = refs[SEQS : SEQS + 8]
    att, moe, grad_vec, prior_hits = refs[SEQS + 8 : SEQS + 12]
    datt = refs[-4]
    dres, kept, sent = refs[-3:]
    pairs, shard, _ = kept.shape
    even = meta[2] == 0
    gain = vectors[NC : NC + 1]
    rows, model = resid.shape
    held, local = stats[...], small[...]
    lanes = lane_of(held.shape)
    dn = jnp.zeros((rows, model), F32)
    tail = jnp.zeros((rows, LANES), F32)
    for s in range(SEQS):
        chosen = slots[around(meta, s)]
        dn += mm(chosen, back[s][:, :model], 0, 0)
        tail += mm(chosen, back[s][:, model:], 0, 0)
    ffn = tail + pltpu.roll(tail, LANES - NE, 1)
    dots = jnp.where(lanes < EF, ffn, jnp.where(lanes < NE, local, 0.0))
    total = jnp.sum(dots, axis=1, keepdims=True)
    keep = (lanes >= NE) & (lanes < NE + 2 * NC)
    dsmall = jnp.where(lanes < NE, dots - held * total, jnp.where(keep, local, 0.0))
    high, rest = two_parts(dsmall)
    dn += mm(high, small_w[...], 1, 1) + mm(rest, small_w[...], 1, 1)
    g = grad[...].astype(F32)
    dn += pick(local, lanes, NE + 2 * NC) * g
    res = resid[...]
    factor = lax.rsqrt(jnp.mean(res * res, axis=-1, keepdims=True) + EPS)
    normal = res * factor
    dgain = jnp.sum(dn * normal, axis=0, keepdims=True)
    scaled = dn * gain
    out = g + factor * (scaled - normal * jnp.mean(scaled * normal, axis=-1, keepdims=True))
    dres[...] = out
    low = out.astype(BF16)
    datt[...] = mm(out_w[...], low, 1, 1).astype(BF16)
    full = mm(att[...], low).reshape(pairs, 2 * shard, model)
    kept[:, :, :model] = jnp.where(even, full[:, :shard], full[:, shard:]).astype(BF16)
    sent[:, :, :model] = jnp.where(even, full[:, shard:], full[:, :shard]).astype(BF16)
    result = mm(moe[...], high, 0, 0) + mm(moe[...], rest, 0, 0)
    result += pltpu.roll(grad_vec[...], NE + 2 * NC, 1)
    lanes = lane_of(result.shape)
    column = jnp.transpose(jnp.broadcast_to(dgain, (LANES, model)))
    result += jnp.where(lanes == NE + 3 * NC, column, 0.0)
    table = mm(prior_hits[...], high, 0, 0) + mm(prior_hits[...], rest, 0, 0)
    table = jnp.where(lane_of((NE, LANES)) < NE, table[:NE], 0.0)
    high, rest = two_parts(table)
    block = pltpu.roll(high.astype(F32), 2 * NE, 1) + pltpu.roll(rest.astype(F32), 3 * NE, 1)
    block = jnp.concatenate([block, jnp.zeros((shard - NE, LANES), F32)], axis=0)
    full = result.reshape(pairs, 2 * shard, LANES)
    first, second = full[:, :shard] + block[None], full[:, shard:] + block[None]
    kept[:, :, model:] = jnp.where(even, first, second).astype(BF16)
    sent[:, :, model:] = jnp.where(even, second, first).astype(BF16)


def unroute(meta, before, back, weights, tokenwise, att, moe, grad_vec, prior_hits, count):
    resid = tokenwise[1]
    rows, model = resid.shape
    inputs = [*come(*back), *weight_blocks(weights), *tokenwise, att, moe, grad_vec, prior_hits]
    results = [((model, rows), BF16), ((rows, model), F32)]
    results += [((count // 2, model // count, model + LANES), BF16)] * 2
    return one_step(unroute_kernel, 100, meta, inputs, results, (), before, 32)


def finish_kernel(meta, *refs):
    dproj, (weight, tok, gain, dres) = refs[:SEQS], refs[SEQS : SEQS + 4]
    out, flat = refs[-2:]
    width = dproj[0].shape[0]
    for s in range(SEQS):
        at = pl.multiple_of(around(meta, s) * width, 64)
        flat[pl.ds(at, width)] = dproj[s][...]
    dn = jnp.transpose(mm(weight[...], flat[...]))
    v = tok[...].astype(F32)
    factor = lax.rsqrt(jnp.mean(v * v, axis=-1, keepdims=True) + EPS)
    normal = v * factor
    scaled = dn * gain[...]
    dx = factor * (scaled - normal * jnp.mean(scaled * normal, axis=-1, keepdims=True))
    out[...] = (dres[...] + dx).astype(BF16)


def finish(meta, dproj, weight, tok, gain, dres, *before):
    width, rows = dproj[0].shape
    scratch = [pltpu.VMEM((SEQS * width, rows), BF16)]
    results = [(tok.shape, BF16)]
    inputs = [*come(*dproj), weight, tok, gain, dres]
    return one_step(finish_kernel, 0.1, meta, inputs, results, scratch, before, 24)[0]


def gather_kernel(meta, *refs):
    pieces = refs[:SEQS]
    grad_in, grad_out = refs[-2:]
    wide = grad_in.shape[2]
    for s in range(SEQS):
        place = around(meta, s)
        grad_in[place] = pieces[s][:, :wide].astype(F32)
        grad_out[place] = tiles_moved(pieces[s][:, wide:].astype(F32), *grad_out.shape[1:])


def gather(meta, pieces, wide, rows, model, *before):
    shard = pieces[0].shape[0]
    results = [((SEQS, shard, wide), F32), ((SEQS, rows, model), F32)]
    return one_step(gather_kernel, 0.1, meta, come(*pieces), results, (), before, 24)


def gather_dense_kernel(meta, *refs):
    pieces, attend_in, gain_a = refs[:SEQS], refs[SEQS], refs[SEQS + 1]
    att_in, grad_gain, att_out, router, const_mix, const_vector, gain, table, held = refs[-9:]
    shard, model = att_out.shape
    group = model // SEQS
    at = model + LANES
    for s in range(SEQS):
        held[around(meta, s)] = pieces[s][...].astype(F32)
    order = [(k, g) for k in range(3) for g in range(SEQS)]
    parts = [held[g][:, at + k * group : at + (k + 1) * group] for k, g in order]
    full = jnp.concatenate(parts, axis=1)
    att_in[...] = full
    low = attend_in[...].astype(BF16).astype(F32)
    column = jnp.sum(full * low, axis=1, keepdims=True)
    column = jnp.concatenate([column, jnp.zeros((LANES - shard, 1), F32)], axis=0)
    row = jnp.transpose(jnp.broadcast_to(column, (LANES, LANES)))[:1, :shard]
    grad_gain[...] = row / gain_a[...].astype(BF16).astype(F32)

    total = held[0][:, :at]
    for s in range(1, SEQS):
        total += held[s][:, :at]
    att_out[...] = total[:, :model]
    small = jnp.concatenate([total[:, model:], jnp.zeros((LANES - shard, LANES), F32)], axis=0)
    both = small + pltpu.roll(small, LANES - NE, 1)
    table[...] = pltpu.roll(both, LANES - 2 * NE, 1)[:NE, :NE]
    small = jnp.transpose(small)[:, :shard]
    at = NE + 2 * NC
    router[...] = small[:NE]
    const_mix[...] = small[NE:at]
    const_vector[...] = small[at : at + NC]
    gain[...] = small[at + NC : at + NC + 1]


def gather_dense(meta, pieces, attend_in, gain):
    shard, wide = pieces[0].shape
    model = attend_in.shape[1] // 3
    results = [attend_in.shape, (1, shard), (shard, model), (NE, shard), (2 * NC, shard)]
    results = [(r, F32) for r in (*results, (NC, shard), (1, shard), (NE, NE))]
    scratch = [pltpu.VMEM((SEQS, shard, wide), F32)]
    inputs = [*come(*pieces), attend_in, gain]
    return one_step(gather_dense_kernel, 0.1, meta, inputs, results, scratch, mib=16)


def shards(
    tokens,
    cotangent,
    lengths,
    routes,
    prior_routes,
    gain_attend,
    attend_in,
    attend_out,
    gain_mix,
    router,
    route_table,
    const_mix,
    const_vector,
    expert_in,
    expert_out,
):
    seqs = lax.axis_size("seq")
    fsdp = lax.axis_size(FSDP)
    here = lax.axis_index("seq")
    tok = tokens[0]
    rows, model = tok.shape
    shard = attend_in.shape[0]
    group = model // seqs
    width = 3 * group
    length = lengths[0]
    meta = jnp.stack([length, here, *(lax.axis_index(a) for a in ("core", *YZ))])
    meta = meta.astype(jnp.int32)

    first, second, back_mine = pack(
        meta,
        attend_in,
        gain_attend[None],
        attend_out,
        router.T,
        const_mix.T,
        const_vector.T,
        gain_mix[None],
        expert_in,
        expert_out,
        fsdp,
    )
    first_all = swap(first, FSDP).reshape(model, width + 64)
    half = rows // 2
    left, right = shift(tok, 1), shift(tok, -1)
    far0, far1 = shift(left[:half], 1), shift(right[half:], -1)
    weights = lax.all_gather(second, FSDP, axis=0, tiled=True)
    back_w = lax.all_gather(back_mine, FSDP, axis=0, tiled=True)
    inner = expert_out.shape[1] * fsdp
    wide = expert_out.shape[1] * model // shard
    w_out = weights[:, model + 2 * LANES + 2 * inner :]
    w_out = w_out.reshape(-1, shard // 8, 8, wide // LANES, LANES).transpose(0, 1, 3, 2, 4)
    w_out = w_out.reshape(-1, model // LANES, 8, LANES).transpose(0, 2, 1, 3).reshape(inner, model)
    gain_a = first_all[:, width].astype(F32)[None]

    slots, grad, prior, prior_hits, *grad_rows = plan(
        meta, routes[0].T, prior_routes[0].T, route_table, cotangent[0]
    )
    inverse = jnp.exp(
        jnp.arange(HALF, dtype=F32) * (-2.0 * math.log(10000.0) / HEAD_DIM)
    )
    angles = jnp.arange(seqs * rows, dtype=F32).reshape(seqs, 1, rows) * inverse[None, :, None]
    cosine, sine = jnp.cos(angles), jnp.sin(angles)

    left, right, *grad_rows = lax.optimization_barrier((left, right, *grad_rows))
    grad_rows = trades(grad_rows)

    qkv, normed = project(
        meta, [tok, left, right, far0, far1], first_all, gain_a, cosine, sine, width
    )
    held, lse = attend(meta, qkv)
    held, *grad_rows = lax.optimization_barrier((held, *grad_rows))
    att = swap(held, "seq").reshape(model, rows)
    *sent, resid, moe, stats, vectors = route(meta, att, weights, tok, prior, slots)
    sent = trades(sent)
    partial, small, grad_vec = local_part(meta, resid, stats, grad, vectors)

    *back, row, scaled, gate, hidden, dgate, dup = expert(
        meta, sent, grad_rows, small, weights, w_out, 512
    )
    back = trades(back)
    in_kept, in_sent, out_kept, out_sent, *branch = expert_grads(
        meta, row, scaled, gate, hidden, dgate, dup, w_out, back_w, 512, fsdp
    )
    in_come, out_come = trade(in_sent, 1, "core"), trade(out_sent, 1, "core")
    tokenwise = (slots, resid, small, stats, grad, vectors)
    datt, dres, kept, gone = unroute(
        meta, (in_kept,), back, weights, tokenwise, att, moe, grad_vec, prior_hits, fsdp
    )
    come_dense = trade(gone, 1, "core")
    dout = swap(datt.reshape(seqs, group, rows), "seq")
    both = add_cores((in_kept, in_come, out_kept, out_come), dres)
    both, *branch = lax.optimization_barrier((both, *branch))
    branch = trades(branch)
    part = both.reshape(-1, both.shape[2])
    part = lax.psum_scatter(part, YZ, scatter_dimension=0, tiled=True)
    *dproj, heads, gone = attend_back(
        meta, (both, come_dense), qkv, dout, held, lse, cosine, sine, normed, fsdp
    )
    mixed_out = mixed(meta, partial, slots, branch, heads)
    gone, mixed_out, *dproj = lax.optimization_barrier((gone, mixed_out, *dproj))
    come_heads = trade(gone, 1, "core")
    back_all = trades(dproj)
    dense = add_dense(meta, kept, come_dense, heads, come_heads)
    dense = swap(dense, YZ)
    dense = add_pieces(meta, dense)
    grad_tokens = finish(meta, back_all, back_w, tok, gain_a, dres, dense)
    grad_attend_in, grad_gain_a, grad_att_out, *rest, table = gather_dense(
        meta, trades([dense] * seqs), attend_in, gain_attend[None]
    )
    grad_router, grad_mix, grad_vector, grad_gain_m = rest
    part, grad_tokens, grad_gain_a = lax.optimization_barrier((part, grad_tokens, grad_gain_a))
    grad_in, grad_out = gather(
        meta, trades([part] * seqs), 2 * inner, expert_out.shape[1], model
    )
    return (
        mixed_out[None],
        grad_tokens[None],
        grad_gain_a[0],
        grad_attend_in,
        grad_att_out,
        grad_gain_m[0],
        grad_router.T,
        table,
        grad_mix.T,
        grad_vector.T,
        grad_in,
        grad_out,
    )


def solution(mesh):
    fsdp = mesh.shape["fsdp"]
    finer = Mesh(
        mesh.devices.reshape(mesh.shape["seq"], fsdp // (2 * SIDE), SIDE, 2), ("seq", *FSDP)
    )
    placed = (
        P(FSDP, "seq", None),
        P(FSDP, "seq", None),
        P(FSDP),
        P(FSDP, "seq", None),
        P(FSDP, "seq", None),
        P(FSDP),
        P(FSDP, None),
        P(FSDP, None),
        P(FSDP),
        P(FSDP, None),
        P(),
        P(FSDP, None),
        P(FSDP, None),
        P(None, FSDP, None),
        P(None, FSDP, None),
    )
    return jax.shard_map(
        shards,
        mesh=finer,
        in_specs=placed,
        out_specs=(
            P(FSDP, "seq", None),
            P(FSDP, "seq", None),
            P(FSDP),
            P(FSDP, None),
            P(FSDP, None),
            P(FSDP),
            P(FSDP, None),
            P(),
            P(FSDP, None),
            P(FSDP, None),
            P(None, FSDP, None),
            P(None, FSDP, None),
        ),
        check_vma=False,
    )
```

```python
import functools
import math

import jax
import jax.numpy as jnp
from jax import lax
from jax.experimental import pallas as pl
from jax.experimental.pallas import tpu as pltpu
from jax.sharding import Mesh
from jax.sharding import PartitionSpec as P

HEADS = 12
HEAD_DIM = 64
HALF = HEAD_DIM // 2
NC = 2
EF = 4
NE = 8
CAP = 192
LANES = 128
SEQS = 4
SIDE = 4
YZ = ("fy", "fz")
FSDP = ("fy", "fz", "core")
ANY = pl.BlockSpec(memory_space=pl.ANY)
EPS = 1e-06
SCALE = HEAD_DIM ** (-0.5)
LOWEST = -1e30
F32 = jnp.float32
BF16 = jnp.bfloat16
VMEM = pl.BlockSpec(memory_space=pltpu.VMEM)
SMEM = pl.BlockSpec(memory_space=pltpu.SMEM)


def mm(a, b, ca=1, cb=0):
    return lax.dot_general(a, b, (((ca,), (cb,)), ((), ())), preferred_element_type=F32)


def params(mib, grid=None):
    if grid is None:
        return pltpu.CompilerParams(vmem_limit_bytes=mib << 20)
    return pltpu.CompilerParams(
        vmem_limit_bytes=mib << 20, dimension_semantics=("arbitrary",) * grid
    )


def sds(shape, dtype):
    return jax.ShapeDtypeStruct(shape, dtype)


def took(us):
    return pl.CostEstimate(flops=int(us * 1.1e9), bytes_accessed=1 << 16, transcendentals=0)


def far(x):
    return pltpu.with_memory_space_constraint(x, pltpu.HBM)


def hbm(shape, dtype):
    return pltpu.HBM(shape, dtype)


def whole(x):
    return pl.BlockSpec(x.shape, lambda i: (0,) * len(x.shape))


def come(*arrays):
    return [(x, whole(x)) for x in arrays]


def one_step(body, us, meta, inputs, results, scratch=(), before=(), mib=14, near=0):
    inputs = [x if isinstance(x, tuple) else (far(x), whole(x)) for x in inputs]
    shapes = [(sds if k < near else hbm)(*r) for k, r in enumerate(results)]
    return pl.pallas_call(
        body,
        grid=(1,),
        in_specs=[SMEM] + [spec for _, spec in inputs] + [ANY] * len(before),
        out_specs=[VMEM if k < near else whole(r) for k, r in enumerate(shapes)],
        out_shape=shapes,
        scratch_shapes=list(scratch),
        compiler_params=params(mib, 1),
        cost_estimate=took(us),
        name=getattr(body, "func", body).__name__.removesuffix("_kernel"),
    )(meta, *[x for x, _ in inputs], *map(far, before))


def shift(x, by):
    count = lax.axis_size("seq")
    return lax.ppermute(x, "seq", [(i, (i + by) % count) for i in range(count)])


def trade(x, by, axis="seq"):
    count = lax.axis_size(axis)
    return lax.ppermute(x, axis, [(i, i ^ by) for i in range(count)]) if by else x


def trades(pieces, axis="seq"):
    return [trade(piece, k, axis) for k, piece in enumerate(pieces)]


def around(meta, by):
    return lax.bitwise_xor(meta[1], by)


def swap(x, axis):
    return lax.all_to_all(x, axis, split_axis=0, concat_axis=0, tiled=True)


def two_parts(x):
    high = x.astype(BF16)
    return high, (x - high.astype(F32)).astype(BF16)


def lane_of(shape):
    return lax.broadcasted_iota(jnp.int32, shape, 1)


def pick(values, lanes, lane):
    return jnp.sum(jnp.where(lanes == lane, values, 0.0), axis=1, keepdims=True)


def tiles_moved(x, rows, columns):
    tiles = [
        x[r : r + 8, c : c + LANES]
        for r in range(0, x.shape[0], 8)
        for c in range(0, x.shape[1], LANES)
    ]
    count = columns // LANES
    lines = [jnp.concatenate(tiles[k : k + count], axis=1) for k in range(0, len(tiles), count)]
    return jnp.concatenate(lines, axis=0)


def pack_kernel(
    meta,
    attend_in,
    gain_a,
    attend_out,
    router,
    const_mix,
    const_vector,
    gain_m,
    w_in,
    w_out,
    first,
    second,
    back,
    in_mine,
    out_mine,
    sems,
):
    shard, model = attend_out.shape
    group = model // SEQS
    me = meta[1]
    in_copy = pltpu.make_async_copy(w_in.at[me], in_mine, sems.at[0])
    out_copy = pltpu.make_async_copy(w_out.at[me], out_mine, sems.at[1])
    in_copy.start()
    out_copy.start()
    used = NE + 3 * NC + 2
    rows = [router[...], const_mix[...], const_vector[...], gain_m[...], gain_a[...]]
    rows = jnp.concatenate([*rows, jnp.zeros((LANES - used, shard), F32)], axis=0)
    rows = jnp.concatenate([rows, jnp.zeros((LANES, LANES - shard), F32)], axis=1)
    small = jnp.transpose(rows)[:shard]
    lanes = lane_of(small.shape)

    pieces, own = [], []
    for k in range(3):
        parts = [
            attend_in[:, k * model + g * group : k * model + (g + 1) * group] for g in range(SEQS)
        ]
        mine = parts[0]
        for g in range(1, SEQS):
            mine = jnp.where(me == g, parts[g], mine)
        pieces.append(parts)
        own.append(mine)
    gain = pltpu.roll(small, LANES - (used - 1), 1)[:, :64]
    gain = jnp.where(lane_of(gain.shape) == 0, gain, 0.0)
    row = jnp.concatenate([*own, gain], axis=1).astype(BF16)
    first[...] = jnp.broadcast_to(row[None], first.shape)
    back[...] = jnp.concatenate(
        [pieces[k][g] for g in range(SEQS) for k in range(3)], axis=1
    ).astype(BF16)

    small = jnp.where(lanes < used - 1, small, 0.0)
    second[:, :model] = attend_out[...].astype(BF16)
    second[:, model : model + 2 * LANES] = jnp.concatenate(
        [small, jnp.zeros_like(small)], axis=1
    ).astype(BF16)
    at = model + 2 * LANES
    wide = in_mine.shape[1]
    in_copy.wait()
    second[:, at : at + wide] = in_mine[...].astype(BF16)
    out_copy.wait()
    at += wide
    second[:, at:] = tiles_moved(out_mine[...], shard, second.shape[1] - at).astype(BF16)


def pack(meta, attend_in, gain_a, attend_out, router, const_mix, const_vector, gain_m, w_in, w_out, count):
    shard, model = attend_out.shape
    wide = model + 2 * LANES + w_in.shape[2] + w_out.shape[1] * model // shard
    plain = (attend_in, gain_a, attend_out, router, const_mix, const_vector, gain_m)
    results = [
        sds((count, shard, 3 * model // SEQS + 64), BF16),
        sds((shard, wide), BF16),
        sds(attend_in.shape, BF16),
    ]
    return pl.pallas_call(
        pack_kernel,
        grid=(1,),
        in_specs=[SMEM] + [whole(x) for x in plain] + [ANY] * 2,
        out_specs=[whole(x) for x in results],
        out_shape=results,
        scratch_shapes=[
            pltpu.VMEM(w_in.shape[1:], F32),
            pltpu.VMEM(w_out.shape[1:], F32),
            pltpu.SemaphoreType.DMA((2,)),
        ],
        compiler_params=params(14, 1),
        cost_estimate=took(2),
        name="pack",
    )(meta, *map(far, (*plain, w_in, w_out)))


def plan_kernel(meta, routes, prior, table, cotangent, slots, grad, logits, counts, *sent):
    rows = routes.shape[1]
    width = cotangent.shape[1]
    ids = lax.broadcasted_iota(jnp.int32, (NE, rows), 0)
    hits = (ids == routes[0:1]) | (ids == routes[1:2])
    before = lax.broadcasted_iota(jnp.int32, (rows, rows), 0)
    before = before < lax.broadcasted_iota(jnp.int32, (rows, rows), 1)
    ranks = mm(jnp.where(hits, 1.0, 0.0).astype(BF16), jnp.where(before, 1.0, 0.0).astype(BF16))
    ranks = jnp.where(hits, ranks.astype(jnp.int32), -1)
    lines = lax.broadcasted_iota(jnp.int32, (CAP, rows), 0)
    for e in range(EF):
        slots[e] = jnp.where(lines == ranks[e : e + 1], 1.0, 0.0).astype(BF16)
    spots = lax.broadcasted_iota(jnp.int32, (rows, width), 0) + meta[1] * rows
    live = jnp.where(spots < meta[0], cotangent[...].astype(F32), 0.0).astype(BF16)
    grad[...] = live
    for s in range(SEQS):
        sent[s][...] = mm(slots[around(meta, s)], live).astype(BF16)
    count = (ids == prior[0:1]).astype(F32) + (ids == prior[1:2]).astype(F32)
    named = routes[...].astype(F32)
    flat = [count, named, jnp.zeros((LANES - NE - 2, rows), F32)]
    flat = jnp.transpose(jnp.concatenate(flat, axis=0))
    lanes = lane_of(flat.shape)
    count = jnp.where(lanes < NE, flat, 0.0).astype(BF16)
    counts[...] = count
    full = jnp.concatenate([table[...], jnp.zeros((NE, LANES - NE), F32)], axis=1)
    full = jnp.concatenate([full, jnp.zeros((LANES - NE, LANES), F32)], axis=0)
    total = jnp.zeros(flat.shape, F32)
    for _ in range(3):
        part = full.astype(BF16)
        full = full - part.astype(F32)
        total += mm(count, part)
    named = pltpu.roll(flat, NE, 1)
    logits[...] = jnp.where((lanes >= 2 * NE) & (lanes < 2 * NE + 2), named, total)


def plan(meta, routes, prior, table, cotangent):
    rows, model = cotangent.shape
    results = [
        ((EF, CAP, rows), BF16),
        ((rows, model), BF16),
        ((rows, LANES), F32),
        ((rows, LANES), BF16),
    ] + [((CAP, model), BF16)] * SEQS
    return one_step(plan_kernel, 1, meta, [routes, prior, table, cotangent], results, mib=24)


def project_kernel(meta, *refs):
    sources, (weight, gain, cosine, sine, qkv, normed) = refs[:5], refs[5:]
    width = qkv.shape[1]
    part = width // 3
    for to, which in ((0, (0,)), (3, (1,)), (1, (2,)), (2, (3, 4))):
        place = lax.rem(meta[1] + to, SEQS)
        done = 0
        for source in [sources[k] for k in which]:
            at = slice(done, done + source.shape[0])
            done = at.stop
            v = source[...].astype(F32)
            n = v * lax.rsqrt(jnp.mean(v * v, axis=-1, keepdims=True) + EPS) * gain[...]
            normed[place, at] = n.astype(BF16)
        flat = jnp.transpose(mm(normed[place], weight[:, :width]))
        c, s = cosine[place], sine[place]
        for which in range(2):
            factor = SCALE if which == 0 else 1.0
            for at in range(which * part, (which + 1) * part, HEAD_DIM):
                a, b = flat[at : at + HALF], flat[at + HALF : at + HEAD_DIM]
                qkv[place, at : at + HALF] = ((a * c - b * s) * factor).astype(BF16)
                qkv[place, at + HALF : at + HEAD_DIM] = ((b * c + a * s) * factor).astype(BF16)
        qkv[place, 2 * part :] = flat[2 * part :].astype(BF16)


def project(meta, sources, weight, gain, cosine, sine, width):
    rows, model = sources[0].shape
    results = [((SEQS, width, rows), BF16), ((SEQS, rows, model), BF16)]
    inputs = [*come(*sources, weight, gain), cosine, sine]
    return one_step(project_kernel, 100, meta, inputs, results, mib=20, near=1)


def mask_diagonal(scores, start, length):
    keys = lax.broadcasted_iota(jnp.int32, scores.shape, 0)
    queries = lax.broadcasted_iota(jnp.int32, scores.shape, 1)
    return jnp.where((keys <= queries) & (keys + start < length), scores, LOWEST)


def attend_kernel(meta, qkv, out, lse, kept, top, total, acc, sem):
    copy = pltpu.make_async_copy(qkv, kept, sem)
    copy.start()
    rows = qkv.shape[2]
    part = qkv.shape[1] // 3
    heads = part // HEAD_DIM
    length = meta[0]
    spans = [
        [slice(k * part + h * HEAD_DIM, k * part + (h + 1) * HEAD_DIM) for k in range(3)]
        for h in range(heads)
    ]
    for block in range(SEQS):
        for h, (at, k_at, v_at) in enumerate(spans):
            scores = mm(qkv[block, k_at], qkv[block, at], 0, 0)
            scores = mask_diagonal(scores, block * rows, length)
            peak = jnp.max(scores, axis=0, keepdims=True)
            e = jnp.exp(scores - peak)
            top[h : h + 1] = peak
            total[h : h + 1] = jnp.sum(e, axis=0, keepdims=True)
            acc[at] = mm(qkv[block, v_at], e.astype(BF16))

        def step(j, carry, block=block):
            for h, (at, k_at, v_at) in enumerate(spans):
                scores = mm(qkv[j, k_at], qkv[block, at], 0, 0)
                last = top[h : h + 1]
                peak = jnp.maximum(last, jnp.max(scores, axis=0, keepdims=True))
                e = jnp.exp(scores - peak)
                fade = jnp.exp(last - peak)
                top[h : h + 1] = peak
                total[h : h + 1] = total[h : h + 1] * fade + jnp.sum(e, axis=0, keepdims=True)
                acc[at] = acc[at] * fade + mm(qkv[j, v_at], e.astype(BF16))
            return carry

        lax.fori_loop(0, block, step, 0)
        for h, (at, _, _) in enumerate(spans):
            out[block, at] = (acc[at] / total[h : h + 1]).astype(BF16)
            lse[block, h : h + 1] = top[h : h + 1] + jnp.log(total[h : h + 1])
    copy.wait()


def attend(meta, qkv):
    _, width, rows = qkv.shape
    part = width // 3
    results = [sds((SEQS, part, rows), BF16), sds((SEQS, 8, rows), F32)]
    return pl.pallas_call(
        attend_kernel,
        grid=(1,),
        in_specs=[SMEM, VMEM],
        out_specs=[whole(x) for x in results] + [ANY],
        out_shape=[hbm(x.shape, x.dtype) for x in (*results, qkv)],
        scratch_shapes=[
            pltpu.VMEM((8, rows), F32),
            pltpu.VMEM((8, rows), F32),
            pltpu.VMEM((part, rows), F32),
            pltpu.SemaphoreType.DMA,
        ],
        compiler_params=params(20, 1),
        cost_estimate=took(0.1),
        name="attend",
    )(meta, qkv)


def attend_back_kernel(meta, qkv, *refs):
    dout, out, lse, cosine, sine, dlogits, grad_vec, dgain, prior_hits = refs[:9]
    later = refs[9:13]
    dproj = refs[-11 - SEQS : -11]
    kept, gone, dq, dk, dv, dots, *ready, sems = refs[-11:]
    blocks, width, rows = qkv.shape
    part = width // 3
    heads = part // HEAD_DIM
    length = meta[0]

    copies = [
        pltpu.make_async_copy(a, b, sems.at[k]) for k, (a, b) in enumerate(zip(later, ready))
    ]
    for copy in copies:
        copy.start()
    normed_held, att, dlow, moe = ready

    def pair(q, k, diagonal):
        for h in range(heads):
            at = slice(h * HEAD_DIM, (h + 1) * HEAD_DIM)
            k_at = slice(part + h * HEAD_DIM, part + (h + 1) * HEAD_DIM)
            v_at = slice(2 * part + h * HEAD_DIM, 2 * part + (h + 1) * HEAD_DIM)
            qh, kh, vh, doh = qkv[q, at], qkv[k, k_at], qkv[k, v_at], dout[q, at]
            scores = mm(kh, qh, 0, 0)
            if diagonal:
                scores = mask_diagonal(scores, k * rows, length)
            probs = jnp.exp(scores - lse[q, h : h + 1])
            dprobs = mm(vh, doh, 0, 0)
            low = probs.astype(BF16)
            dscores = (probs * (dprobs - dots[q, h : h + 1])).astype(BF16)
            if diagonal:
                dv[k, at] = mm(doh, low, 1, 1)
                dk[k, at] = mm(qh, dscores, 1, 1)
                dq[q, at] = mm(kh, dscores)
            else:
                dv[k, at] += mm(doh, low, 1, 1)
                dk[k, at] += mm(qh, dscores, 1, 1)
                dq[q, at] += mm(kh, dscores)

    for b in range(SEQS):
        for h in range(heads):
            at = slice(h * HEAD_DIM, (h + 1) * HEAD_DIM)
            both = dout[b, at].astype(F32) * out[b, at].astype(F32)
            dots[b, h : h + 1] = jnp.sum(both, axis=0, keepdims=True)

    def diagonal(b, carry):
        pair(b, b, True)
        return carry

    def below(q, carry):
        def one(k, inner):
            pair(q, k, False)
            return inner

        return lax.fori_loop(0, q, one, carry)

    lax.fori_loop(0, blocks, diagonal, 0)
    lax.fori_loop(1, blocks, below, 0)
    for to in range(SEQS):
        b = around(meta, to)
        c, s = cosine[b], sine[b]
        for which, held in ((0, dq), (1, dk)):
            factor = SCALE if which == 0 else 1.0
            for h in range(heads):
                at = h * HEAD_DIM
                rounded = (held[b, at : at + HEAD_DIM] * factor).astype(BF16).astype(F32)
                x, y = rounded[:HALF], rounded[HALF:]
                at += which * part
                dproj[to][at : at + HALF] = (x * c + y * s).astype(BF16)
                dproj[to][at + HALF : at + HEAD_DIM] = (y * c - x * s).astype(BF16)
        dproj[to][2 * part :] = dv[b].astype(BF16)

    for copy in copies:
        copy.wait()
    pairs, shard, wide = kept.shape
    model = att.shape[0]
    even = meta[2] == 0

    def halves(x, at):
        x = x.reshape(pairs, 2 * shard, x.shape[1])
        first, second = x[:, :shard], x[:, shard:]
        kept[:, :, at : at + x.shape[2]] = jnp.where(even, first, second).astype(BF16)
        gone[:, :, at : at + x.shape[2]] = jnp.where(even, second, first).astype(BF16)

    halves(mm(att[...], dlow[...]), 0)
    high, rest = two_parts(dlogits[...])
    result = mm(moe[...], high, 0, 0) + mm(moe[...], rest, 0, 0)
    result += pltpu.roll(grad_vec[...], NE + 2 * NC, 1)
    lanes = lane_of(result.shape)
    column = jnp.transpose(jnp.broadcast_to(dgain[...], (LANES, model)))
    result += jnp.where(lanes == NE + 3 * NC, column, 0.0)
    table = mm(prior_hits[...], high, 0, 0) + mm(prior_hits[...], rest, 0, 0)
    table = jnp.where(lane_of((NE, LANES)) < NE, table[:NE], 0.0)
    high, rest = two_parts(table)
    block = pltpu.roll(high.astype(F32), 2 * NE, 1) + pltpu.roll(rest.astype(F32), 3 * NE, 1)
    block = jnp.concatenate([block, jnp.zeros((shard - NE, LANES), F32)], axis=0)
    result = result.reshape(2 * pairs, shard, LANES) + block[None]
    halves(result.reshape(model, LANES), model)
    total = mm(dproj[0][...], normed_held[around(meta, 0)])
    for to in range(1, SEQS):
        total += mm(dproj[to][...], normed_held[around(meta, to)])
    total = [jnp.transpose(total), jnp.zeros((model, wide - model - LANES - width), F32)]
    halves(jnp.concatenate(total, axis=1), model + LANES)


def attend_back(meta, before, qkv, dout, out, lse, cosine, sine, few, later, count):
    blocks, width, rows = qkv.shape
    part = width // 3
    model = later[1].shape[0]
    scratch = [pltpu.VMEM((blocks, part, rows), F32)] * 3 + [pltpu.VMEM((blocks, 8, rows), F32)]
    scratch += [pltpu.VMEM(x.shape, BF16) for x in later] + [pltpu.SemaphoreType.DMA((4,))]
    inputs = [qkv, *come(dout), out, lse, cosine, sine, *few, *((far(x), ANY) for x in later)]
    wide = -(-(model + LANES + width) // LANES) * LANES
    results = [((width, rows), BF16)] * SEQS
    results += [((count // 2, model // count, wide), BF16)] * 2
    return one_step(attend_back_kernel, 12, meta, inputs, results, scratch, before, 48)


def route_kernel(meta, att, out_w, small_w, tok, prior, slots, *refs):
    sent = refs[-4 - SEQS : -4]
    resid, moe, stats, vectors = refs[-4:]
    res = tok[...].astype(F32) + mm(att[...], out_w[...], 0, 0)
    flipped = jnp.transpose(small_w[...].astype(F32))
    vectors[...] = flipped[NE + 2 * NC : NE + 2 * NC + 8]
    gain = flipped[NE + 3 * NC : NE + 3 * NC + 1]
    resid[...] = res
    normed = res * lax.rsqrt(jnp.mean(res * res, axis=-1, keepdims=True) + EPS) * gain
    low = normed.astype(BF16)
    moe[...] = low
    small = mm(low, small_w[...])
    small = jnp.where(lane_of(small.shape) < NE + 2 * NC, small, 0.0)
    lanes = lane_of(small.shape)
    known = prior[...]
    logits = small + jnp.where(lanes < NE, known, 0.0)
    named = lanes.astype(F32)
    hit0 = named == known[:, 2 * NE : 2 * NE + 1]
    hit1 = named == known[:, 2 * NE + 1 : 2 * NE + 2]
    chosen0 = jnp.sum(jnp.where(hit0, logits, 0.0), axis=1, keepdims=True)
    chosen1 = jnp.sum(jnp.where(hit1, logits, 0.0), axis=1, keepdims=True)
    gate0 = 1.0 / (1.0 + jnp.exp(chosen1 - chosen0))
    gate1 = 1.0 / (1.0 + jnp.exp(chosen0 - chosen1))
    share = jnp.where(hit0, gate0, 0.0) + jnp.where(hit1, gate1, 0.0)
    partner = jnp.where(lanes % 2 == 0, pltpu.roll(small, LANES - 1, 1), pltpu.roll(small, 1, 1))
    mix = 1.0 / (1.0 + jnp.exp(partner - small))
    mixing = (lanes >= NE) & (lanes < NE + 2 * NC)
    stats[...] = share + jnp.where(mixing, mix, 0.0)
    high, rest = two_parts(share)
    parts = (high.astype(F32) + pltpu.roll(rest.astype(F32), NE, 1)).astype(BF16)
    model = low.shape[1]
    for s in range(SEQS):
        chosen = slots[around(meta, s)]
        sent[s][:, :model] = mm(chosen, low).astype(BF16)
        sent[s][:, model:] = mm(chosen, parts).astype(BF16)


def weight_blocks(weights):
    model = weights.shape[0]
    return [
        (far(weights), pl.BlockSpec((model, model), lambda i: (0, 0))),
        (far(weights), pl.BlockSpec((model, LANES), lambda i: (0, model // LANES))),
    ]


def route(meta, att, weights, tok, prior, slots, *before):
    rows, model = tok.shape
    results = [((CAP, model + LANES), BF16)] * SEQS + [
        ((rows, model), F32),
        ((rows, model), BF16),
        ((rows, LANES), F32),
        ((8, model), F32),
    ]
    inputs = [*come(att), *weight_blocks(weights), tok, prior, slots]
    return one_step(route_kernel, 100, meta, inputs, results, (), before, 24)


def local_part_kernel(meta, resid, stats, grad, vectors, partial, small, grad_vec):
    gain = vectors[NC : NC + 1]
    res, g = resid[...], grad[...].astype(F32)
    normed = res * lax.rsqrt(jnp.mean(res * res, axis=-1, keepdims=True) + EPS) * gain
    held = stats[...]
    lanes = lane_of(held.shape)
    copy_dot = jnp.sum(g * normed, axis=1, keepdims=True)
    factor = pick(held, lanes, EF + 1)
    result = jnp.where(lanes == EF + 1, factor * copy_dot, 0.0)
    ways = jnp.zeros_like(held)
    added = jnp.zeros_like(res)
    for j in range(NC):
        row = vectors[j : j + 1]
        weight = pick(held, lanes, EF + 2 + j)
        first = pick(held, lanes, NE + 2 * j)
        second = pick(held, lanes, NE + 2 * j + 1)
        vec_dot = jnp.sum(g * row, axis=1, keepdims=True)
        mean = first * copy_dot + second * vec_dot
        result += jnp.where(lanes == EF + 2 + j, weight * mean, 0.0)
        result += jnp.where(lanes == NE + 2 * j, weight * first * (copy_dot - mean), 0.0)
        result += jnp.where(lanes == NE + 2 * j + 1, weight * second * (vec_dot - mean), 0.0)
        ways += jnp.where(lanes == j, weight * second, 0.0)
        added += (weight * second) * row
        factor += weight * first
    small[...] = result + jnp.where(lanes == NE + 2 * NC, factor, 0.0)
    partial[...] = res + factor * normed + added
    high, rest = two_parts(ways)
    grad_vec[...] = mm(grad[...], high, 0, 0) + mm(grad[...], rest, 0, 0)


def local_part(meta, resid, stats, grad, vectors):
    rows, model = resid.shape
    results = [((rows, model), F32), ((rows, LANES), F32), ((model, LANES), F32)]
    return one_step(local_part_kernel, 0.1, meta, [resid, stats, grad, vectors], results, mib=16)


def expert_kernel(meta, *refs):
    sent, grads = refs[:SEQS], refs[SEQS : 2 * SEQS]
    gate_w, up_w, out_w = refs[2 * SEQS + 1 : 2 * SEQS + 4]
    back, branch = refs[2 * SEQS + 4 : 3 * SEQS + 4], refs[3 * SEQS + 4]
    in_kept, in_sent, out_kept, out_sent = refs[3 * SEQS + 5 : 3 * SEQS + 9]
    rows, flipped, held, scaled, gate, hidden, dgate, dup, acc, mixed_acc, dots = refs[-11:]
    step = pl.program_id(0)
    count, model = rows.shape
    block = gate_w.shape[1]
    me = meta[1]
    even = meta[2] == 0

    def split(x, kept, gone):
        pairs, shard, wide = kept.shape
        x = x.reshape(pairs, 2 * shard, wide)
        first, second = x[:, :shard], x[:, shard:]
        kept[...] = jnp.where(even, first, second).astype(BF16)
        gone[...] = jnp.where(even, second, first).astype(BF16)

    @pl.when(step == 0)
    def _():
        for s in range(SEQS):
            at = slice(s * CAP, (s + 1) * CAP)
            rows[at] = sent[s][:, :model]
            flipped[:, at] = jnp.transpose(sent[s][:, :model])
            held[at] = grads[s][...]
            parts = sent[s][:, model:].astype(F32)
            lanes = lane_of(parts.shape)
            own = (lanes == me) | (lanes == me + NE)
            share = jnp.sum(jnp.where(own, parts, 0.0), axis=1, keepdims=True)
            gate[at] = jnp.broadcast_to(share, (CAP, LANES))
            scaled[at] = (grads[s][...].astype(F32) * share).astype(BF16)
        acc[...] = jnp.zeros_like(acc)
        mixed_acc[...] = jnp.zeros_like(mixed_acc)
        dots[...] = jnp.zeros_like(dots)

    for at in (slice(0, count // 2), slice(count // 2, count)):
        g = mm(rows[at], gate_w[...])
        u = mm(rows[at], up_w[...])
        v = mm(held[at], out_w[...], 1, 1)
        sig = 1.0 / (1.0 + jnp.exp(-g))
        silu = g * sig
        low = (silu * u).astype(BF16)
        hidden[at] = low
        both = v * low.astype(F32)
        folded = both[:, :LANES]
        for c in range(LANES, block, LANES):
            folded = folded + both[:, c : c + LANES]
        dots[at] += folded
        d = v * gate[at, 0:1]
        du = (d * silu).astype(BF16)
        dg = (d * u * (sig * (1.0 + g * (1.0 - sig)))).astype(BF16)
        dgate[at] = dg
        dup[at] = du
        acc[at] += mm(dg, gate_w[...], 1, 1) + mm(du, up_w[...], 1, 1)
        mixed_acc[at] += mm(low, out_w[...])

    split(mm(flipped[...], dgate[...]), in_kept.at[0, 0], in_sent.at[0, 0])
    split(mm(flipped[...], dup[...]), in_kept.at[0, 1], in_sent.at[0, 1])
    split(mm(hidden[...], scaled[...], 0, 0), out_kept, out_sent)

    @pl.when(step == pl.num_programs(0) - 1)
    def _():
        for s in range(SEQS):
            at = slice(s * CAP, (s + 1) * CAP)
            back[s][:, :model] = acc[at].astype(BF16)
            value = jnp.sum(dots[at], axis=1, keepdims=True) * gate[at]
            lanes = lane_of(value.shape)
            high, rest = two_parts(value)
            back[s][:, model:] = (
                jnp.where(lanes == me, high.astype(F32), 0.0)
                + jnp.where(lanes == me + NE, rest.astype(F32), 0.0)
            ).astype(BF16)
            branch[around(meta, s)] = (mixed_acc[at] * gate[at, 0:1]).astype(BF16)


def expert(meta, sent, grads, before, weights, w_out, block, fsdp):
    count, model = SEQS * CAP, grads[0].shape[1]
    inner = w_out.shape[0]
    steps = inner // block
    skip = (model + 2 * LANES) // block
    pairs, in_rows, out_rows = fsdp // 2, model // fsdp, inner // fsdp
    per = block // (2 * out_rows)
    results = [sds(sent[0].shape, BF16)] * SEQS + [sds((SEQS, CAP, model), BF16)]
    in_spec = pl.BlockSpec((1, 2, pairs, in_rows, block), lambda i: (i, 0, 0, 0, 0))
    out_spec = pl.BlockSpec((per, out_rows, model), lambda i: (i, 0, 0))
    return pl.pallas_call(
        expert_kernel,
        grid=(steps,),
        in_specs=[SMEM]
        + [whole(x) for x in (*sent, *grads)]
        + [
            ANY,
            pl.BlockSpec((model, block), lambda i: (0, i + skip)),
            pl.BlockSpec((model, block), lambda i: (0, i + skip + steps)),
            pl.BlockSpec((block, model), lambda i: (i, 0)),
        ],
        out_specs=[whole(x) for x in results] + [in_spec, in_spec, out_spec, out_spec],
        out_shape=[hbm(r.shape, r.dtype) for r in results]
        + [hbm((steps, 2, pairs, in_rows, block), BF16)] * 2
        + [hbm((pairs, out_rows, model), BF16)] * 2,
        scratch_shapes=[
            pltpu.VMEM((count, model), BF16),
            pltpu.VMEM((model, count), BF16),
            pltpu.VMEM((count, model), BF16),
            pltpu.VMEM((count, model), BF16),
            pltpu.VMEM((count, LANES), F32),
            pltpu.VMEM((count, block), BF16),
            pltpu.VMEM((count, block), BF16),
            pltpu.VMEM((count, block), BF16),
            pltpu.VMEM((count, model), F32),
            pltpu.VMEM((count, model), F32),
            pltpu.VMEM((count, LANES), F32),
        ],
        compiler_params=params(52, 1),
        cost_estimate=took(10),
        name="expert",
    )(meta, *sent, *grads, *map(far, (before, weights, weights, w_out)))


def split_again(small):
    lanes = lane_of(small.shape)
    table = small + pltpu.roll(small, LANES - NE, 1)
    high = table.astype(BF16).astype(F32)
    rest = pltpu.roll(table - high, NE, 1)
    at = lanes // NE
    return jnp.where(at == 2, high, jnp.where(at == 3, rest, small))


def add_cores_kernel(in_a, in_b, out_a, out_b, *refs):
    blocks, _, _, shard, block = in_a.shape
    wide = 2 * blocks * block
    for k in range(in_a.shape[2]):
        both = refs[-1].at[k]
        for j in range(2 * blocks):
            at = (j % blocks, j // blocks, k)
            total = in_a[at].astype(F32) + in_b[at].astype(F32)
            both[:, j * block : (j + 1) * block] = total.astype(BF16)
        more = out_a[k].astype(F32) + out_b[k].astype(F32)
        both[:, wide:] = tiles_moved(more, shard, both.shape[1] - wide).astype(BF16)


def add_cores(parts, *before):
    blocks, _, pairs, shard, block = parts[0].shape
    wide = 2 * blocks * block
    more = parts[2].shape[1] * parts[2].shape[2] // shard

    def some(shape):
        return pl.BlockSpec((SIDE, *shape), lambda i: (i, 0, 0))

    return pl.pallas_call(
        add_cores_kernel,
        grid=(pairs // SIDE,),
        in_specs=[pl.BlockSpec((blocks, 2, SIDE, shard, block), lambda i: (0, 0, i, 0, 0))] * 2
        + [some(x.shape[1:]) for x in parts[2:]]
        + [ANY] * len(before),
        out_specs=some((shard, wide + more)),
        out_shape=hbm((pairs, shard, wide + more), BF16),
        compiler_params=params(24, 1),
        cost_estimate=took(0.1),
        name="add_cores",
    )(*[x if k % 2 else far(x) for k, x in enumerate(parts)], *map(far, before))


def add_dense_kernel(meta, kept, other, out):
    pairs, shard, wide = kept.shape
    model = 2 * pairs * shard
    for k in range(pairs):
        total = kept[k].astype(F32) + other[k].astype(F32)
        out[k] = total.astype(BF16)
        out[k, :, model : model + LANES] = split_again(total[:, model : model + LANES]).astype(BF16)


def add_dense(meta, kept, other):
    inputs = [kept, *come(other)]
    return one_step(add_dense_kernel, 0.1, meta, inputs, [(kept.shape, BF16)], mib=24)[0]


def add_pieces_kernel(meta, pieces, *refs):
    total = pieces[0].astype(F32)
    for k in range(1, pieces.shape[0]):
        total += pieces[k].astype(F32)
    model = pieces.shape[0] * pieces.shape[1] * 2
    small = split_again(total[:, model : model + LANES])
    parts = [total[:, :model], small, total[:, model + LANES :]]
    total = jnp.concatenate(parts, axis=1).astype(BF16)
    refs[-1][...] = total


def add_pieces(meta, pieces, *before):
    results = [(pieces.shape[1:], BF16)]
    return one_step(add_pieces_kernel, 0.1, meta, come(pieces), results, (), before, 24)[0]


def mixed_kernel(meta, partial, slots, *refs):
    result = partial[...]
    for e in range(EF):
        result += mm(slots[e], refs[0][e], 0, 0)
    refs[-1][...] = result.astype(BF16)


def mixed(meta, partial, slots, branch, *before):
    results = [(partial.shape, BF16)]
    (out,) = one_step(mixed_kernel, 0.1, meta, [partial, slots, *come(branch)], results, (), before)
    return out


def unroute_kernel(meta, *refs):
    back = refs[:SEQS]
    out_w, small_w, slots, resid, small, stats, grad, vectors = refs[SEQS : SEQS + 8]
    datt, dres, dlow, dlogits, dgain = refs[-5:]
    gain = vectors[NC : NC + 1]
    rows, model = resid.shape
    held, local = stats[...], small[...]
    lanes = lane_of(held.shape)
    dn = jnp.zeros((rows, model), F32)
    tail = jnp.zeros((rows, LANES), F32)
    for s in range(SEQS):
        chosen = slots[around(meta, s)]
        dn += mm(chosen, back[s][:, :model], 0, 0)
        tail += mm(chosen, back[s][:, model:], 0, 0)
    ffn = tail + pltpu.roll(tail, LANES - NE, 1)
    dots = jnp.where(lanes < EF, ffn, jnp.where(lanes < NE, local, 0.0))
    total = jnp.sum(dots, axis=1, keepdims=True)
    keep = (lanes >= NE) & (lanes < NE + 2 * NC)
    dsmall = jnp.where(lanes < NE, dots - held * total, jnp.where(keep, local, 0.0))
    high, rest = two_parts(dsmall)
    dn += mm(high, small_w[...], 1, 1) + mm(rest, small_w[...], 1, 1)
    g = grad[...].astype(F32)
    dn += pick(local, lanes, NE + 2 * NC) * g
    res = resid[...]
    factor = lax.rsqrt(jnp.mean(res * res, axis=-1, keepdims=True) + EPS)
    normal = res * factor
    dgain[...] = jnp.sum(dn * normal, axis=0, keepdims=True)
    dlogits[...] = dsmall
    scaled = dn * gain
    out = g + factor * (scaled - normal * jnp.mean(scaled * normal, axis=-1, keepdims=True))
    dres[...] = out
    low = out.astype(BF16)
    dlow[...] = low
    datt[...] = mm(out_w[...], low, 1, 1).astype(BF16)


def unroute(meta, before, back, weights, tokenwise):
    rows, model = tokenwise[1].shape
    inputs = [*come(*back), *weight_blocks(weights), *tokenwise]
    results = [
        ((model, rows), BF16),
        ((rows, model), F32),
        ((rows, model), BF16),
        ((rows, LANES), F32),
        ((1, model), F32),
    ]
    return one_step(unroute_kernel, 100, meta, inputs, results, (), before, 32)


def finish_kernel(meta, *refs):
    dproj, (weight, tok, gain, dres) = refs[:SEQS], refs[SEQS : SEQS + 4]
    out, flat = refs[-2:]
    width = dproj[0].shape[0]
    for s in range(SEQS):
        at = pl.multiple_of(around(meta, s) * width, 64)
        flat[pl.ds(at, width)] = dproj[s][...]
    dn = jnp.transpose(mm(weight[...], flat[...]))
    v = tok[...].astype(F32)
    factor = lax.rsqrt(jnp.mean(v * v, axis=-1, keepdims=True) + EPS)
    normal = v * factor
    scaled = dn * gain[...]
    dx = factor * (scaled - normal * jnp.mean(scaled * normal, axis=-1, keepdims=True))
    out[...] = (dres[...] + dx).astype(BF16)


def finish(meta, dproj, weight, tok, gain, dres, *before):
    width, rows = dproj[0].shape
    scratch = [pltpu.VMEM((SEQS * width, rows), BF16)]
    results = [(tok.shape, BF16)]
    inputs = [*come(*dproj), weight, tok, gain, dres]
    return one_step(finish_kernel, 10, meta, inputs, results, scratch, before, 24)[0]


def gather_kernel(meta, *refs):
    pieces = refs[:SEQS]
    grad_in, grad_out = refs[-2:]
    wide = grad_in.shape[2]
    for s in range(SEQS):
        place = around(meta, s)
        grad_in[place] = pieces[s][:, :wide].astype(F32)
        grad_out[place] = tiles_moved(pieces[s][:, wide:].astype(F32), *grad_out.shape[1:])


def gather(meta, pieces, wide, rows, model, *before):
    shard = pieces[0].shape[0]
    results = [((SEQS, shard, wide), F32), ((SEQS, rows, model), F32)]
    return one_step(gather_kernel, 0.1, meta, come(*pieces), results, (), before, 24)


def gather_dense_kernel(meta, *refs):
    pieces, attend_in, gain_a = refs[:SEQS], refs[SEQS], refs[SEQS + 1]
    att_in, grad_gain, att_out, router, const_mix, const_vector, gain, table, held = refs[-9:]
    shard, model = att_out.shape
    group = model // SEQS
    at = model + LANES
    for s in range(SEQS):
        held[around(meta, s)] = pieces[s][...].astype(F32)
    order = [(k, g) for k in range(3) for g in range(SEQS)]
    parts = [held[g][:, at + k * group : at + (k + 1) * group] for k, g in order]
    full = jnp.concatenate(parts, axis=1)
    att_in[...] = full
    low = attend_in[...].astype(BF16).astype(F32)
    column = jnp.sum(full * low, axis=1, keepdims=True)
    column = jnp.concatenate([column, jnp.zeros((LANES - shard, 1), F32)], axis=0)
    row = jnp.transpose(jnp.broadcast_to(column, (LANES, LANES)))[:1, :shard]
    grad_gain[...] = row / gain_a[...].astype(BF16).astype(F32)

    total = held[0][:, :at]
    for s in range(1, SEQS):
        total += held[s][:, :at]
    att_out[...] = total[:, :model]
    small = jnp.concatenate([total[:, model:], jnp.zeros((LANES - shard, LANES), F32)], axis=0)
    both = small + pltpu.roll(small, LANES - NE, 1)
    table[...] = pltpu.roll(both, LANES - 2 * NE, 1)[:NE, :NE]
    small = jnp.transpose(small)[:, :shard]
    at = NE + 2 * NC
    router[...] = small[:NE]
    const_mix[...] = small[NE:at]
    const_vector[...] = small[at : at + NC]
    gain[...] = small[at + NC : at + NC + 1]


def gather_dense(meta, pieces, attend_in, gain):
    shard, wide = pieces[0].shape
    model = attend_in.shape[1] // 3
    results = [attend_in.shape, (1, shard), (shard, model), (NE, shard), (2 * NC, shard)]
    results = [(r, F32) for r in (*results, (NC, shard), (1, shard), (NE, NE))]
    scratch = [pltpu.VMEM((SEQS, shard, wide), F32)]
    inputs = [*come(*pieces), attend_in, gain]
    return one_step(gather_dense_kernel, 0.1, meta, inputs, results, scratch, mib=16)


def shards(
    tokens,
    cotangent,
    lengths,
    routes,
    prior_routes,
    gain_attend,
    attend_in,
    attend_out,
    gain_mix,
    router,
    route_table,
    const_mix,
    const_vector,
    expert_in,
    expert_out,
):
    seqs = lax.axis_size("seq")
    fsdp = lax.axis_size(FSDP)
    here = lax.axis_index("seq")
    tok = tokens[0]
    rows, model = tok.shape
    shard = attend_in.shape[0]
    group = model // seqs
    width = 3 * group
    length = lengths[0]
    meta = jnp.stack([length, here, *(lax.axis_index(a) for a in ("core", *YZ))])
    meta = meta.astype(jnp.int32)

    first, second, back_mine = pack(
        meta,
        attend_in,
        gain_attend[None],
        attend_out,
        router.T,
        const_mix.T,
        const_vector.T,
        gain_mix[None],
        expert_in,
        expert_out,
        fsdp,
    )
    first_all = swap(first, FSDP).reshape(model, width + 64)
    half = rows // 2
    left, right = shift(tok, 1), shift(tok, -1)
    far0, far1 = shift(left[:half], 1), shift(right[half:], -1)
    weights = lax.all_gather(second, FSDP, axis=0, tiled=True)
    back_w = lax.all_gather(back_mine, FSDP, axis=0, tiled=True)
    inner = expert_out.shape[1] * fsdp
    wide = expert_out.shape[1] * model // shard
    w_out = weights[:, model + 2 * LANES + 2 * inner :]
    w_out = w_out.reshape(-1, shard // 8, 8, wide // LANES, LANES).transpose(0, 1, 3, 2, 4)
    w_out = w_out.reshape(-1, model // LANES, 8, LANES).transpose(0, 2, 1, 3).reshape(inner, model)
    gain_a = first_all[:, width].astype(F32)[None]

    slots, grad, prior, prior_hits, *grad_rows = plan(
        meta, routes[0].T, prior_routes[0].T, route_table, cotangent[0]
    )
    inverse = jnp.exp(
        jnp.arange(HALF, dtype=F32) * (-2.0 * math.log(10000.0) / HEAD_DIM)
    )
    angles = jnp.arange(seqs * rows, dtype=F32).reshape(seqs, 1, rows) * inverse[None, :, None]
    cosine, sine = jnp.cos(angles), jnp.sin(angles)

    left, right, *grad_rows = lax.optimization_barrier((left, right, *grad_rows))
    grad_rows = trades(grad_rows)

    qkv, normed = project(
        meta, [tok, left, right, far0, far1], first_all, gain_a, cosine, sine, width
    )
    held, lse, qkv = attend(meta, qkv)
    held, *grad_rows = lax.optimization_barrier((held, *grad_rows))
    att = swap(held, "seq").reshape(model, rows)
    *sent, resid, moe, stats, vectors = route(meta, att, weights, tok, prior, slots)
    sent = trades(sent)
    partial, small, grad_vec = local_part(meta, resid, stats, grad, vectors)

    *results, in_kept, in_sent, out_kept, out_sent = expert(
        meta, sent, grad_rows, small, weights, w_out, 512, fsdp
    )
    back, branch = trades(results[:seqs]), swap(results[seqs], "seq")
    in_come, out_come = trade(in_sent, 1, "core"), trade(out_sent, 1, "core")
    both = add_cores((in_kept, in_come, out_kept, out_come), back_w)
    part = both.reshape(-1, both.shape[2])
    part = lax.psum_scatter(part, YZ, scatter_dimension=0, tiled=True)
    tokenwise = (slots, resid, small, stats, grad, vectors)
    datt, dres, dlow, dlogits, dgain_m = unroute(meta, (both,), back, weights, tokenwise)
    dout = swap(datt.reshape(seqs, group, rows), "seq")
    mixed_out = mixed(meta, partial, slots, branch, dres)
    few = (dlogits, grad_vec, dgain_m, prior_hits)
    *dproj, kept, gone = attend_back(
        meta, (mixed_out,), qkv, dout, held, lse, cosine, sine, few, (normed, att, dlow, moe), fsdp
    )
    other = trade(gone, 1, "core")
    back_all = trades(dproj)
    dense = add_dense(meta, kept, other)
    dense = swap(dense, YZ)
    part, back_all[2] = lax.optimization_barrier((part, back_all[2]))
    pieces = trades([part] * seqs)
    grad_tokens = finish(meta, back_all, back_w, tok, gain_a, dres)
    dense = add_pieces(meta, dense, grad_tokens)
    dense, *pieces = lax.optimization_barrier((dense, *pieces))
    dense = trades([dense] * seqs)
    grad_attend_in, grad_gain_a, grad_att_out, *rest, table = gather_dense(
        meta, dense, attend_in, gain_attend[None]
    )
    grad_router, grad_mix, grad_vector, grad_gain_m = rest
    grad_in, grad_out = gather(
        meta, pieces, 2 * inner, expert_out.shape[1], model
    )
    return (
        mixed_out[None],
        grad_tokens[None],
        grad_gain_a[0],
        grad_attend_in,
        grad_att_out,
        grad_gain_m[0],
        grad_router.T,
        table,
        grad_mix.T,
        grad_vector.T,
        grad_in,
        grad_out,
    )


def solution(mesh):
    fsdp = mesh.shape["fsdp"]
    finer = Mesh(
        mesh.devices.reshape(mesh.shape["seq"], fsdp // (2 * SIDE), SIDE, 2), ("seq", *FSDP)
    )
    placed = (
        P(FSDP, "seq", None),
        P(FSDP, "seq", None),
        P(FSDP),
        P(FSDP, "seq", None),
        P(FSDP, "seq", None),
        P(FSDP),
        P(FSDP, None),
        P(FSDP, None),
        P(FSDP),
        P(FSDP, None),
        P(),
        P(FSDP, None),
        P(FSDP, None),
        P(None, FSDP, None),
        P(None, FSDP, None),
    )
    return jax.shard_map(
        shards,
        mesh=finer,
        in_specs=placed,
        out_specs=(
            P(FSDP, "seq", None),
            P(FSDP, "seq", None),
            P(FSDP),
            P(FSDP, None),
            P(FSDP, None),
            P(FSDP),
            P(FSDP, None),
            P(),
            P(FSDP, None),
            P(FSDP, None),
            P(None, FSDP, None),
            P(None, FSDP, None),
        ),
        check_vma=False,
    )
```

```python
import functools
import math

import jax
import jax.numpy as jnp
from jax import lax
from jax.experimental import pallas as pl
from jax.experimental.pallas import tpu as pltpu
from jax.sharding import Mesh
from jax.sharding import PartitionSpec as P

HEADS = 12
HEAD_DIM = 64
HALF = HEAD_DIM // 2
NC = 2
EF = 4
NE = 8
CAP = 192
LANES = 128
SEQS = 4
SIDE = 4
YZ = ("fy", "fz")
FSDP = ("fy", "fz", "core")
ANY = pl.BlockSpec(memory_space=pl.ANY)
EPS = 1e-06
SCALE = HEAD_DIM ** (-0.5)
LOWEST = -1e30
F32 = jnp.float32
BF16 = jnp.bfloat16
VMEM = pl.BlockSpec(memory_space=pltpu.VMEM)
SMEM = pl.BlockSpec(memory_space=pltpu.SMEM)


def mm(a, b, ca=1, cb=0):
    return lax.dot_general(a, b, (((ca,), (cb,)), ((), ())), preferred_element_type=F32)


def params(mib, grid=None):
    if grid is None:
        return pltpu.CompilerParams(vmem_limit_bytes=mib << 20)
    return pltpu.CompilerParams(
        vmem_limit_bytes=mib << 20, dimension_semantics=("arbitrary",) * grid
    )


def sds(shape, dtype):
    return jax.ShapeDtypeStruct(shape, dtype)


def took(us):
    return pl.CostEstimate(flops=int(us * 1.1e9), bytes_accessed=1 << 16, transcendentals=0)


def far(x):
    return pltpu.with_memory_space_constraint(x, pltpu.HBM)


def hbm(shape, dtype):
    return pltpu.HBM(shape, dtype)


def whole(x):
    return pl.BlockSpec(x.shape, lambda i: (0,) * len(x.shape))


def come(*arrays):
    return [(x, whole(x)) for x in arrays]


def one_step(body, us, meta, inputs, results, scratch=(), before=(), mib=14, near=0):
    inputs = [x if isinstance(x, tuple) else (far(x), whole(x)) for x in inputs]
    shapes = [(sds if k < near else hbm)(*r) for k, r in enumerate(results)]
    return pl.pallas_call(
        body,
        grid=(1,),
        in_specs=[SMEM] + [spec for _, spec in inputs] + [ANY] * len(before),
        out_specs=[VMEM if k < near else whole(r) for k, r in enumerate(shapes)],
        out_shape=shapes,
        scratch_shapes=list(scratch),
        compiler_params=params(mib, 1),
        cost_estimate=took(us),
        name=getattr(body, "func", body).__name__.removesuffix("_kernel"),
    )(meta, *[x for x, _ in inputs], *map(far, before))


def shift(x, by):
    count = lax.axis_size("seq")
    return lax.ppermute(x, "seq", [(i, (i + by) % count) for i in range(count)])


def trade(x, by, axis="seq"):
    count = lax.axis_size(axis)
    return lax.ppermute(x, axis, [(i, i ^ by) for i in range(count)]) if by else x


def trades(pieces, axis="seq"):
    return [trade(piece, k, axis) for k, piece in enumerate(pieces)]


def around(meta, by):
    return lax.bitwise_xor(meta[1], by)


def swap(x, axis):
    return lax.all_to_all(x, axis, split_axis=0, concat_axis=0, tiled=True)


def two_parts(x):
    high = x.astype(BF16)
    return high, (x - high.astype(F32)).astype(BF16)


def lane_of(shape):
    return lax.broadcasted_iota(jnp.int32, shape, 1)


def pick(values, lanes, lane):
    return jnp.sum(jnp.where(lanes == lane, values, 0.0), axis=1, keepdims=True)


def tiles_moved(x, rows, columns):
    tiles = [
        x[r : r + 8, c : c + LANES]
        for r in range(0, x.shape[0], 8)
        for c in range(0, x.shape[1], LANES)
    ]
    count = columns // LANES
    lines = [jnp.concatenate(tiles[k : k + count], axis=1) for k in range(0, len(tiles), count)]
    return jnp.concatenate(lines, axis=0)


def pack_kernel(
    meta,
    attend_in,
    gain_a,
    attend_out,
    router,
    const_mix,
    const_vector,
    gain_m,
    w_in,
    w_out,
    first,
    second,
    back,
    in_mine,
    out_mine,
    sems,
):
    shard, model = attend_out.shape
    group = model // SEQS
    me = meta[1]
    in_copy = pltpu.make_async_copy(w_in.at[me], in_mine, sems.at[0])
    out_copy = pltpu.make_async_copy(w_out.at[me], out_mine, sems.at[1])
    in_copy.start()
    out_copy.start()
    used = NE + 3 * NC + 2
    rows = [router[...], const_mix[...], const_vector[...], gain_m[...], gain_a[...]]
    rows = jnp.concatenate([*rows, jnp.zeros((LANES - used, shard), F32)], axis=0)
    rows = jnp.concatenate([rows, jnp.zeros((LANES, LANES - shard), F32)], axis=1)
    small = jnp.transpose(rows)[:shard]
    lanes = lane_of(small.shape)

    pieces, own = [], []
    for k in range(3):
        parts = [
            attend_in[:, k * model + g * group : k * model + (g + 1) * group] for g in range(SEQS)
        ]
        mine = parts[0]
        for g in range(1, SEQS):
            mine = jnp.where(me == g, parts[g], mine)
        pieces.append(parts)
        own.append(mine)
    gain = pltpu.roll(small, LANES - (used - 1), 1)[:, :64]
    gain = jnp.where(lane_of(gain.shape) == 0, gain, 0.0)
    row = jnp.concatenate([*own, gain], axis=1).astype(BF16)
    first[...] = jnp.broadcast_to(row[None], first.shape)
    back[...] = jnp.concatenate(
        [pieces[k][g] for g in range(SEQS) for k in range(3)], axis=1
    ).astype(BF16)

    small = jnp.where(lanes < used - 1, small, 0.0)
    second[:, :model] = attend_out[...].astype(BF16)
    second[:, model : model + 2 * LANES] = jnp.concatenate(
        [small, jnp.zeros_like(small)], axis=1
    ).astype(BF16)
    at = model + 2 * LANES
    wide = in_mine.shape[1]
    in_copy.wait()
    second[:, at : at + wide] = in_mine[...].astype(BF16)
    out_copy.wait()
    at += wide
    second[:, at:] = tiles_moved(out_mine[...], shard, second.shape[1] - at).astype(BF16)


def pack(meta, attend_in, gain_a, attend_out, router, const_mix, const_vector, gain_m, w_in, w_out, count):
    shard, model = attend_out.shape
    wide = model + 2 * LANES + w_in.shape[2] + w_out.shape[1] * model // shard
    plain = (attend_in, gain_a, attend_out, router, const_mix, const_vector, gain_m)
    results = [
        sds((count, shard, 3 * model // SEQS + 64), BF16),
        sds((shard, wide), BF16),
        sds(attend_in.shape, BF16),
    ]
    return pl.pallas_call(
        pack_kernel,
        grid=(1,),
        in_specs=[SMEM] + [whole(x) for x in plain] + [ANY] * 2,
        out_specs=[whole(x) for x in results],
        out_shape=results,
        scratch_shapes=[
            pltpu.VMEM(w_in.shape[1:], F32),
            pltpu.VMEM(w_out.shape[1:], F32),
            pltpu.SemaphoreType.DMA((2,)),
        ],
        compiler_params=params(14, 1),
        cost_estimate=took(2),
        name="pack",
    )(meta, *map(far, (*plain, w_in, w_out)))


def plan_kernel(meta, routes, prior, table, cotangent, slots, grad, logits, counts, *sent):
    rows = routes.shape[1]
    width = cotangent.shape[1]
    ids = lax.broadcasted_iota(jnp.int32, (NE, rows), 0)
    hits = (ids == routes[0:1]) | (ids == routes[1:2])
    before = lax.broadcasted_iota(jnp.int32, (rows, rows), 0)
    before = before < lax.broadcasted_iota(jnp.int32, (rows, rows), 1)
    ranks = mm(jnp.where(hits, 1.0, 0.0).astype(BF16), jnp.where(before, 1.0, 0.0).astype(BF16))
    ranks = jnp.where(hits, ranks.astype(jnp.int32), -1)
    lines = lax.broadcasted_iota(jnp.int32, (CAP, rows), 0)
    for e in range(EF):
        slots[e] = jnp.where(lines == ranks[e : e + 1], 1.0, 0.0).astype(BF16)
    spots = lax.broadcasted_iota(jnp.int32, (rows, width), 0) + meta[1] * rows
    live = jnp.where(spots < meta[0], cotangent[...].astype(F32), 0.0).astype(BF16)
    grad[...] = live
    for s in range(SEQS):
        sent[s][...] = mm(slots[around(meta, s)], live).astype(BF16)
    count = (ids == prior[0:1]).astype(F32) + (ids == prior[1:2]).astype(F32)
    named = routes[...].astype(F32)
    flat = [count, named, jnp.zeros((LANES - NE - 2, rows), F32)]
    flat = jnp.transpose(jnp.concatenate(flat, axis=0))
    lanes = lane_of(flat.shape)
    count = jnp.where(lanes < NE, flat, 0.0).astype(BF16)
    counts[...] = count
    full = jnp.concatenate([table[...], jnp.zeros((NE, LANES - NE), F32)], axis=1)
    full = jnp.concatenate([full, jnp.zeros((LANES - NE, LANES), F32)], axis=0)
    total = jnp.zeros(flat.shape, F32)
    for _ in range(3):
        part = full.astype(BF16)
        full = full - part.astype(F32)
        total += mm(count, part)
    named = pltpu.roll(flat, NE, 1)
    logits[...] = jnp.where((lanes >= 2 * NE) & (lanes < 2 * NE + 2), named, total)


def plan(meta, routes, prior, table, cotangent):
    rows, model = cotangent.shape
    results = [
        ((EF, CAP, rows), BF16),
        ((rows, model), BF16),
        ((rows, LANES), F32),
        ((rows, LANES), BF16),
    ] + [((CAP, model), BF16)] * SEQS
    return one_step(plan_kernel, 1, meta, [routes, prior, table, cotangent], results, mib=24)


def project_kernel(meta, *refs):
    sources, (weight, gain, cosine, sine, qkv, normed) = refs[:5], refs[5:]
    width = qkv.shape[1]
    part = width // 3
    for to, which in ((0, (0,)), (3, (1,)), (1, (2,)), (2, (3, 4))):
        place = lax.rem(meta[1] + to, SEQS)
        done = 0
        for source in [sources[k] for k in which]:
            at = slice(done, done + source.shape[0])
            done = at.stop
            v = source[...].astype(F32)
            n = v * lax.rsqrt(jnp.mean(v * v, axis=-1, keepdims=True) + EPS) * gain[...]
            normed[place, at] = n.astype(BF16)
        flat = jnp.transpose(mm(normed[place], weight[:, :width]))
        c, s = cosine[place], sine[place]
        for which in range(2):
            factor = SCALE if which == 0 else 1.0
            for at in range(which * part, (which + 1) * part, HEAD_DIM):
                a, b = flat[at : at + HALF], flat[at + HALF : at + HEAD_DIM]
                qkv[place, at : at + HALF] = ((a * c - b * s) * factor).astype(BF16)
                qkv[place, at + HALF : at + HEAD_DIM] = ((b * c + a * s) * factor).astype(BF16)
        qkv[place, 2 * part :] = flat[2 * part :].astype(BF16)


def project(meta, sources, weight, gain, cosine, sine, width):
    rows, model = sources[0].shape
    results = [((SEQS, width, rows), BF16), ((SEQS, rows, model), BF16)]
    inputs = [*come(*sources, weight, gain), cosine, sine]
    return one_step(project_kernel, 100, meta, inputs, results, mib=20, near=1)


def mask_diagonal(scores, start, length):
    keys = lax.broadcasted_iota(jnp.int32, scores.shape, 0)
    queries = lax.broadcasted_iota(jnp.int32, scores.shape, 1)
    return jnp.where((keys <= queries) & (keys + start < length), scores, LOWEST)


def attend_kernel(meta, qkv, out, lse, kept, top, total, acc, sem):
    copy = pltpu.make_async_copy(qkv, kept, sem)
    copy.start()
    rows = qkv.shape[2]
    part = qkv.shape[1] // 3
    heads = part // HEAD_DIM
    length = meta[0]
    spans = [
        [slice(k * part + h * HEAD_DIM, k * part + (h + 1) * HEAD_DIM) for k in range(3)]
        for h in range(heads)
    ]
    for block in range(SEQS):
        for h, (at, k_at, v_at) in enumerate(spans):
            scores = mm(qkv[block, k_at], qkv[block, at], 0, 0)
            scores = mask_diagonal(scores, block * rows, length)
            peak = jnp.max(scores, axis=0, keepdims=True)
            e = jnp.exp(scores - peak)
            top[h : h + 1] = peak
            total[h : h + 1] = jnp.sum(e, axis=0, keepdims=True)
            acc[at] = mm(qkv[block, v_at], e.astype(BF16))

        def step(j, carry, block=block):
            for h, (at, k_at, v_at) in enumerate(spans):
                scores = mm(qkv[j, k_at], qkv[block, at], 0, 0)
                last = top[h : h + 1]
                peak = jnp.maximum(last, jnp.max(scores, axis=0, keepdims=True))
                e = jnp.exp(scores - peak)
                fade = jnp.exp(last - peak)
                top[h : h + 1] = peak
                total[h : h + 1] = total[h : h + 1] * fade + jnp.sum(e, axis=0, keepdims=True)
                acc[at] = acc[at] * fade + mm(qkv[j, v_at], e.astype(BF16))
            return carry

        lax.fori_loop(0, block, step, 0)
        for h, (at, _, _) in enumerate(spans):
            out[block, at] = (acc[at] / total[h : h + 1]).astype(BF16)
            lse[block, h : h + 1] = top[h : h + 1] + jnp.log(total[h : h + 1])
    copy.wait()


def attend(meta, qkv):
    _, width, rows = qkv.shape
    part = width // 3
    results = [sds((SEQS, part, rows), BF16), sds((SEQS, 8, rows), F32)]
    return pl.pallas_call(
        attend_kernel,
        grid=(1,),
        in_specs=[SMEM, VMEM],
        out_specs=[whole(x) for x in results] + [ANY],
        out_shape=[hbm(x.shape, x.dtype) for x in (*results, qkv)],
        scratch_shapes=[
            pltpu.VMEM((8, rows), F32),
            pltpu.VMEM((8, rows), F32),
            pltpu.VMEM((part, rows), F32),
            pltpu.SemaphoreType.DMA,
        ],
        compiler_params=params(20, 1),
        cost_estimate=took(0.1),
        name="attend",
    )(meta, qkv)


def attend_back_kernel(meta, qkv, *refs):
    dout, out, lse, cosine, sine, normed = refs[:6]
    dproj = refs[-8 - SEQS : -8]
    kept, gone, dq, dk, dv, dots, normed_held, sem = refs[-8:]
    blocks, width, rows = qkv.shape
    part = width // 3
    heads = part // HEAD_DIM
    length = meta[0]

    copy = pltpu.make_async_copy(normed, normed_held, sem)
    copy.start()

    def pair(q, k, diagonal):
        for h in range(heads):
            at = slice(h * HEAD_DIM, (h + 1) * HEAD_DIM)
            k_at = slice(part + h * HEAD_DIM, part + (h + 1) * HEAD_DIM)
            v_at = slice(2 * part + h * HEAD_DIM, 2 * part + (h + 1) * HEAD_DIM)
            qh, kh, vh, doh = qkv[q, at], qkv[k, k_at], qkv[k, v_at], dout[q, at]
            scores = mm(kh, qh, 0, 0)
            if diagonal:
                scores = mask_diagonal(scores, k * rows, length)
            probs = jnp.exp(scores - lse[q, h : h + 1])
            dprobs = mm(vh, doh, 0, 0)
            low = probs.astype(BF16)
            dscores = (probs * (dprobs - dots[q, h : h + 1])).astype(BF16)
            if diagonal:
                dv[k, at] = mm(doh, low, 1, 1)
                dk[k, at] = mm(qh, dscores, 1, 1)
                dq[q, at] = mm(kh, dscores)
            else:
                dv[k, at] += mm(doh, low, 1, 1)
                dk[k, at] += mm(qh, dscores, 1, 1)
                dq[q, at] += mm(kh, dscores)

    for b in range(SEQS):
        for h in range(heads):
            at = slice(h * HEAD_DIM, (h + 1) * HEAD_DIM)
            both = dout[b, at].astype(F32) * out[b, at].astype(F32)
            dots[b, h : h + 1] = jnp.sum(both, axis=0, keepdims=True)

    def diagonal(b, carry):
        pair(b, b, True)
        return carry

    def below(q, carry):
        def one(k, inner):
            pair(q, k, False)
            return inner

        return lax.fori_loop(0, q, one, carry)

    lax.fori_loop(0, blocks, diagonal, 0)
    lax.fori_loop(1, blocks, below, 0)
    for to in range(SEQS):
        b = around(meta, to)
        c, s = cosine[b], sine[b]
        for which, held in ((0, dq), (1, dk)):
            factor = SCALE if which == 0 else 1.0
            for h in range(heads):
                at = h * HEAD_DIM
                rounded = (held[b, at : at + HEAD_DIM] * factor).astype(BF16).astype(F32)
                x, y = rounded[:HALF], rounded[HALF:]
                at += which * part
                dproj[to][at : at + HALF] = (x * c + y * s).astype(BF16)
                dproj[to][at + HALF : at + HEAD_DIM] = (y * c - x * s).astype(BF16)
        dproj[to][2 * part :] = dv[b].astype(BF16)

    copy.wait()
    pairs, shard, _ = kept.shape
    even = meta[2] == 0

    def halves(x, at):
        x = x.reshape(pairs, 2 * shard, x.shape[1])
        first, second = x[:, :shard], x[:, shard:]
        kept[:, :, at : at + x.shape[2]] = jnp.where(even, first, second).astype(BF16)
        gone[:, :, at : at + x.shape[2]] = jnp.where(even, second, first).astype(BF16)

    total = mm(dproj[0][...], normed_held[around(meta, 0)])
    for to in range(1, SEQS):
        total += mm(dproj[to][...], normed_held[around(meta, to)])
    halves(jnp.transpose(total), 0)


def attend_back(meta, before, qkv, dout, out, lse, cosine, sine, normed, count):
    blocks, width, rows = qkv.shape
    part = width // 3
    model = normed.shape[2]
    scratch = [pltpu.VMEM((blocks, part, rows), F32)] * 3 + [pltpu.VMEM((blocks, 8, rows), F32)]
    scratch += [pltpu.VMEM(normed.shape, BF16), pltpu.SemaphoreType.DMA]
    inputs = [qkv, *come(dout), out, lse, cosine, sine, (far(normed), ANY)]
    results = [((width, rows), BF16)] * SEQS
    results += [((count // 2, model // count, width), BF16)] * 2
    return one_step(attend_back_kernel, 12, meta, inputs, results, scratch, before, 48)


def dense_kernel(meta, att, dlow, moe, dlogits, grad_vec, dgain, prior_hits, *refs):
    kept, gone = refs[-2:]
    pairs, shard, _ = kept.shape
    model = att.shape[0]
    even = meta[2] == 0

    def halves(x, at):
        x = x.reshape(pairs, 2 * shard, x.shape[1])
        first, second = x[:, :shard], x[:, shard:]
        kept[:, :, at : at + x.shape[2]] = jnp.where(even, first, second).astype(BF16)
        gone[:, :, at : at + x.shape[2]] = jnp.where(even, second, first).astype(BF16)

    halves(mm(att[...], dlow[...]), 0)
    high, rest = two_parts(dlogits[...])
    result = mm(moe[...], high, 0, 0) + mm(moe[...], rest, 0, 0)
    result += pltpu.roll(grad_vec[...], NE + 2 * NC, 1)
    lanes = lane_of(result.shape)
    column = jnp.transpose(jnp.broadcast_to(dgain[...], (LANES, model)))
    result += jnp.where(lanes == NE + 3 * NC, column, 0.0)
    table = mm(prior_hits[...], high, 0, 0) + mm(prior_hits[...], rest, 0, 0)
    table = jnp.where(lane_of((NE, LANES)) < NE, table[:NE], 0.0)
    high, rest = two_parts(table)
    block = pltpu.roll(high.astype(F32), 2 * NE, 1) + pltpu.roll(rest.astype(F32), 3 * NE, 1)
    block = jnp.concatenate([block, jnp.zeros((shard - NE, LANES), F32)], axis=0)
    result = result.reshape(2 * pairs, shard, LANES) + block[None]
    halves(result.reshape(model, LANES), model)


def dense(meta, att, dlow, moe, dlogits, grad_vec, dgain, prior_hits, count, *before):
    model = dlow.shape[1]
    inputs = [*come(att), dlow, moe, dlogits, grad_vec, dgain, prior_hits]
    results = [((count // 2, model // count, model + LANES), BF16)] * 2
    return one_step(dense_kernel, 0.1, meta, inputs, results, (), before, 24)


def route_kernel(meta, att, out_w, small_w, tok, prior, slots, *refs):
    sent = refs[-4 - SEQS : -4]
    resid, moe, stats, vectors = refs[-4:]
    res = tok[...].astype(F32) + mm(att[...], out_w[...], 0, 0)
    flipped = jnp.transpose(small_w[...].astype(F32))
    vectors[...] = flipped[NE + 2 * NC : NE + 2 * NC + 8]
    gain = flipped[NE + 3 * NC : NE + 3 * NC + 1]
    resid[...] = res
    normed = res * lax.rsqrt(jnp.mean(res * res, axis=-1, keepdims=True) + EPS) * gain
    low = normed.astype(BF16)
    moe[...] = low
    small = mm(low, small_w[...])
    small = jnp.where(lane_of(small.shape) < NE + 2 * NC, small, 0.0)
    lanes = lane_of(small.shape)
    known = prior[...]
    logits = small + jnp.where(lanes < NE, known, 0.0)
    named = lanes.astype(F32)
    hit0 = named == known[:, 2 * NE : 2 * NE + 1]
    hit1 = named == known[:, 2 * NE + 1 : 2 * NE + 2]
    chosen0 = jnp.sum(jnp.where(hit0, logits, 0.0), axis=1, keepdims=True)
    chosen1 = jnp.sum(jnp.where(hit1, logits, 0.0), axis=1, keepdims=True)
    gate0 = 1.0 / (1.0 + jnp.exp(chosen1 - chosen0))
    gate1 = 1.0 / (1.0 + jnp.exp(chosen0 - chosen1))
    share = jnp.where(hit0, gate0, 0.0) + jnp.where(hit1, gate1, 0.0)
    partner = jnp.where(lanes % 2 == 0, pltpu.roll(small, LANES - 1, 1), pltpu.roll(small, 1, 1))
    mix = 1.0 / (1.0 + jnp.exp(partner - small))
    mixing = (lanes >= NE) & (lanes < NE + 2 * NC)
    stats[...] = share + jnp.where(mixing, mix, 0.0)
    high, rest = two_parts(share)
    parts = (high.astype(F32) + pltpu.roll(rest.astype(F32), NE, 1)).astype(BF16)
    model = low.shape[1]
    for s in range(SEQS):
        chosen = slots[around(meta, s)]
        sent[s][:, :model] = mm(chosen, low).astype(BF16)
        sent[s][:, model:] = mm(chosen, parts).astype(BF16)


def weight_blocks(weights):
    model = weights.shape[0]
    return [
        (far(weights), pl.BlockSpec((model, model), lambda i: (0, 0))),
        (far(weights), pl.BlockSpec((model, LANES), lambda i: (0, model // LANES))),
    ]


def route(meta, att, weights, tok, prior, slots, *before):
    rows, model = tok.shape
    results = [((CAP, model + LANES), BF16)] * SEQS + [
        ((rows, model), F32),
        ((rows, model), BF16),
        ((rows, LANES), F32),
        ((8, model), F32),
    ]
    inputs = [*come(att), *weight_blocks(weights), tok, prior, slots]
    return one_step(route_kernel, 100, meta, inputs, results, (), before, 24)


def local_part_kernel(meta, resid, stats, grad, vectors, partial, small, grad_vec):
    gain = vectors[NC : NC + 1]
    res, g = resid[...], grad[...].astype(F32)
    normed = res * lax.rsqrt(jnp.mean(res * res, axis=-1, keepdims=True) + EPS) * gain
    held = stats[...]
    lanes = lane_of(held.shape)
    copy_dot = jnp.sum(g * normed, axis=1, keepdims=True)
    factor = pick(held, lanes, EF + 1)
    result = jnp.where(lanes == EF + 1, factor * copy_dot, 0.0)
    ways = jnp.zeros_like(held)
    added = jnp.zeros_like(res)
    for j in range(NC):
        row = vectors[j : j + 1]
        weight = pick(held, lanes, EF + 2 + j)
        first = pick(held, lanes, NE + 2 * j)
        second = pick(held, lanes, NE + 2 * j + 1)
        vec_dot = jnp.sum(g * row, axis=1, keepdims=True)
        mean = first * copy_dot + second * vec_dot
        result += jnp.where(lanes == EF + 2 + j, weight * mean, 0.0)
        result += jnp.where(lanes == NE + 2 * j, weight * first * (copy_dot - mean), 0.0)
        result += jnp.where(lanes == NE + 2 * j + 1, weight * second * (vec_dot - mean), 0.0)
        ways += jnp.where(lanes == j, weight * second, 0.0)
        added += (weight * second) * row
        factor += weight * first
    small[...] = result + jnp.where(lanes == NE + 2 * NC, factor, 0.0)
    partial[...] = res + factor * normed + added
    high, rest = two_parts(ways)
    grad_vec[...] = mm(grad[...], high, 0, 0) + mm(grad[...], rest, 0, 0)


def local_part(meta, resid, stats, grad, vectors):
    rows, model = resid.shape
    results = [((rows, model), F32), ((rows, LANES), F32), ((model, LANES), F32)]
    return one_step(local_part_kernel, 0.1, meta, [resid, stats, grad, vectors], results, mib=16)


def expert_kernel(meta, *refs):
    sent, grads = refs[:SEQS], refs[SEQS : 2 * SEQS]
    gate_w, up_w, out_w = refs[2 * SEQS + 1 : 2 * SEQS + 4]
    back, branch = refs[2 * SEQS + 4 : 3 * SEQS + 4], refs[3 * SEQS + 4]
    in_kept, in_sent, out_kept, out_sent = refs[3 * SEQS + 5 : 3 * SEQS + 9]
    rows, flipped, held, scaled, gate, hidden, dgate, dup, acc, mixed_acc, dots = refs[-11:]
    step = pl.program_id(0)
    count, model = rows.shape
    block = gate_w.shape[1]
    me = meta[1]
    even = meta[2] == 0

    def split(x, kept, gone):
        pairs, shard, wide = kept.shape
        x = x.reshape(pairs, 2 * shard, wide)
        first, second = x[:, :shard], x[:, shard:]
        kept[...] = jnp.where(even, first, second).astype(BF16)
        gone[...] = jnp.where(even, second, first).astype(BF16)

    @pl.when(step == 0)
    def _():
        for s in range(SEQS):
            at = slice(s * CAP, (s + 1) * CAP)
            rows[at] = sent[s][:, :model]
            flipped[:, at] = jnp.transpose(sent[s][:, :model])
            held[at] = grads[s][...]
            parts = sent[s][:, model:].astype(F32)
            lanes = lane_of(parts.shape)
            own = (lanes == me) | (lanes == me + NE)
            share = jnp.sum(jnp.where(own, parts, 0.0), axis=1, keepdims=True)
            gate[at] = jnp.broadcast_to(share, (CAP, LANES))
            scaled[at] = (grads[s][...].astype(F32) * share).astype(BF16)
        acc[...] = jnp.zeros_like(acc)
        mixed_acc[...] = jnp.zeros_like(mixed_acc)
        dots[...] = jnp.zeros_like(dots)

    for at in (slice(0, count // 2), slice(count // 2, count)):
        g = mm(rows[at], gate_w[...])
        u = mm(rows[at], up_w[...])
        v = mm(held[at], out_w[...], 1, 1)
        sig = 1.0 / (1.0 + jnp.exp(-g))
        silu = g * sig
        low = (silu * u).astype(BF16)
        hidden[at] = low
        both = v * low.astype(F32)
        folded = both[:, :LANES]
        for c in range(LANES, block, LANES):
            folded = folded + both[:, c : c + LANES]
        dots[at] += folded
        d = v * gate[at, 0:1]
        du = (d * silu).astype(BF16)
        dg = (d * u * (sig * (1.0 + g * (1.0 - sig)))).astype(BF16)
        dgate[at] = dg
        dup[at] = du
        acc[at] += mm(dg, gate_w[...], 1, 1) + mm(du, up_w[...], 1, 1)
        mixed_acc[at] += mm(low, out_w[...])

    split(mm(flipped[...], dgate[...]), in_kept.at[0, 0], in_sent.at[0, 0])
    split(mm(flipped[...], dup[...]), in_kept.at[0, 1], in_sent.at[0, 1])
    split(mm(hidden[...], scaled[...], 0, 0), out_kept, out_sent)

    @pl.when(step == pl.num_programs(0) - 1)
    def _():
        for s in range(SEQS):
            at = slice(s * CAP, (s + 1) * CAP)
            back[s][:, :model] = acc[at].astype(BF16)
            value = jnp.sum(dots[at], axis=1, keepdims=True) * gate[at]
            lanes = lane_of(value.shape)
            high, rest = two_parts(value)
            back[s][:, model:] = (
                jnp.where(lanes == me, high.astype(F32), 0.0)
                + jnp.where(lanes == me + NE, rest.astype(F32), 0.0)
            ).astype(BF16)
            branch[around(meta, s)] = (mixed_acc[at] * gate[at, 0:1]).astype(BF16)


def expert(meta, sent, grads, before, weights, w_out, block, fsdp):
    count, model = SEQS * CAP, grads[0].shape[1]
    inner = w_out.shape[0]
    steps = inner // block
    skip = (model + 2 * LANES) // block
    pairs, in_rows, out_rows = fsdp // 2, model // fsdp, inner // fsdp
    per = block // (2 * out_rows)
    results = [sds(sent[0].shape, BF16)] * SEQS + [sds((SEQS, CAP, model), BF16)]
    in_spec = pl.BlockSpec((1, 2, pairs, in_rows, block), lambda i: (i, 0, 0, 0, 0))
    out_spec = pl.BlockSpec((per, out_rows, model), lambda i: (i, 0, 0))
    return pl.pallas_call(
        expert_kernel,
        grid=(steps,),
        in_specs=[SMEM]
        + [whole(x) for x in (*sent, *grads)]
        + [
            ANY,
            pl.BlockSpec((model, block), lambda i: (0, i + skip)),
            pl.BlockSpec((model, block), lambda i: (0, i + skip + steps)),
            pl.BlockSpec((block, model), lambda i: (i, 0)),
        ],
        out_specs=[whole(x) for x in results] + [in_spec, in_spec, out_spec, out_spec],
        out_shape=[hbm(r.shape, r.dtype) for r in results]
        + [hbm((steps, 2, pairs, in_rows, block), BF16)] * 2
        + [hbm((pairs, out_rows, model), BF16)] * 2,
        scratch_shapes=[
            pltpu.VMEM((count, model), BF16),
            pltpu.VMEM((model, count), BF16),
            pltpu.VMEM((count, model), BF16),
            pltpu.VMEM((count, model), BF16),
            pltpu.VMEM((count, LANES), F32),
            pltpu.VMEM((count, block), BF16),
            pltpu.VMEM((count, block), BF16),
            pltpu.VMEM((count, block), BF16),
            pltpu.VMEM((count, model), F32),
            pltpu.VMEM((count, model), F32),
            pltpu.VMEM((count, LANES), F32),
        ],
        compiler_params=params(52, 1),
        cost_estimate=took(10),
        name="expert",
    )(meta, *sent, *grads, *map(far, (before, weights, weights, w_out)))


def split_again(small):
    lanes = lane_of(small.shape)
    table = small + pltpu.roll(small, LANES - NE, 1)
    high = table.astype(BF16).astype(F32)
    rest = pltpu.roll(table - high, NE, 1)
    at = lanes // NE
    return jnp.where(at == 2, high, jnp.where(at == 3, rest, small))


def add_cores_kernel(in_a, in_b, out_a, out_b, *refs):
    blocks, _, _, shard, block = in_a.shape
    wide = 2 * blocks * block
    for k in range(in_a.shape[2]):
        both = refs[-1].at[k]
        for j in range(2 * blocks):
            at = (j % blocks, j // blocks, k)
            total = in_a[at].astype(F32) + in_b[at].astype(F32)
            both[:, j * block : (j + 1) * block] = total.astype(BF16)
        more = out_a[k].astype(F32) + out_b[k].astype(F32)
        both[:, wide:] = tiles_moved(more, shard, both.shape[1] - wide).astype(BF16)


def add_cores(parts, *before):
    blocks, _, pairs, shard, block = parts[0].shape
    wide = 2 * blocks * block
    more = parts[2].shape[1] * parts[2].shape[2] // shard

    def some(shape):
        return pl.BlockSpec((SIDE, *shape), lambda i: (i, 0, 0))

    return pl.pallas_call(
        add_cores_kernel,
        grid=(pairs // SIDE,),
        in_specs=[pl.BlockSpec((blocks, 2, SIDE, shard, block), lambda i: (0, 0, i, 0, 0))] * 2
        + [some(x.shape[1:]) for x in parts[2:]]
        + [ANY] * len(before),
        out_specs=some((shard, wide + more)),
        out_shape=hbm((pairs, shard, wide + more), BF16),
        compiler_params=params(24, 1),
        cost_estimate=took(0.1),
        name="add_cores",
    )(*[x if k % 2 else far(x) for k, x in enumerate(parts)], *map(far, before))


def add_dense_kernel(meta, dense_a, dense_b, heads_a, heads_b, *refs):
    out = refs[-1]
    pairs, shard, wide = dense_a.shape
    width, model = heads_a.shape[2], wide - LANES
    for k in range(pairs):
        total = dense_a[k].astype(F32) + dense_b[k].astype(F32)
        out[k, :, :model] = total[:, :model].astype(BF16)
        out[k, :, model:wide] = split_again(total[:, model:]).astype(BF16)
        heads = heads_a[k].astype(F32) + heads_b[k].astype(F32)
        rest = jnp.zeros((shard, out.shape[2] - wide - width), F32)
        out[k, :, wide:] = jnp.concatenate([heads, rest], axis=1).astype(BF16)


def add_dense(meta, kept, come_dense, heads, come_heads, *before):
    pairs, shard, wide = kept.shape
    results = [((pairs, shard, -(-(wide + heads.shape[2]) // LANES) * LANES), BF16)]
    inputs = [kept, *come(come_dense), heads, *come(come_heads)]
    return one_step(add_dense_kernel, 0.1, meta, inputs, results, (), before, 24)[0]


def add_pieces_kernel(meta, pieces, *refs):
    total = pieces[0].astype(F32)
    for k in range(1, pieces.shape[0]):
        total += pieces[k].astype(F32)
    model = pieces.shape[0] * pieces.shape[1] * 2
    small = split_again(total[:, model : model + LANES])
    parts = [total[:, :model], small, total[:, model + LANES :]]
    total = jnp.concatenate(parts, axis=1).astype(BF16)
    refs[-1][...] = total


def add_pieces(meta, pieces, *before):
    results = [(pieces.shape[1:], BF16)]
    return one_step(add_pieces_kernel, 0.1, meta, come(pieces), results, (), before, 24)[0]


def mixed_kernel(meta, partial, slots, *refs):
    result = partial[...]
    for e in range(EF):
        result += mm(slots[e], refs[0][e], 0, 0)
    refs[-1][...] = result.astype(BF16)


def mixed(meta, partial, slots, branch, *before):
    results = [(partial.shape, BF16)]
    (out,) = one_step(mixed_kernel, 0.1, meta, [partial, slots, *come(branch)], results, (), before)
    return out


def unroute_kernel(meta, *refs):
    back = refs[:SEQS]
    out_w, small_w, slots, resid, small, stats, grad, vectors = refs[SEQS : SEQS + 8]
    datt, dres, dlow, dlogits, dgain = refs[-5:]
    gain = vectors[NC : NC + 1]
    rows, model = resid.shape
    held, local = stats[...], small[...]
    lanes = lane_of(held.shape)
    dn = jnp.zeros((rows, model), F32)
    tail = jnp.zeros((rows, LANES), F32)
    for s in range(SEQS):
        chosen = slots[around(meta, s)]
        dn += mm(chosen, back[s][:, :model], 0, 0)
        tail += mm(chosen, back[s][:, model:], 0, 0)
    ffn = tail + pltpu.roll(tail, LANES - NE, 1)
    dots = jnp.where(lanes < EF, ffn, jnp.where(lanes < NE, local, 0.0))
    total = jnp.sum(dots, axis=1, keepdims=True)
    keep = (lanes >= NE) & (lanes < NE + 2 * NC)
    dsmall = jnp.where(lanes < NE, dots - held * total, jnp.where(keep, local, 0.0))
    high, rest = two_parts(dsmall)
    dn += mm(high, small_w[...], 1, 1) + mm(rest, small_w[...], 1, 1)
    g = grad[...].astype(F32)
    dn += pick(local, lanes, NE + 2 * NC) * g
    res = resid[...]
    factor = lax.rsqrt(jnp.mean(res * res, axis=-1, keepdims=True) + EPS)
    normal = res * factor
    dgain[...] = jnp.sum(dn * normal, axis=0, keepdims=True)
    dlogits[...] = dsmall
    scaled = dn * gain
    out = g + factor * (scaled - normal * jnp.mean(scaled * normal, axis=-1, keepdims=True))
    dres[...] = out
    low = out.astype(BF16)
    dlow[...] = low
    datt[...] = mm(out_w[...], low, 1, 1).astype(BF16)


def unroute(meta, before, back, weights, tokenwise):
    rows, model = tokenwise[1].shape
    inputs = [*come(*back), *weight_blocks(weights), *tokenwise]
    results = [
        ((model, rows), BF16),
        ((rows, model), F32),
        ((rows, model), BF16),
        ((rows, LANES), F32),
        ((1, model), F32),
    ]
    return one_step(unroute_kernel, 100, meta, inputs, results, (), before, 32)


def finish_kernel(meta, *refs):
    dproj, (weight, tok, gain, dres) = refs[:SEQS], refs[SEQS : SEQS + 4]
    out, flat = refs[-2:]
    width = dproj[0].shape[0]
    for s in range(SEQS):
        at = pl.multiple_of(around(meta, s) * width, 64)
        flat[pl.ds(at, width)] = dproj[s][...]
    dn = jnp.transpose(mm(weight[...], flat[...]))
    v = tok[...].astype(F32)
    factor = lax.rsqrt(jnp.mean(v * v, axis=-1, keepdims=True) + EPS)
    normal = v * factor
    scaled = dn * gain[...]
    dx = factor * (scaled - normal * jnp.mean(scaled * normal, axis=-1, keepdims=True))
    out[...] = (dres[...] + dx).astype(BF16)


def finish(meta, dproj, weight, tok, gain, dres, *before):
    width, rows = dproj[0].shape
    scratch = [pltpu.VMEM((SEQS * width, rows), BF16)]
    results = [(tok.shape, BF16)]
    inputs = [*come(*dproj), weight, tok, gain, dres]
    return one_step(finish_kernel, 10, meta, inputs, results, scratch, before, 24)[0]


def gather_kernel(meta, *refs):
    pieces = refs[:SEQS]
    grad_in, grad_out = refs[-2:]
    wide = grad_in.shape[2]
    for s in range(SEQS):
        place = around(meta, s)
        grad_in[place] = pieces[s][:, :wide].astype(F32)
        grad_out[place] = tiles_moved(pieces[s][:, wide:].astype(F32), *grad_out.shape[1:])


def gather(meta, pieces, wide, rows, model, *before):
    shard = pieces[0].shape[0]
    results = [((SEQS, shard, wide), F32), ((SEQS, rows, model), F32)]
    return one_step(gather_kernel, 0.1, meta, come(*pieces), results, (), before, 24)


def gather_dense_kernel(meta, *refs):
    pieces, attend_in, gain_a = refs[:SEQS], refs[SEQS], refs[SEQS + 1]
    att_in, grad_gain, att_out, router, const_mix, const_vector, gain, table, held = refs[-9:]
    shard, model = att_out.shape
    group = model // SEQS
    at = model + LANES
    for s in range(SEQS):
        held[around(meta, s)] = pieces[s][...].astype(F32)
    order = [(k, g) for k in range(3) for g in range(SEQS)]
    parts = [held[g][:, at + k * group : at + (k + 1) * group] for k, g in order]
    full = jnp.concatenate(parts, axis=1)
    att_in[...] = full
    low = attend_in[...].astype(BF16).astype(F32)
    column = jnp.sum(full * low, axis=1, keepdims=True)
    column = jnp.concatenate([column, jnp.zeros((LANES - shard, 1), F32)], axis=0)
    row = jnp.transpose(jnp.broadcast_to(column, (LANES, LANES)))[:1, :shard]
    grad_gain[...] = row / gain_a[...].astype(BF16).astype(F32)

    total = held[0][:, :at]
    for s in range(1, SEQS):
        total += held[s][:, :at]
    att_out[...] = total[:, :model]
    small = jnp.concatenate([total[:, model:], jnp.zeros((LANES - shard, LANES), F32)], axis=0)
    both = small + pltpu.roll(small, LANES - NE, 1)
    table[...] = pltpu.roll(both, LANES - 2 * NE, 1)[:NE, :NE]
    small = jnp.transpose(small)[:, :shard]
    at = NE + 2 * NC
    router[...] = small[:NE]
    const_mix[...] = small[NE:at]
    const_vector[...] = small[at : at + NC]
    gain[...] = small[at + NC : at + NC + 1]


def gather_dense(meta, pieces, attend_in, gain):
    shard, wide = pieces[0].shape
    model = attend_in.shape[1] // 3
    results = [attend_in.shape, (1, shard), (shard, model), (NE, shard), (2 * NC, shard)]
    results = [(r, F32) for r in (*results, (NC, shard), (1, shard), (NE, NE))]
    scratch = [pltpu.VMEM((SEQS, shard, wide), F32)]
    inputs = [*come(*pieces), attend_in, gain]
    return one_step(gather_dense_kernel, 0.1, meta, inputs, results, scratch, mib=16)


def shards(
    tokens,
    cotangent,
    lengths,
    routes,
    prior_routes,
    gain_attend,
    attend_in,
    attend_out,
    gain_mix,
    router,
    route_table,
    const_mix,
    const_vector,
    expert_in,
    expert_out,
):
    seqs = lax.axis_size("seq")
    fsdp = lax.axis_size(FSDP)
    here = lax.axis_index("seq")
    tok = tokens[0]
    rows, model = tok.shape
    shard = attend_in.shape[0]
    group = model // seqs
    width = 3 * group
    length = lengths[0]
    meta = jnp.stack([length, here, *(lax.axis_index(a) for a in ("core", *YZ))])
    meta = meta.astype(jnp.int32)

    first, second, back_mine = pack(
        meta,
        attend_in,
        gain_attend[None],
        attend_out,
        router.T,
        const_mix.T,
        const_vector.T,
        gain_mix[None],
        expert_in,
        expert_out,
        fsdp,
    )
    first_all = swap(first, FSDP).reshape(model, width + 64)
    half = rows // 2
    left, right = shift(tok, 1), shift(tok, -1)
    far0, far1 = shift(left[:half], 1), shift(right[half:], -1)
    weights = lax.all_gather(second, FSDP, axis=0, tiled=True)
    back_w = lax.all_gather(back_mine, FSDP, axis=0, tiled=True)
    inner = expert_out.shape[1] * fsdp
    wide = expert_out.shape[1] * model // shard
    w_out = weights[:, model + 2 * LANES + 2 * inner :]
    w_out = w_out.reshape(-1, shard // 8, 8, wide // LANES, LANES).transpose(0, 1, 3, 2, 4)
    w_out = w_out.reshape(-1, model // LANES, 8, LANES).transpose(0, 2, 1, 3).reshape(inner, model)
    gain_a = first_all[:, width].astype(F32)[None]

    slots, grad, prior, prior_hits, *grad_rows = plan(
        meta, routes[0].T, prior_routes[0].T, route_table, cotangent[0]
    )
    inverse = jnp.exp(
        jnp.arange(HALF, dtype=F32) * (-2.0 * math.log(10000.0) / HEAD_DIM)
    )
    angles = jnp.arange(seqs * rows, dtype=F32).reshape(seqs, 1, rows) * inverse[None, :, None]
    cosine, sine = jnp.cos(angles), jnp.sin(angles)

    left, right, *grad_rows = lax.optimization_barrier((left, right, *grad_rows))
    grad_rows = trades(grad_rows)

    qkv, normed = project(
        meta, [tok, left, right, far0, far1], first_all, gain_a, cosine, sine, width
    )
    held, lse, qkv = attend(meta, qkv)
    held, *grad_rows = lax.optimization_barrier((held, *grad_rows))
    att = swap(held, "seq").reshape(model, rows)
    *sent, resid, moe, stats, vectors = route(meta, att, weights, tok, prior, slots)
    sent = trades(sent)
    partial, small, grad_vec = local_part(meta, resid, stats, grad, vectors)

    *results, in_kept, in_sent, out_kept, out_sent = expert(
        meta, sent, grad_rows, small, weights, w_out, 512, fsdp
    )
    back, branch = trades(results[:seqs]), results[seqs]
    in_come, out_come = trade(in_sent, 1, "core"), trade(out_sent, 1, "core")
    both = add_cores((in_kept, in_come, out_kept, out_come), back_w)
    part = both.reshape(-1, both.shape[2])
    part = lax.psum_scatter(part, YZ, scatter_dimension=0, tiled=True)
    tokenwise = (slots, resid, small, stats, grad, vectors)
    datt, dres, dlow, dlogits, dgain_m = unroute(meta, (both,), back, weights, tokenwise)
    dout = swap(datt.reshape(seqs, group, rows), "seq")
    dout, branch = lax.optimization_barrier((dout, branch))
    branch = swap(branch, "seq")
    kept, gone = dense(
        meta, att, dlow, moe, dlogits, grad_vec, dgain_m, prior_hits, fsdp
    )
    come_dense = trade(gone, 1, "core")
    *dproj, heads, gone = attend_back(
        meta, (kept,), qkv, dout, held, lse, cosine, sine, normed, fsdp
    )
    come_heads = trade(gone, 1, "core")
    back_all = trades(dproj)
    sums = add_dense(meta, kept, come_dense, heads, come_heads, branch)
    sums = swap(sums, YZ)
    part, back_all[2] = lax.optimization_barrier((part, back_all[2]))
    pieces = trades([part] * seqs)
    grad_tokens = finish(meta, back_all, back_w, tok, gain_a, dres)
    sums = add_pieces(meta, sums, grad_tokens)
    sums, *pieces = lax.optimization_barrier((sums, *pieces))
    mixed_out = mixed(meta, partial, slots, branch, sums)
    sums = trades([sums] * seqs)
    grad_attend_in, grad_gain_a, grad_att_out, *rest, table = gather_dense(
        meta, sums, attend_in, gain_attend[None]
    )
    grad_router, grad_mix, grad_vector, grad_gain_m = rest
    grad_in, grad_out = gather(
        meta, pieces, 2 * inner, expert_out.shape[1], model
    )
    return (
        mixed_out[None],
        grad_tokens[None],
        grad_gain_a[0],
        grad_attend_in,
        grad_att_out,
        grad_gain_m[0],
        grad_router.T,
        table,
        grad_mix.T,
        grad_vector.T,
        grad_in,
        grad_out,
    )


def solution(mesh):
    fsdp = mesh.shape["fsdp"]
    finer = Mesh(
        mesh.devices.reshape(mesh.shape["seq"], fsdp // (2 * SIDE), SIDE, 2), ("seq", *FSDP)
    )
    placed = (
        P(FSDP, "seq", None),
        P(FSDP, "seq", None),
        P(FSDP),
        P(FSDP, "seq", None),
        P(FSDP, "seq", None),
        P(FSDP),
        P(FSDP, None),
        P(FSDP, None),
        P(FSDP),
        P(FSDP, None),
        P(),
        P(FSDP, None),
        P(FSDP, None),
        P(None, FSDP, None),
        P(None, FSDP, None),
    )
    return jax.shard_map(
        shards,
        mesh=finer,
        in_specs=placed,
        out_specs=(
            P(FSDP, "seq", None),
            P(FSDP, "seq", None),
            P(FSDP),
            P(FSDP, None),
            P(FSDP, None),
            P(FSDP),
            P(FSDP, None),
            P(),
            P(FSDP, None),
            P(FSDP, None),
            P(None, FSDP, None),
            P(None, FSDP, None),
        ),
        check_vma=False,
    )
```

```python
import functools
import math

import jax
import jax.numpy as jnp
from jax import lax
from jax.experimental import pallas as pl
from jax.experimental.pallas import tpu as pltpu
from jax.sharding import Mesh
from jax.sharding import PartitionSpec as P

HEADS = 12
HEAD_DIM = 64
HALF = HEAD_DIM // 2
NC = 2
EF = 4
NE = 8
CAP = 192
LANES = 128
SEQS = 4
SIDE = 4
YZ = ("fy", "fz")
FSDP = ("fy", "fz", "core")
ANY = pl.BlockSpec(memory_space=pl.ANY)
EPS = 1e-06
SCALE = HEAD_DIM ** (-0.5)
LOWEST = -1e30
F32 = jnp.float32
BF16 = jnp.bfloat16
VMEM = pl.BlockSpec(memory_space=pltpu.VMEM)
SMEM = pl.BlockSpec(memory_space=pltpu.SMEM)


def mm(a, b, ca=1, cb=0):
    return lax.dot_general(a, b, (((ca,), (cb,)), ((), ())), preferred_element_type=F32)


def params(mib, grid=None):
    if grid is None:
        return pltpu.CompilerParams(vmem_limit_bytes=mib << 20)
    return pltpu.CompilerParams(
        vmem_limit_bytes=mib << 20, dimension_semantics=("arbitrary",) * grid
    )


def sds(shape, dtype):
    return jax.ShapeDtypeStruct(shape, dtype)


def took(us):
    return pl.CostEstimate(flops=int(us * 1.1e9), bytes_accessed=1 << 16, transcendentals=0)


def far(x):
    return pltpu.with_memory_space_constraint(x, pltpu.HBM)


def hbm(shape, dtype):
    return pltpu.HBM(shape, dtype)


def whole(x):
    return pl.BlockSpec(x.shape, lambda i: (0,) * len(x.shape))


def come(*arrays):
    return [(x, whole(x)) for x in arrays]


def one_step(body, us, meta, inputs, results, scratch=(), before=(), mib=14, near=0):
    inputs = [x if isinstance(x, tuple) else (far(x), whole(x)) for x in inputs]
    shapes = [(sds if k < near else hbm)(*r) for k, r in enumerate(results)]
    return pl.pallas_call(
        body,
        grid=(1,),
        in_specs=[SMEM] + [spec for _, spec in inputs] + [ANY] * len(before),
        out_specs=[VMEM if k < near else whole(r) for k, r in enumerate(shapes)],
        out_shape=shapes,
        scratch_shapes=list(scratch),
        compiler_params=params(mib, 1),
        cost_estimate=took(us),
        name=getattr(body, "func", body).__name__.removesuffix("_kernel"),
    )(meta, *[x for x, _ in inputs], *map(far, before))


def shift(x, by):
    count = lax.axis_size("seq")
    return lax.ppermute(x, "seq", [(i, (i + by) % count) for i in range(count)])


def trade(x, by, axis="seq"):
    count = lax.axis_size(axis)
    return lax.ppermute(x, axis, [(i, i ^ by) for i in range(count)]) if by else x


def trades(pieces, axis="seq"):
    done = {k: trade(pieces[k], k, axis) for k in (2, 1, 3)}
    return [pieces[0]] + [done[k] for k in (1, 2, 3)]


def around(meta, by):
    return lax.bitwise_xor(meta[1], by)


def swap(x, axis):
    return lax.all_to_all(x, axis, split_axis=0, concat_axis=0, tiled=True)


def two_parts(x):
    high = x.astype(BF16)
    return high, (x - high.astype(F32)).astype(BF16)


def lane_of(shape):
    return lax.broadcasted_iota(jnp.int32, shape, 1)


def pick(values, lanes, lane):
    return jnp.sum(jnp.where(lanes == lane, values, 0.0), axis=1, keepdims=True)


def tiles_moved(x, rows, columns):
    tiles = [
        x[r : r + 8, c : c + LANES]
        for r in range(0, x.shape[0], 8)
        for c in range(0, x.shape[1], LANES)
    ]
    count = columns // LANES
    lines = [jnp.concatenate(tiles[k : k + count], axis=1) for k in range(0, len(tiles), count)]
    return jnp.concatenate(lines, axis=0)


def pack_kernel(
    meta,
    attend_in,
    gain_a,
    attend_out,
    router,
    const_mix,
    const_vector,
    gain_m,
    w_in,
    w_out,
    first,
    second,
    back,
    in_mine,
    out_mine,
    sems,
):
    shard, model = attend_out.shape
    group = model // SEQS
    me = meta[1]
    in_copy = pltpu.make_async_copy(w_in.at[me], in_mine, sems.at[0])
    out_copy = pltpu.make_async_copy(w_out.at[me], out_mine, sems.at[1])
    in_copy.start()
    out_copy.start()
    used = NE + 3 * NC + 2
    rows = [router[...], const_mix[...], const_vector[...], gain_m[...], gain_a[...]]
    rows = jnp.concatenate([*rows, jnp.zeros((LANES - used, shard), F32)], axis=0)
    rows = jnp.concatenate([rows, jnp.zeros((LANES, LANES - shard), F32)], axis=1)
    small = jnp.transpose(rows)[:shard]
    lanes = lane_of(small.shape)

    pieces, own = [], []
    for k in range(3):
        parts = [
            attend_in[:, k * model + g * group : k * model + (g + 1) * group] for g in range(SEQS)
        ]
        mine = parts[0]
        for g in range(1, SEQS):
            mine = jnp.where(me == g, parts[g], mine)
        pieces.append(parts)
        own.append(mine)
    gain = pltpu.roll(small, LANES - (used - 1), 1)[:, :64]
    gain = jnp.where(lane_of(gain.shape) == 0, gain, 0.0)
    row = jnp.concatenate([*own, gain], axis=1).astype(BF16)
    first[...] = jnp.broadcast_to(row[None], first.shape)
    back[...] = jnp.concatenate(
        [pieces[k][g] for g in range(SEQS) for k in range(3)], axis=1
    ).astype(BF16)

    small = jnp.where(lanes < used - 1, small, 0.0)
    second[:, :model] = attend_out[...].astype(BF16)
    second[:, model : model + 2 * LANES] = jnp.concatenate(
        [small, jnp.zeros_like(small)], axis=1
    ).astype(BF16)
    at = model + 2 * LANES
    wide = in_mine.shape[1]
    in_copy.wait()
    second[:, at : at + wide] = in_mine[...].astype(BF16)
    out_copy.wait()
    at += wide
    second[:, at:] = tiles_moved(out_mine[...], shard, second.shape[1] - at).astype(BF16)


def pack(meta, attend_in, gain_a, attend_out, router, const_mix, const_vector, gain_m, w_in, w_out, count):
    shard, model = attend_out.shape
    wide = model + 2 * LANES + w_in.shape[2] + w_out.shape[1] * model // shard
    plain = (attend_in, gain_a, attend_out, router, const_mix, const_vector, gain_m)
    results = [
        sds((count, shard, 3 * model // SEQS + 64), BF16),
        sds((shard, wide), BF16),
        sds(attend_in.shape, BF16),
    ]
    return pl.pallas_call(
        pack_kernel,
        grid=(1,),
        in_specs=[SMEM] + [whole(x) for x in plain] + [ANY] * 2,
        out_specs=[whole(x) for x in results],
        out_shape=results,
        scratch_shapes=[
            pltpu.VMEM(w_in.shape[1:], F32),
            pltpu.VMEM(w_out.shape[1:], F32),
            pltpu.SemaphoreType.DMA((2,)),
        ],
        compiler_params=params(14, 1),
        cost_estimate=took(2),
        name="pack",
    )(meta, *map(far, (*plain, w_in, w_out)))


def plan_kernel(meta, routes, prior, table, cotangent, slots, grad, logits, counts, *sent):
    rows = routes.shape[1]
    width = cotangent.shape[1]
    ids = lax.broadcasted_iota(jnp.int32, (NE, rows), 0)
    hits = (ids == routes[0:1]) | (ids == routes[1:2])
    before = lax.broadcasted_iota(jnp.int32, (rows, rows), 0)
    before = before < lax.broadcasted_iota(jnp.int32, (rows, rows), 1)
    ranks = mm(jnp.where(hits, 1.0, 0.0).astype(BF16), jnp.where(before, 1.0, 0.0).astype(BF16))
    ranks = jnp.where(hits, ranks.astype(jnp.int32), -1)
    lines = lax.broadcasted_iota(jnp.int32, (CAP, rows), 0)
    for e in range(EF):
        slots[e] = jnp.where(lines == ranks[e : e + 1], 1.0, 0.0).astype(BF16)
    spots = lax.broadcasted_iota(jnp.int32, (rows, width), 0) + meta[1] * rows
    live = jnp.where(spots < meta[0], cotangent[...].astype(F32), 0.0).astype(BF16)
    grad[...] = live
    for s in range(SEQS):
        sent[s][...] = mm(slots[around(meta, s)], live).astype(BF16)
    count = (ids == prior[0:1]).astype(F32) + (ids == prior[1:2]).astype(F32)
    named = routes[...].astype(F32)
    flat = [count, named, jnp.zeros((LANES - NE - 2, rows), F32)]
    flat = jnp.transpose(jnp.concatenate(flat, axis=0))
    lanes = lane_of(flat.shape)
    count = jnp.where(lanes < NE, flat, 0.0).astype(BF16)
    counts[...] = count
    full = jnp.concatenate([table[...], jnp.zeros((NE, LANES - NE), F32)], axis=1)
    full = jnp.concatenate([full, jnp.zeros((LANES - NE, LANES), F32)], axis=0)
    total = jnp.zeros(flat.shape, F32)
    for _ in range(3):
        part = full.astype(BF16)
        full = full - part.astype(F32)
        total += mm(count, part)
    named = pltpu.roll(flat, NE, 1)
    logits[...] = jnp.where((lanes >= 2 * NE) & (lanes < 2 * NE + 2), named, total)


def plan(meta, routes, prior, table, cotangent):
    rows, model = cotangent.shape
    results = [
        ((EF, CAP, rows), BF16),
        ((rows, model), BF16),
        ((rows, LANES), F32),
        ((rows, LANES), BF16),
    ] + [((CAP, model), BF16)] * SEQS
    return one_step(plan_kernel, 1, meta, [routes, prior, table, cotangent], results, mib=24)


def project_kernel(meta, *refs):
    sources, (weight, gain, cosine, sine, qkv, normed) = refs[:5], refs[5:]
    width = qkv.shape[1]
    part = width // 3
    for to, which in ((0, (0,)), (3, (1,)), (1, (2,)), (2, (3, 4))):
        place = lax.rem(meta[1] + to, SEQS)
        done = 0
        for source in [sources[k] for k in which]:
            at = slice(done, done + source.shape[0])
            done = at.stop
            v = source[...].astype(F32)
            n = v * lax.rsqrt(jnp.mean(v * v, axis=-1, keepdims=True) + EPS) * gain[...]
            normed[place, at] = n.astype(BF16)
        flat = jnp.transpose(mm(normed[place], weight[:, :width]))
        c, s = cosine[place], sine[place]
        for which in range(2):
            factor = SCALE if which == 0 else 1.0
            for at in range(which * part, (which + 1) * part, HEAD_DIM):
                a, b = flat[at : at + HALF], flat[at + HALF : at + HEAD_DIM]
                qkv[place, at : at + HALF] = ((a * c - b * s) * factor).astype(BF16)
                qkv[place, at + HALF : at + HEAD_DIM] = ((b * c + a * s) * factor).astype(BF16)
        qkv[place, 2 * part :] = flat[2 * part :].astype(BF16)


def project(meta, sources, weight, gain, cosine, sine, width):
    rows, model = sources[0].shape
    results = [((SEQS, width, rows), BF16), ((SEQS, rows, model), BF16)]
    inputs = [*come(*sources, weight, gain), cosine, sine]
    return one_step(project_kernel, 100, meta, inputs, results, mib=20, near=1)


def mask_diagonal(scores, start, length):
    keys = lax.broadcasted_iota(jnp.int32, scores.shape, 0)
    queries = lax.broadcasted_iota(jnp.int32, scores.shape, 1)
    return jnp.where((keys <= queries) & (keys + start < length), scores, LOWEST)


def attend_kernel(meta, qkv, out, lse, kept, top, total, acc, sem):
    copy = pltpu.make_async_copy(qkv, kept, sem)
    copy.start()
    rows = qkv.shape[2]
    part = qkv.shape[1] // 3
    heads = part // HEAD_DIM
    length = meta[0]
    spans = [
        [slice(k * part + h * HEAD_DIM, k * part + (h + 1) * HEAD_DIM) for k in range(3)]
        for h in range(heads)
    ]
    for block in range(SEQS):
        for h, (at, k_at, v_at) in enumerate(spans):
            scores = mm(qkv[block, k_at], qkv[block, at], 0, 0)
            scores = mask_diagonal(scores, block * rows, length)
            peak = jnp.max(scores, axis=0, keepdims=True)
            e = jnp.exp(scores - peak)
            top[h : h + 1] = peak
            total[h : h + 1] = jnp.sum(e, axis=0, keepdims=True)
            acc[at] = mm(qkv[block, v_at], e.astype(BF16))

        def step(j, carry, block=block):
            for h, (at, k_at, v_at) in enumerate(spans):
                scores = mm(qkv[j, k_at], qkv[block, at], 0, 0)
                last = top[h : h + 1]
                peak = jnp.maximum(last, jnp.max(scores, axis=0, keepdims=True))
                e = jnp.exp(scores - peak)
                fade = jnp.exp(last - peak)
                top[h : h + 1] = peak
                total[h : h + 1] = total[h : h + 1] * fade + jnp.sum(e, axis=0, keepdims=True)
                acc[at] = acc[at] * fade + mm(qkv[j, v_at], e.astype(BF16))
            return carry

        lax.fori_loop(0, block, step, 0)
        for h, (at, _, _) in enumerate(spans):
            out[block, at] = (acc[at] / total[h : h + 1]).astype(BF16)
            lse[block, h : h + 1] = top[h : h + 1] + jnp.log(total[h : h + 1])
    copy.wait()


def attend(meta, qkv):
    _, width, rows = qkv.shape
    part = width // 3
    results = [sds((SEQS, part, rows), BF16), sds((SEQS, 8, rows), F32)]
    return pl.pallas_call(
        attend_kernel,
        grid=(1,),
        in_specs=[SMEM, VMEM],
        out_specs=[whole(x) for x in results] + [ANY],
        out_shape=[hbm(x.shape, x.dtype) for x in (*results, qkv)],
        scratch_shapes=[
            pltpu.VMEM((8, rows), F32),
            pltpu.VMEM((8, rows), F32),
            pltpu.VMEM((part, rows), F32),
            pltpu.SemaphoreType.DMA,
        ],
        compiler_params=params(20, 1),
        cost_estimate=took(0.1),
        name="attend",
    )(meta, qkv)


def attend_back_kernel(meta, qkv, *refs):
    dout, out, lse, cosine, sine, normed = refs[:6]
    dproj = refs[-8 - SEQS : -8]
    kept, gone, dq, dk, dv, dots, normed_held, sem = refs[-8:]
    blocks, width, rows = qkv.shape
    part = width // 3
    heads = part // HEAD_DIM
    length = meta[0]

    copy = pltpu.make_async_copy(normed, normed_held, sem)
    copy.start()

    def pair(q, k, diagonal):
        for h in range(heads):
            at = slice(h * HEAD_DIM, (h + 1) * HEAD_DIM)
            k_at = slice(part + h * HEAD_DIM, part + (h + 1) * HEAD_DIM)
            v_at = slice(2 * part + h * HEAD_DIM, 2 * part + (h + 1) * HEAD_DIM)
            qh, kh, vh, doh = qkv[q, at], qkv[k, k_at], qkv[k, v_at], dout[q, at]
            scores = mm(kh, qh, 0, 0)
            if diagonal:
                scores = mask_diagonal(scores, k * rows, length)
            probs = jnp.exp(scores - lse[q, h : h + 1])
            dprobs = mm(vh, doh, 0, 0)
            low = probs.astype(BF16)
            dscores = (probs * (dprobs - dots[q, h : h + 1])).astype(BF16)
            if diagonal:
                dv[k, at] = mm(doh, low, 1, 1)
                dk[k, at] = mm(qh, dscores, 1, 1)
                dq[q, at] = mm(kh, dscores)
            else:
                dv[k, at] += mm(doh, low, 1, 1)
                dk[k, at] += mm(qh, dscores, 1, 1)
                dq[q, at] += mm(kh, dscores)

    for b in range(SEQS):
        for h in range(heads):
            at = slice(h * HEAD_DIM, (h + 1) * HEAD_DIM)
            both = dout[b, at].astype(F32) * out[b, at].astype(F32)
            dots[b, h : h + 1] = jnp.sum(both, axis=0, keepdims=True)

    def diagonal(b, carry):
        pair(b, b, True)
        return carry

    def below(q, carry):
        def one(k, inner):
            pair(q, k, False)
            return inner

        return lax.fori_loop(0, q, one, carry)

    lax.fori_loop(0, blocks, diagonal, 0)
    lax.fori_loop(1, blocks, below, 0)
    for to in range(SEQS):
        b = around(meta, to)
        c, s = cosine[b], sine[b]
        for which, held in ((0, dq), (1, dk)):
            factor = SCALE if which == 0 else 1.0
            for h in range(heads):
                at = h * HEAD_DIM
                rounded = (held[b, at : at + HEAD_DIM] * factor).astype(BF16).astype(F32)
                x, y = rounded[:HALF], rounded[HALF:]
                at += which * part
                dproj[to][at : at + HALF] = (x * c + y * s).astype(BF16)
                dproj[to][at + HALF : at + HEAD_DIM] = (y * c - x * s).astype(BF16)
        dproj[to][2 * part :] = dv[b].astype(BF16)

    copy.wait()
    pairs, shard, _ = kept.shape
    even = meta[2] == 0

    def halves(x, at):
        x = x.reshape(pairs, 2 * shard, x.shape[1])
        first, second = x[:, :shard], x[:, shard:]
        kept[:, :, at : at + x.shape[2]] = jnp.where(even, first, second).astype(BF16)
        gone[:, :, at : at + x.shape[2]] = jnp.where(even, second, first).astype(BF16)

    total = mm(dproj[0][...], normed_held[around(meta, 0)])
    for to in range(1, SEQS):
        total += mm(dproj[to][...], normed_held[around(meta, to)])
    halves(jnp.transpose(total), 0)


def attend_back(meta, before, qkv, dout, out, lse, cosine, sine, normed, count):
    blocks, width, rows = qkv.shape
    part = width // 3
    model = normed.shape[2]
    scratch = [pltpu.VMEM((blocks, part, rows), F32)] * 3 + [pltpu.VMEM((blocks, 8, rows), F32)]
    scratch += [pltpu.VMEM(normed.shape, BF16), pltpu.SemaphoreType.DMA]
    inputs = [qkv, *come(dout), out, lse, cosine, sine, (far(normed), ANY)]
    results = [((width, rows), BF16)] * SEQS
    results += [((count // 2, model // count, width), BF16)] * 2
    return one_step(attend_back_kernel, 12, meta, inputs, results, scratch, before, 48)


def dense_kernel(meta, att, dlow, moe, dlogits, grad_vec, dgain, prior_hits, *refs):
    kept, gone = refs[-2:]
    pairs, shard, _ = kept.shape
    model = att.shape[0]
    even = meta[2] == 0

    def halves(x, at):
        x = x.reshape(pairs, 2 * shard, x.shape[1])
        first, second = x[:, :shard], x[:, shard:]
        kept[:, :, at : at + x.shape[2]] = jnp.where(even, first, second).astype(BF16)
        gone[:, :, at : at + x.shape[2]] = jnp.where(even, second, first).astype(BF16)

    halves(mm(att[...], dlow[...]), 0)
    high, rest = two_parts(dlogits[...])
    result = mm(moe[...], high, 0, 0) + mm(moe[...], rest, 0, 0)
    result += pltpu.roll(grad_vec[...], NE + 2 * NC, 1)
    lanes = lane_of(result.shape)
    column = jnp.transpose(jnp.broadcast_to(dgain[...], (LANES, model)))
    result += jnp.where(lanes == NE + 3 * NC, column, 0.0)
    table = mm(prior_hits[...], high, 0, 0) + mm(prior_hits[...], rest, 0, 0)
    table = jnp.where(lane_of((NE, LANES)) < NE, table[:NE], 0.0)
    high, rest = two_parts(table)
    block = pltpu.roll(high.astype(F32), 2 * NE, 1) + pltpu.roll(rest.astype(F32), 3 * NE, 1)
    block = jnp.concatenate([block, jnp.zeros((shard - NE, LANES), F32)], axis=0)
    result = result.reshape(2 * pairs, shard, LANES) + block[None]
    halves(result.reshape(model, LANES), model)


def dense(meta, att, dlow, moe, dlogits, grad_vec, dgain, prior_hits, count, *before):
    model = dlow.shape[1]
    inputs = [*come(att), dlow, moe, dlogits, grad_vec, dgain, prior_hits]
    results = [((count // 2, model // count, model + LANES), BF16)] * 2
    return one_step(dense_kernel, 0.1, meta, inputs, results, (), before, 24)


def route_kernel(meta, att, out_w, small_w, tok, prior, slots, *refs):
    sent = refs[-4 - SEQS : -4]
    resid, moe, stats, vectors = refs[-4:]
    res = tok[...].astype(F32) + mm(att[...], out_w[...], 0, 0)
    flipped = jnp.transpose(small_w[...].astype(F32))
    vectors[...] = flipped[NE + 2 * NC : NE + 2 * NC + 8]
    gain = flipped[NE + 3 * NC : NE + 3 * NC + 1]
    resid[...] = res
    normed = res * lax.rsqrt(jnp.mean(res * res, axis=-1, keepdims=True) + EPS) * gain
    low = normed.astype(BF16)
    moe[...] = low
    small = mm(low, small_w[...])
    small = jnp.where(lane_of(small.shape) < NE + 2 * NC, small, 0.0)
    lanes = lane_of(small.shape)
    known = prior[...]
    logits = small + jnp.where(lanes < NE, known, 0.0)
    named = lanes.astype(F32)
    hit0 = named == known[:, 2 * NE : 2 * NE + 1]
    hit1 = named == known[:, 2 * NE + 1 : 2 * NE + 2]
    chosen0 = jnp.sum(jnp.where(hit0, logits, 0.0), axis=1, keepdims=True)
    chosen1 = jnp.sum(jnp.where(hit1, logits, 0.0), axis=1, keepdims=True)
    gate0 = 1.0 / (1.0 + jnp.exp(chosen1 - chosen0))
    gate1 = 1.0 / (1.0 + jnp.exp(chosen0 - chosen1))
    share = jnp.where(hit0, gate0, 0.0) + jnp.where(hit1, gate1, 0.0)
    partner = jnp.where(lanes % 2 == 0, pltpu.roll(small, LANES - 1, 1), pltpu.roll(small, 1, 1))
    mix = 1.0 / (1.0 + jnp.exp(partner - small))
    mixing = (lanes >= NE) & (lanes < NE + 2 * NC)
    stats[...] = share + jnp.where(mixing, mix, 0.0)
    high, rest = two_parts(share)
    parts = (high.astype(F32) + pltpu.roll(rest.astype(F32), NE, 1)).astype(BF16)
    model = low.shape[1]
    for s in range(SEQS):
        chosen = slots[around(meta, s)]
        sent[s][:, :model] = mm(chosen, low).astype(BF16)
        sent[s][:, model:] = mm(chosen, parts).astype(BF16)


def weight_blocks(weights):
    model = weights.shape[0]
    return [
        (far(weights), pl.BlockSpec((model, model), lambda i: (0, 0))),
        (far(weights), pl.BlockSpec((model, LANES), lambda i: (0, model // LANES))),
    ]


def route(meta, att, weights, tok, prior, slots, *before):
    rows, model = tok.shape
    results = [((CAP, model + LANES), BF16)] * SEQS + [
        ((rows, model), F32),
        ((rows, model), BF16),
        ((rows, LANES), F32),
        ((8, model), F32),
    ]
    inputs = [*come(att), *weight_blocks(weights), tok, prior, slots]
    return one_step(route_kernel, 100, meta, inputs, results, (), before, 24)


def local_part_kernel(meta, resid, stats, grad, vectors, partial, small, grad_vec):
    gain = vectors[NC : NC + 1]
    res, g = resid[...], grad[...].astype(F32)
    normed = res * lax.rsqrt(jnp.mean(res * res, axis=-1, keepdims=True) + EPS) * gain
    held = stats[...]
    lanes = lane_of(held.shape)
    copy_dot = jnp.sum(g * normed, axis=1, keepdims=True)
    factor = pick(held, lanes, EF + 1)
    result = jnp.where(lanes == EF + 1, factor * copy_dot, 0.0)
    ways = jnp.zeros_like(held)
    added = jnp.zeros_like(res)
    for j in range(NC):
        row = vectors[j : j + 1]
        weight = pick(held, lanes, EF + 2 + j)
        first = pick(held, lanes, NE + 2 * j)
        second = pick(held, lanes, NE + 2 * j + 1)
        vec_dot = jnp.sum(g * row, axis=1, keepdims=True)
        mean = first * copy_dot + second * vec_dot
        result += jnp.where(lanes == EF + 2 + j, weight * mean, 0.0)
        result += jnp.where(lanes == NE + 2 * j, weight * first * (copy_dot - mean), 0.0)
        result += jnp.where(lanes == NE + 2 * j + 1, weight * second * (vec_dot - mean), 0.0)
        ways += jnp.where(lanes == j, weight * second, 0.0)
        added += (weight * second) * row
        factor += weight * first
    small[...] = result + jnp.where(lanes == NE + 2 * NC, factor, 0.0)
    partial[...] = res + factor * normed + added
    high, rest = two_parts(ways)
    grad_vec[...] = mm(grad[...], high, 0, 0) + mm(grad[...], rest, 0, 0)


def local_part(meta, resid, stats, grad, vectors):
    rows, model = resid.shape
    results = [((rows, model), F32), ((rows, LANES), F32), ((model, LANES), F32)]
    return one_step(local_part_kernel, 0.1, meta, [resid, stats, grad, vectors], results, mib=16)


def expert_kernel(meta, *refs):
    sent, grads = refs[:SEQS], refs[SEQS : 2 * SEQS]
    gate_w, up_w, out_w = refs[2 * SEQS + 1 : 2 * SEQS + 4]
    back, branch = refs[2 * SEQS + 4 : 3 * SEQS + 4], refs[3 * SEQS + 4]
    in_kept, in_sent, out_kept, out_sent = refs[3 * SEQS + 5 : 3 * SEQS + 9]
    rows, flipped, held, scaled, gate, hidden, dgate, dup, acc, mixed_acc, dots = refs[-11:]
    step = pl.program_id(0)
    count, model = rows.shape
    block = gate_w.shape[1]
    me = meta[1]
    even = meta[2] == 0

    def split(x, kept, gone):
        pairs, shard, wide = kept.shape
        x = x.reshape(pairs, 2 * shard, wide)
        first, second = x[:, :shard], x[:, shard:]
        kept[...] = jnp.where(even, first, second).astype(BF16)
        gone[...] = jnp.where(even, second, first).astype(BF16)

    @pl.when(step == 0)
    def _():
        for s in range(SEQS):
            at = slice(s * CAP, (s + 1) * CAP)
            rows[at] = sent[s][:, :model]
            flipped[:, at] = jnp.transpose(sent[s][:, :model])
            held[at] = grads[s][...]
            parts = sent[s][:, model:].astype(F32)
            lanes = lane_of(parts.shape)
            own = (lanes == me) | (lanes == me + NE)
            share = jnp.sum(jnp.where(own, parts, 0.0), axis=1, keepdims=True)
            gate[at] = jnp.broadcast_to(share, (CAP, LANES))
            scaled[at] = (grads[s][...].astype(F32) * share).astype(BF16)
        acc[...] = jnp.zeros_like(acc)
        mixed_acc[...] = jnp.zeros_like(mixed_acc)
        dots[...] = jnp.zeros_like(dots)

    for at in (slice(0, count // 2), slice(count // 2, count)):
        g = mm(rows[at], gate_w[...])
        u = mm(rows[at], up_w[...])
        v = mm(held[at], out_w[...], 1, 1)
        sig = 1.0 / (1.0 + jnp.exp(-g))
        silu = g * sig
        low = (silu * u).astype(BF16)
        hidden[at] = low
        both = v * low.astype(F32)
        folded = both[:, :LANES]
        for c in range(LANES, block, LANES):
            folded = folded + both[:, c : c + LANES]
        dots[at] += folded
        d = v * gate[at, 0:1]
        du = (d * silu).astype(BF16)
        dg = (d * u * (sig * (1.0 + g * (1.0 - sig)))).astype(BF16)
        dgate[at] = dg
        dup[at] = du
        acc[at] += mm(dg, gate_w[...], 1, 1) + mm(du, up_w[...], 1, 1)
        mixed_acc[at] += mm(low, out_w[...])

    split(mm(flipped[...], dgate[...]), in_kept.at[0, 0], in_sent.at[0, 0])
    split(mm(flipped[...], dup[...]), in_kept.at[0, 1], in_sent.at[0, 1])
    split(mm(hidden[...], scaled[...], 0, 0), out_kept, out_sent)

    @pl.when(step == pl.num_programs(0) - 1)
    def _():
        for s in range(SEQS):
            at = slice(s * CAP, (s + 1) * CAP)
            back[s][:, :model] = acc[at].astype(BF16)
            value = jnp.sum(dots[at], axis=1, keepdims=True) * gate[at]
            lanes = lane_of(value.shape)
            high, rest = two_parts(value)
            back[s][:, model:] = (
                jnp.where(lanes == me, high.astype(F32), 0.0)
                + jnp.where(lanes == me + NE, rest.astype(F32), 0.0)
            ).astype(BF16)
            branch[around(meta, s)] = (mixed_acc[at] * gate[at, 0:1]).astype(BF16)


def expert(meta, sent, grads, before, weights, w_out, block, fsdp):
    count, model = SEQS * CAP, grads[0].shape[1]
    inner = w_out.shape[0]
    steps = inner // block
    skip = (model + 2 * LANES) // block
    pairs, in_rows, out_rows = fsdp // 2, model // fsdp, inner // fsdp
    per = block // (2 * out_rows)
    results = [sds(sent[0].shape, BF16)] * SEQS + [sds((SEQS, CAP, model), BF16)]
    in_spec = pl.BlockSpec((1, 2, pairs, in_rows, block), lambda i: (i, 0, 0, 0, 0))
    out_spec = pl.BlockSpec((per, out_rows, model), lambda i: (i, 0, 0))
    return pl.pallas_call(
        expert_kernel,
        grid=(steps,),
        in_specs=[SMEM]
        + [whole(x) for x in (*sent, *grads)]
        + [
            ANY,
            pl.BlockSpec((model, block), lambda i: (0, i + skip)),
            pl.BlockSpec((model, block), lambda i: (0, i + skip + steps)),
            pl.BlockSpec((block, model), lambda i: (i, 0)),
        ],
        out_specs=[whole(x) for x in results] + [in_spec, in_spec, out_spec, out_spec],
        out_shape=[hbm(r.shape, r.dtype) for r in results]
        + [hbm((steps, 2, pairs, in_rows, block), BF16)] * 2
        + [hbm((pairs, out_rows, model), BF16)] * 2,
        scratch_shapes=[
            pltpu.VMEM((count, model), BF16),
            pltpu.VMEM((model, count), BF16),
            pltpu.VMEM((count, model), BF16),
            pltpu.VMEM((count, model), BF16),
            pltpu.VMEM((count, LANES), F32),
            pltpu.VMEM((count, block), BF16),
            pltpu.VMEM((count, block), BF16),
            pltpu.VMEM((count, block), BF16),
            pltpu.VMEM((count, model), F32),
            pltpu.VMEM((count, model), F32),
            pltpu.VMEM((count, LANES), F32),
        ],
        compiler_params=params(52, 1),
        cost_estimate=took(10),
        name="expert",
    )(meta, *sent, *grads, *map(far, (before, weights, weights, w_out)))


def split_again(small):
    lanes = lane_of(small.shape)
    table = small + pltpu.roll(small, LANES - NE, 1)
    high = table.astype(BF16).astype(F32)
    rest = pltpu.roll(table - high, NE, 1)
    at = lanes // NE
    return jnp.where(at == 2, high, jnp.where(at == 3, rest, small))


def add_cores_kernel(in_a, in_b, out_a, out_b, *refs):
    blocks, _, _, shard, block = in_a.shape
    wide = 2 * blocks * block
    for k in range(in_a.shape[2]):
        both = refs[-1].at[k]
        for j in range(2 * blocks):
            at = (j % blocks, j // blocks, k)
            total = in_a[at].astype(F32) + in_b[at].astype(F32)
            both[:, j * block : (j + 1) * block] = total.astype(BF16)
        more = out_a[k].astype(F32) + out_b[k].astype(F32)
        both[:, wide:] = tiles_moved(more, shard, both.shape[1] - wide).astype(BF16)


def add_cores(parts, *before):
    blocks, _, pairs, shard, block = parts[0].shape
    wide = 2 * blocks * block
    more = parts[2].shape[1] * parts[2].shape[2] // shard

    def some(shape):
        return pl.BlockSpec((SIDE, *shape), lambda i: (i, 0, 0))

    return pl.pallas_call(
        add_cores_kernel,
        grid=(pairs // SIDE,),
        in_specs=[pl.BlockSpec((blocks, 2, SIDE, shard, block), lambda i: (0, 0, i, 0, 0))] * 2
        + [some(x.shape[1:]) for x in parts[2:]]
        + [ANY] * len(before),
        out_specs=some((shard, wide + more)),
        out_shape=hbm((pairs, shard, wide + more), BF16),
        compiler_params=params(24, 1),
        cost_estimate=took(0.1),
        name="add_cores",
    )(*[x if k % 2 else far(x) for k, x in enumerate(parts)], *map(far, before))


def add_dense_kernel(meta, dense_a, dense_b, heads_a, heads_b, *refs):
    out = refs[-1]
    pairs, shard, wide = dense_a.shape
    width, model = heads_a.shape[2], wide - LANES
    for k in range(pairs):
        total = dense_a[k].astype(F32) + dense_b[k].astype(F32)
        out[k, :, :model] = total[:, :model].astype(BF16)
        out[k, :, model:wide] = split_again(total[:, model:]).astype(BF16)
        heads = heads_a[k].astype(F32) + heads_b[k].astype(F32)
        rest = jnp.zeros((shard, out.shape[2] - wide - width), F32)
        out[k, :, wide:] = jnp.concatenate([heads, rest], axis=1).astype(BF16)


def add_dense(meta, kept, come_dense, heads, come_heads, *before):
    pairs, shard, wide = kept.shape
    results = [((pairs, shard, -(-(wide + heads.shape[2]) // LANES) * LANES), BF16)]
    inputs = [kept, *come(come_dense), heads, *come(come_heads)]
    return one_step(add_dense_kernel, 0.1, meta, inputs, results, (), before, 24)[0]


def add_pieces_kernel(meta, pieces, *refs):
    total = pieces[0].astype(F32)
    for k in range(1, pieces.shape[0]):
        total += pieces[k].astype(F32)
    model = pieces.shape[0] * pieces.shape[1] * 2
    small = split_again(total[:, model : model + LANES])
    parts = [total[:, :model], small, total[:, model + LANES :]]
    total = jnp.concatenate(parts, axis=1).astype(BF16)
    refs[-1][...] = total


def add_pieces(meta, pieces, *before):
    results = [(pieces.shape[1:], BF16)]
    return one_step(add_pieces_kernel, 0.1, meta, come(pieces), results, (), before, 24)[0]


def mixed_kernel(meta, partial, slots, *refs):
    result = partial[...]
    for e in range(EF):
        result += mm(slots[e], refs[0][e], 0, 0)
    refs[-1][...] = result.astype(BF16)


def mixed(meta, partial, slots, branch, *before):
    results = [(partial.shape, BF16)]
    (out,) = one_step(mixed_kernel, 0.1, meta, [partial, slots, *come(branch)], results, (), before)
    return out


def unroute_kernel(meta, *refs):
    back = refs[:SEQS]
    out_w, small_w, slots, resid, small, stats, grad, vectors = refs[SEQS : SEQS + 8]
    datt, dres, dlow, dlogits, dgain = refs[-5:]
    gain = vectors[NC : NC + 1]
    rows, model = resid.shape
    held, local = stats[...], small[...]
    lanes = lane_of(held.shape)
    dn = jnp.zeros((rows, model), F32)
    tail = jnp.zeros((rows, LANES), F32)
    for s in range(SEQS):
        chosen = slots[around(meta, s)]
        dn += mm(chosen, back[s][:, :model], 0, 0)
        tail += mm(chosen, back[s][:, model:], 0, 0)
    ffn = tail + pltpu.roll(tail, LANES - NE, 1)
    dots = jnp.where(lanes < EF, ffn, jnp.where(lanes < NE, local, 0.0))
    total = jnp.sum(dots, axis=1, keepdims=True)
    keep = (lanes >= NE) & (lanes < NE + 2 * NC)
    dsmall = jnp.where(lanes < NE, dots - held * total, jnp.where(keep, local, 0.0))
    high, rest = two_parts(dsmall)
    dn += mm(high, small_w[...], 1, 1) + mm(rest, small_w[...], 1, 1)
    g = grad[...].astype(F32)
    dn += pick(local, lanes, NE + 2 * NC) * g
    res = resid[...]
    factor = lax.rsqrt(jnp.mean(res * res, axis=-1, keepdims=True) + EPS)
    normal = res * factor
    dgain[...] = jnp.sum(dn * normal, axis=0, keepdims=True)
    dlogits[...] = dsmall
    scaled = dn * gain
    out = g + factor * (scaled - normal * jnp.mean(scaled * normal, axis=-1, keepdims=True))
    dres[...] = out
    low = out.astype(BF16)
    dlow[...] = low
    datt[...] = mm(out_w[...], low, 1, 1).astype(BF16)


def unroute(meta, before, back, weights, tokenwise):
    rows, model = tokenwise[1].shape
    inputs = [*come(*back), *weight_blocks(weights), *tokenwise]
    results = [
        ((model, rows), BF16),
        ((rows, model), F32),
        ((rows, model), BF16),
        ((rows, LANES), F32),
        ((1, model), F32),
    ]
    return one_step(unroute_kernel, 100, meta, inputs, results, (), before, 32)


def finish_kernel(meta, *refs):
    dproj, (weight, tok, gain, dres) = refs[:SEQS], refs[SEQS : SEQS + 4]
    out, flat = refs[-2:]
    width = dproj[0].shape[0]
    for s in range(SEQS):
        at = pl.multiple_of(around(meta, s) * width, 64)
        flat[pl.ds(at, width)] = dproj[s][...]
    dn = jnp.transpose(mm(weight[...], flat[...]))
    v = tok[...].astype(F32)
    factor = lax.rsqrt(jnp.mean(v * v, axis=-1, keepdims=True) + EPS)
    normal = v * factor
    scaled = dn * gain[...]
    dx = factor * (scaled - normal * jnp.mean(scaled * normal, axis=-1, keepdims=True))
    out[...] = (dres[...] + dx).astype(BF16)


def finish(meta, dproj, weight, tok, gain, dres, *before):
    width, rows = dproj[0].shape
    scratch = [pltpu.VMEM((SEQS * width, rows), BF16)]
    results = [(tok.shape, BF16)]
    inputs = [*come(*dproj), weight, tok, gain, dres]
    return one_step(finish_kernel, 10, meta, inputs, results, scratch, before, 24)[0]


def gather_kernel(meta, *refs):
    pieces = refs[:SEQS]
    grad_in, grad_out = refs[-2:]
    wide = grad_in.shape[2]
    for s in range(SEQS):
        place = around(meta, s)
        grad_in[place] = pieces[s][:, :wide].astype(F32)
        grad_out[place] = tiles_moved(pieces[s][:, wide:].astype(F32), *grad_out.shape[1:])


def gather(meta, pieces, wide, rows, model, *before):
    shard = pieces[0].shape[0]
    results = [((SEQS, shard, wide), F32), ((SEQS, rows, model), F32)]
    return one_step(gather_kernel, 0.1, meta, come(*pieces), results, (), before, 24)


def gather_dense_kernel(meta, *refs):
    pieces, attend_in, gain_a = refs[:SEQS], refs[SEQS], refs[SEQS + 1]
    att_in, grad_gain, att_out, router, const_mix, const_vector, gain, table, held = refs[-9:]
    shard, model = att_out.shape
    group = model // SEQS
    at = model + LANES
    for s in range(SEQS):
        held[around(meta, s)] = pieces[s][...].astype(F32)
    order = [(k, g) for k in range(3) for g in range(SEQS)]
    parts = [held[g][:, at + k * group : at + (k + 1) * group] for k, g in order]
    full = jnp.concatenate(parts, axis=1)
    att_in[...] = full
    low = attend_in[...].astype(BF16).astype(F32)
    column = jnp.sum(full * low, axis=1, keepdims=True)
    column = jnp.concatenate([column, jnp.zeros((LANES - shard, 1), F32)], axis=0)
    row = jnp.transpose(jnp.broadcast_to(column, (LANES, LANES)))[:1, :shard]
    grad_gain[...] = row / gain_a[...].astype(BF16).astype(F32)

    total = held[0][:, :at]
    for s in range(1, SEQS):
        total += held[s][:, :at]
    att_out[...] = total[:, :model]
    small = jnp.concatenate([total[:, model:], jnp.zeros((LANES - shard, LANES), F32)], axis=0)
    both = small + pltpu.roll(small, LANES - NE, 1)
    table[...] = pltpu.roll(both, LANES - 2 * NE, 1)[:NE, :NE]
    small = jnp.transpose(small)[:, :shard]
    at = NE + 2 * NC
    router[...] = small[:NE]
    const_mix[...] = small[NE:at]
    const_vector[...] = small[at : at + NC]
    gain[...] = small[at + NC : at + NC + 1]


def gather_dense(meta, pieces, attend_in, gain):
    shard, wide = pieces[0].shape
    model = attend_in.shape[1] // 3
    results = [attend_in.shape, (1, shard), (shard, model), (NE, shard), (2 * NC, shard)]
    results = [(r, F32) for r in (*results, (NC, shard), (1, shard), (NE, NE))]
    scratch = [pltpu.VMEM((SEQS, shard, wide), F32)]
    inputs = [*come(*pieces), attend_in, gain]
    return one_step(gather_dense_kernel, 0.1, meta, inputs, results, scratch, mib=16)


def shards(
    tokens,
    cotangent,
    lengths,
    routes,
    prior_routes,
    gain_attend,
    attend_in,
    attend_out,
    gain_mix,
    router,
    route_table,
    const_mix,
    const_vector,
    expert_in,
    expert_out,
):
    seqs = lax.axis_size("seq")
    fsdp = lax.axis_size(FSDP)
    here = lax.axis_index("seq")
    tok = tokens[0]
    rows, model = tok.shape
    shard = attend_in.shape[0]
    group = model // seqs
    width = 3 * group
    length = lengths[0]
    meta = jnp.stack([length, here, *(lax.axis_index(a) for a in ("core", *YZ))])
    meta = meta.astype(jnp.int32)

    first, second, back_mine = pack(
        meta,
        attend_in,
        gain_attend[None],
        attend_out,
        router.T,
        const_mix.T,
        const_vector.T,
        gain_mix[None],
        expert_in,
        expert_out,
        fsdp,
    )
    first_all = swap(first, FSDP).reshape(model, width + 64)
    half = rows // 2
    left, right = shift(tok, 1), shift(tok, -1)
    far0, far1 = shift(left[:half], 1), shift(right[half:], -1)
    weights = lax.all_gather(second, FSDP, axis=0, tiled=True)
    back_w = lax.all_gather(back_mine, FSDP, axis=0, tiled=True)
    inner = expert_out.shape[1] * fsdp
    wide = expert_out.shape[1] * model // shard
    w_out = weights[:, model + 2 * LANES + 2 * inner :]
    w_out = w_out.reshape(-1, shard // 8, 8, wide // LANES, LANES).transpose(0, 1, 3, 2, 4)
    w_out = w_out.reshape(-1, model // LANES, 8, LANES).transpose(0, 2, 1, 3).reshape(inner, model)
    gain_a = first_all[:, width].astype(F32)[None]

    slots, grad, prior, prior_hits, *grad_rows = plan(
        meta, routes[0].T, prior_routes[0].T, route_table, cotangent[0]
    )
    inverse = jnp.exp(
        jnp.arange(HALF, dtype=F32) * (-2.0 * math.log(10000.0) / HEAD_DIM)
    )
    angles = jnp.arange(seqs * rows, dtype=F32).reshape(seqs, 1, rows) * inverse[None, :, None]
    cosine, sine = jnp.cos(angles), jnp.sin(angles)

    left, right, *grad_rows = lax.optimization_barrier((left, right, *grad_rows))
    grad_rows = trades(grad_rows)

    qkv, normed = project(
        meta, [tok, left, right, far0, far1], first_all, gain_a, cosine, sine, width
    )
    held, lse, qkv = attend(meta, qkv)
    held, *grad_rows = lax.optimization_barrier((held, *grad_rows))
    att = swap(held, "seq").reshape(model, rows)
    *sent, resid, moe, stats, vectors = route(meta, att, weights, tok, prior, slots)
    sent = trades(sent)
    partial, small, grad_vec = local_part(meta, resid, stats, grad, vectors)

    *results, in_kept, in_sent, out_kept, out_sent = expert(
        meta, sent, grad_rows, small, weights, w_out, 512, fsdp
    )
    back, branch = trades(results[:seqs]), results[seqs]
    in_come, out_come = trade(in_sent, 1, "core"), trade(out_sent, 1, "core")
    both = add_cores((in_kept, in_come, out_kept, out_come), back_w)
    part = both.reshape(-1, both.shape[2])
    part = lax.psum_scatter(part, YZ, scatter_dimension=0, tiled=True)
    tokenwise = (slots, resid, small, stats, grad, vectors)
    datt, dres, dlow, dlogits, dgain_m = unroute(meta, (both,), back, weights, tokenwise)
    dout = swap(datt.reshape(seqs, group, rows), "seq")
    dout, branch = lax.optimization_barrier((dout, branch))
    branch = swap(branch, "seq")
    kept, gone = dense(
        meta, att, dlow, moe, dlogits, grad_vec, dgain_m, prior_hits, fsdp
    )
    come_dense = trade(gone, 1, "core")
    *dproj, heads, gone = attend_back(
        meta, (kept,), qkv, dout, held, lse, cosine, sine, normed, fsdp
    )
    come_heads = trade(gone, 1, "core")
    back_all = trades(dproj)
    sums = add_dense(meta, kept, come_dense, heads, come_heads, branch)
    mixed_out = mixed(meta, partial, slots, branch, sums)
    sums = swap(sums, YZ)
    part, back_all[2] = lax.optimization_barrier((part, back_all[2]))
    pieces = trades([part] * seqs)
    grad_tokens = finish(meta, back_all, back_w, tok, gain_a, dres, mixed_out)
    sums = add_pieces(meta, sums, grad_tokens)
    sums, *pieces = lax.optimization_barrier((sums, *pieces))
    sums = trades([sums] * seqs)
    grad_attend_in, grad_gain_a, grad_att_out, *rest, table = gather_dense(
        meta, sums, attend_in, gain_attend[None]
    )
    grad_router, grad_mix, grad_vector, grad_gain_m = rest
    grad_in, grad_out = gather(
        meta, pieces, 2 * inner, expert_out.shape[1], model
    )
    return (
        mixed_out[None],
        grad_tokens[None],
        grad_gain_a[0],
        grad_attend_in,
        grad_att_out,
        grad_gain_m[0],
        grad_router.T,
        table,
        grad_mix.T,
        grad_vector.T,
        grad_in,
        grad_out,
    )


def solution(mesh):
    fsdp = mesh.shape["fsdp"]
    finer = Mesh(
        mesh.devices.reshape(mesh.shape["seq"], fsdp // (2 * SIDE), SIDE, 2), ("seq", *FSDP)
    )
    placed = (
        P(FSDP, "seq", None),
        P(FSDP, "seq", None),
        P(FSDP),
        P(FSDP, "seq", None),
        P(FSDP, "seq", None),
        P(FSDP),
        P(FSDP, None),
        P(FSDP, None),
        P(FSDP),
        P(FSDP, None),
        P(),
        P(FSDP, None),
        P(FSDP, None),
        P(None, FSDP, None),
        P(None, FSDP, None),
    )
    return jax.shard_map(
        shards,
        mesh=finer,
        in_specs=placed,
        out_specs=(
            P(FSDP, "seq", None),
            P(FSDP, "seq", None),
            P(FSDP),
            P(FSDP, None),
            P(FSDP, None),
            P(FSDP),
            P(FSDP, None),
            P(),
            P(FSDP, None),
            P(FSDP, None),
            P(None, FSDP, None),
            P(None, FSDP, None),
        ),
        check_vma=False,
    )
```
